32 devices in a mesh: section: 2 (over y), shard: 16 (over z, x, core).
Axes of the slice: x: 2, y: 2, z: 4, core: 2. Of those that a mesh axis runs over, the one named last changes fastest.
Arguments:
- features: bfloat16 [2, 4096, 512], P(None, 'shard'), may hold values from -0.029907227 to 0.029907227
- labels: int32 [2, 4096], P(None, 'shard'), may hold values from 0 to 3
- label_table: float32 [4, 512], replicated, may hold values from -0.01 to 0.01
- tiles: bfloat16 [2, 96, 128, 128], P(None, 'shard'), may hold values from -1 to 1
- tile_rows: int32 [2, 96], P(None, 'shard'), may hold values from 0 to 31, as said below
- tile_cols: int32 [2, 96], P(None, 'shard'), may hold values from 0 to 31, as said below
- tile_live: int32 [2, 16], P(None, 'shard'), may hold values from 2 to 6, as said below
- weights: bfloat16 [2, 512, 512], P('section'), may hold values from -0.25 to 0.25
- gains: bfloat16 [2, 512], P('section'), may hold values from 0 to 1
- head_weight: float32 [512], replicated, may hold values from -0.75 to 0.75
Outputs:
- outcome: float32 [2, 4096], P('section', 'shard')
The draws below stay inside these ranges and needn't reach their ends.
Inputs may be any that keep to these rules, and one draw needn't show every extreme that they name: `tile_rows`: slot k of shard j has a row block from j * 2 - 1 to (j + 1) * 2. `tile_cols`: slot k of shard j has a column block of that shard's own nodes, j * 2 to (j + 1) * 2 - 1; where its row block is j * 2 - 1 the column block is j * 2, and where its row block is (j + 1) * 2 the column block is (j + 1) * 2 - 1. `tile_live`: in every graph group some shard has all 6 slots live.
All inputs are finite; a program needn't handle non-finite values.
Results may differ from the reference program's by a relative error of at most 0.02.
Values may be sent and summed in bfloat16 or wider, within the bound.
No kernel may reach another device: no remote copies, remote signals or barrier semaphores. Data moves between devices by JAX's collectives and lax.ppermute only.
A program may use at most 64 MiB of HBM per device.

```python
import jax
import jax.numpy as jnp
from jax import lax

D = 512
LABELS = 4
TILE = 128
TILES = 6
ROWS_DEV = 256
MB_SECTION = 1
MB = 2
NODES = 4096
BLOCKS = 32
SLOTS = 96
N_SECTION = 2


def tile_layout(key):
    per_rows = ROWS_DEV // TILE
    shard_count = NODES // ROWS_DEV
    key_place, key_column, key_count, key_heavy, key_pick = jax.random.split(jax.random.fold_in(key, 7), 5)
    position = jax.random.randint(key_place, (MB, shard_count, TILES), 0, per_rows + 2)
    position = position.at[:, :, 0].set(0).at[:, :, 1].set(per_rows + 1)
    shard_ids = jnp.arange(shard_count, dtype=jnp.int32)[None, :, None]
    row_blocks = jnp.clip(shard_ids * per_rows - 1 + position, 0, BLOCKS - 1)
    col_offset = jax.random.randint(key_column, (MB, shard_count, TILES), 0, per_rows)
    col_offset = jnp.where(position == 0, 0, jnp.where(position == per_rows + 1, per_rows - 1, col_offset))
    col_blocks = shard_ids * per_rows + col_offset
    base_count = jax.random.randint(key_count, (MB, shard_count), 2, 4)
    busy_shard = jax.random.randint(key_heavy, (MB, shard_count), 0, 8) == 0
    chosen = jax.random.randint(key_pick, (MB, 1), 0, shard_count)
    forced_shard = jnp.arange(shard_count, dtype=jnp.int32)[None, :] == chosen
    counts = jnp.where(busy_shard | forced_shard, TILES, jnp.minimum(base_count, TILES)).astype(jnp.int32)
    return (row_blocks.reshape(MB, SLOTS).astype(jnp.int32), col_blocks.reshape(MB, SLOTS).astype(jnp.int32), counts, position.reshape(MB, SLOTS).astype(jnp.int32))


def draw_tile_rows(key, part):
    return tile_layout(key)[0]


def draw_tile_cols(key, part):
    return tile_layout(key)[1]


def draw_tile_live(key, part):
    return tile_layout(key)[2]


def draw_tiles(key, part):
    position = tile_layout(key)[3]
    toward_lower = position == 0
    array_shape = (MB, SLOTS, TILE, TILE)
    value_key = jax.random.fold_in(key, 11)
    sample = jnp.clip(jax.random.normal(value_key, array_shape, jnp.float32), -5.0, 5.0)
    factor = jnp.where(toward_lower, 0.15, 1.0).astype(jnp.float32)
    values = sample * factor[:, :, None, None] * (2.0 * TILE) ** (-0.5)
    return values.astype(jnp.bfloat16)


def draw_gains(key, part):
    sections = MB // MB_SECTION
    layer_ids = jnp.arange(sections, dtype=jnp.float32)[:, None]
    base_gain = 0.5 * jnp.exp(jnp.log(1.7) * (layer_ids - (sections - 1)))
    gain_key = jax.random.fold_in(key, 13)
    spread = jnp.exp(jax.random.uniform(gain_key, (sections, D), jnp.float32, -0.5, 0.5))
    return (base_gain * spread).astype(jnp.bfloat16)


def set_ends(drawn, key, least, high):
    index_at = [jax.random.randint(jax.random.fold_in(key, axis), (), 0, length) for axis, length in enumerate(drawn.shape)]
    longest = drawn.shape.index(max(drawn.shape))
    beside = index_at[:longest] + [(index_at[longest] + 1) % drawn.shape[longest]] + index_at[longest + 1:]
    return drawn.at[tuple(index_at)].set(least).at[tuple(beside)].set(high)


def block_scale(stream_key, shape, shards, smallest, largest):
    level = 1.0
    for axis_at, shards_of in shards:
        draws = jax.random.uniform(jax.random.fold_in(jax.random.fold_in(stream_key, 6), axis_at), (shards_of,), jnp.float32, smallest / len(shards), largest / len(shards))
        level = level * jnp.repeat(jnp.exp(draws), shape[axis_at] // shards_of).reshape((-1,) + (1,) * (len(shape) - 1 - axis_at))
    return level


def normal_values(rng, dims, scale, reach, cuts=(), held_as=jnp.bfloat16):
    factor_of = block_scale(rng, dims, cuts, -0.22, 0.18) if cuts else 1.0
    values = jax.random.normal(rng, dims, jnp.float32) * scale * factor_of
    return jnp.minimum(jnp.maximum(values, -reach), reach).astype(held_as)


def setup_inputs(seed: int = 0) -> dict:
    streams_of = jax.random.split(jax.random.key(seed), 11)
    return {
        "features": normal_values(streams_of[0], (MB, NODES, D), 0.005, 0.029907227, ((1, 16),)),
        "labels": set_ends(jax.random.randint(streams_of[1], (MB, NODES), 0, LABELS), jax.random.fold_in(streams_of[1], 1), 0, LABELS - 1).astype(jnp.int32),
        "label_table": jnp.clip(jax.random.uniform(streams_of[2], (LABELS, D), jnp.float32, -0.01, 0.01), -0.01, 0.01),
        "tiles": draw_tiles(jax.random.fold_in(streams_of[10], 71), 0),
        "tile_rows": draw_tile_rows(jax.random.fold_in(streams_of[10], 71), 0),
        "tile_cols": draw_tile_cols(jax.random.fold_in(streams_of[10], 71), 0),
        "tile_live": draw_tile_live(jax.random.fold_in(streams_of[10], 71), 0),
        "weights": normal_values(streams_of[7], (N_SECTION, D, D), D ** -0.5, 0.25, ((0, 2),)),
        "gains": draw_gains(jax.random.fold_in(streams_of[10], 71), 0),
        "head_weight": normal_values(streams_of[9], (D,), (D // 8) ** -0.5, 0.75, (), jnp.float32),
    }


def reference(features, labels, label_table, tiles, tile_rows, tile_cols, tile_live, weights, gains, head_weight):
    slot_ids = jnp.arange(SLOTS, dtype=jnp.int32) % TILES

    def one_group(batch_index):
        labels_hot = (labels[batch_index][:, None] == jnp.arange(LABELS, dtype=jnp.int32)[None, :]).astype(jnp.float32)
        embedded = jnp.dot(labels_hot, label_table, precision=lax.Precision.HIGHEST)
        state = (features[batch_index].astype(jnp.float32) + embedded).astype(jnp.bfloat16)
        live_mask = (slot_ids < jnp.repeat(tile_live[batch_index], TILES)).astype(jnp.float32)
        group_tiles = tiles[batch_index].astype(jnp.float32)
        for layer_index in range(N_SECTION):
            block_view = state.reshape(BLOCKS, TILE, D)
            chosen_blocks = jnp.take(block_view, tile_cols[batch_index], axis=0).astype(jnp.float32)
            products = jnp.einsum('kab,kbd->kad', group_tiles, chosen_blocks, precision=lax.Precision.HIGHEST)
            products = products * live_mask[:, None, None]
            aggregate = jax.ops.segment_sum(products, tile_rows[batch_index], num_segments=BLOCKS)
            aggregate = aggregate.reshape(NODES, D).astype(jnp.bfloat16)
            projected = jnp.dot(aggregate, weights[layer_index], preferred_element_type=jnp.float32)
            scale = lax.rsqrt(lax.optimization_barrier(jnp.mean(projected * projected, axis=-1, keepdims=True)) + 1e-06)
            normed = projected * scale * gains[layer_index].astype(jnp.float32)
            state = (state.astype(jnp.float32) + jax.nn.gelu(normed)).astype(jnp.bfloat16)
        return jnp.dot(state.astype(jnp.float32), head_weight, precision=lax.Precision.HIGHEST)
    return lax.map(one_group, jnp.arange(MB, dtype=jnp.int32))
```

```python
import jax
import jax.numpy as jnp
from jax import lax
from jax.experimental import pallas as pl
from jax.experimental.pallas import tpu as pltpu
from jax.sharding import PartitionSpec as P

BF16 = jnp.bfloat16
F32 = jnp.float32
PAD = 16


def split3(value):
    high = value.astype(BF16).astype(F32)
    rest = value - high
    mid = rest.astype(BF16).astype(F32)
    return high, mid, rest - mid


def dot(a, b, dims=((1,), (0,))):
    return lax.dot_general(a, b, (dims, ((), ())), preferred_element_type=F32)


def layer(aggregate, weight, gain, state):
    projected = dot(aggregate, weight)
    scale = lax.rsqrt(jnp.mean(projected * projected, axis=-1, keepdims=True) + 1e-06)
    normed = projected * scale * gain
    return (state.astype(F32) + jax.nn.gelu(normed)).astype(BF16)


def first_kernel(
    tile_rows, tile_cols, tile_live, labels, label_table, gains, features, tiles, weights,
    near, far, crossing, state_out, adjacency_out,
    features_buf, tiles_buf, table_buf, sums, sems,
):
    section = lax.axis_index("section")
    shard = lax.axis_index("shard")
    parity = lax.rem(shard, 2)
    rows, width = features_buf.shape
    slots, size, _ = tiles_buf.shape
    blocks = rows // size
    kept = crossing.shape[0] - PAD
    group = section

    copy_features = pltpu.make_async_copy(features.at[group], features_buf, sems.at[0])
    copy_tiles = pltpu.make_async_copy(tiles.at[group], tiles_buf, sems.at[1])
    copy_weight = pltpu.make_async_copy(
        weights.at[0, pl.ds(pl.multiple_of(parity * kept, kept), kept)],
        crossing.at[pl.ds(0, kept)],
        sems.at[2],
    )
    copy_tiles.start()
    copy_features.start()
    copy_weight.start()

    crossing[pl.ds(kept, PAD), :] = jnp.broadcast_to(gains[...].astype(F32), (PAD, width)).astype(BF16)
    classes = label_table.shape[0]
    table_buf[...] = jnp.zeros_like(table_buf)
    for part, value in enumerate(split3(label_table[...])):
        table_buf[pl.ds(part * classes, classes), :] = value
    depth = table_buf.shape[0]
    index = lax.broadcasted_iota(jnp.int32, (depth, rows), 0)
    wanted = jnp.where(
        index < classes, index,
        jnp.where(index < 2 * classes, index - classes, jnp.where(index < 3 * classes, index - 2 * classes, -1)),
    )
    hot = (wanted == labels[pl.ds(group, 1), :]).astype(F32).astype(BF16)
    embedded = dot(hot, table_buf[...].astype(BF16), ((0,), (0,)))

    sums[...] = jnp.zeros_like(sums)
    copy_tiles.wait()
    for slot in range(slots):
        @pl.when(slot < tile_live[group, 0])
        def _():
            row = tile_rows[group, slot] - (shard * blocks - 1)
            col = tile_cols[group, slot] - shard * blocks
            place = (pl.ds(pl.multiple_of(row * size, size), size), pl.ds(pl.multiple_of(col * size, size), size))
            sums[place] += tiles_buf[slot].astype(F32)
    adjacency = sums[...].astype(BF16)
    adjacency_out[...] = adjacency

    copy_features.wait()
    state = (features_buf[...].astype(F32) + embedded).astype(BF16)
    state_out[...] = state
    partial = dot(adjacency[size : size + rows], state).astype(BF16)

    def write(target, block, edge):
        target[:, pl.ds(0, width)] = partial[block * size : (block + 1) * size]
        target[:, pl.ds(width, width)] = state[block * size : (block + 1) * size]
        target[:, pl.ds(2 * width, size)] = edge

    upper = adjacency[rows + size :, rows - size :]
    lower = adjacency[:size, :size]

    @pl.when(parity == 0)
    def _():
        write(near, blocks - 1, upper)
        write(far, 0, lower)

    @pl.when(parity == 1)
    def _():
        write(far, blocks - 1, upper)
        write(near, 0, lower)

    copy_weight.wait()


def second_kernel(
    head, gains, adjacency, state_own, near, far, crossed, relayed, weights,
    outcome,
    adj, ext_state, low, high, mats, other_gains, wide, next_state, head_buf, sems,
):
    section = lax.axis_index("section")
    parity = lax.rem(lax.axis_index("shard"), 2)
    rows, width = state_own.shape
    size = low.shape[0]
    kept = mats.shape[1] // 2

    copies = {}

    def copy(name, source, target, index):
        copies[name] = pltpu.make_async_copy(source, target, sems.at[index])
        copies[name].start()

    copy("adj", adjacency, adj, 0)
    copy("state", state_own, ext_state.at[pl.ds(size, rows)], 1)

    @pl.when(parity == 0)
    def _():
        pltpu.make_async_copy(far, low, sems.at[2]).start()
        pltpu.make_async_copy(near, high, sems.at[3]).start()

    @pl.when(parity == 1)
    def _():
        pltpu.make_async_copy(near, low, sems.at[2]).start()
        pltpu.make_async_copy(far, high, sems.at[3]).start()

    copy("own", weights.at[0], mats.at[section], 4)
    copy("crossed", crossed.at[pl.ds(0, kept)], mats.at[1 - section, pl.ds(pl.multiple_of(parity * kept, kept), kept)], 5)
    copy("relayed", relayed.at[pl.ds(0, kept)], mats.at[1 - section, pl.ds(pl.multiple_of((1 - parity) * kept, kept), kept)], 6)
    copy("gain", crossed.at[pl.ds(kept, PAD)], other_gains, 7)

    copies["adj"].wait()
    copies["state"].wait()
    pltpu.make_async_copy(near, low, sems.at[2]).wait()
    pltpu.make_async_copy(near, high, sems.at[3]).wait()

    ext_state[pl.ds(0, size), :] = low[:, pl.ds(width, width)]
    ext_state[pl.ds(size + rows, size), :] = high[:, pl.ds(width, width)]
    low_tile = low[:, pl.ds(2 * width, size)]
    high_tile = high[:, pl.ds(2 * width, size)]
    wide[...] = jnp.zeros_like(wide)
    wide[pl.ds(0, size), pl.ds(0, size)] = low[:, pl.ds(2 * width, size)]
    wide[pl.ds(rows - size, size), pl.ds(size + rows, size)] = high[:, pl.ds(2 * width, size)]
    wide[:, pl.ds(size, rows)] = adj[pl.ds(size, rows), :]

    copies["gain"].wait()
    own_gain = gains[...].astype(F32)
    got_gain = other_gains[pl.ds(0, 1), :].astype(F32)
    first = section == 0
    gain = (jnp.where(first, own_gain, got_gain), jnp.where(first, got_gain, own_gain))

    copies["own"].wait()
    copies["crossed"].wait()
    copies["relayed"].wait()
    weight = mats[0]
    own = ext_state[pl.ds(size, rows), :]
    low_aggregate = dot(adj[pl.ds(0, size), :], own) + low[:, pl.ds(0, width)].astype(F32)
    high_aggregate = dot(adj[pl.ds(size + rows, size), :], own) + high[:, pl.ds(0, width)].astype(F32)
    aggregate = dot(wide[...], ext_state[...])
    next_state[pl.ds(0, size), :] = layer(low_aggregate.astype(BF16), weight, gain[0], ext_state[pl.ds(0, size), :])
    next_state[pl.ds(size, rows), :] = layer(aggregate.astype(BF16), weight, gain[0], own)
    next_state[pl.ds(size + rows, size), :] = layer(
        high_aggregate.astype(BF16), weight, gain[0], ext_state[pl.ds(size + rows, size), :]
    )

    aggregate = dot(wide[...], next_state[...])
    state = layer(aggregate.astype(BF16), mats[1], gain[1], next_state[pl.ds(size, rows), :])
    head_buf[...] = jnp.zeros_like(head_buf)
    for part, value in enumerate(split3(head[...])):
        head_buf[pl.ds(part, 1), :] = value
    scores = dot(head_buf[...].astype(BF16), state, ((1,), (1,)))
    outcome[...] = scores[0:1] + scores[1:2] + scores[2:3]


def paired(features, labels, label_table, tiles, tile_rows, tile_cols, tile_live, weights, gains, head_weight):
    shard_count = lax.axis_size("shard")
    _, rows, width = features.shape
    _, slots, size, _ = tiles.shape
    depth = weights.shape[1]
    kept = depth // 2
    message = jax.ShapeDtypeStruct((size, 2 * width + size), BF16)
    vmem = pl.BlockSpec(memory_space=pltpu.VMEM)
    smem = pl.BlockSpec(memory_space=pltpu.SMEM)
    hbm = pl.BlockSpec(memory_space=pl.ANY)
    table_rows = -(-3 * label_table.shape[0] // PAD) * PAD

    near, far, crossing, state, adjacency = pl.pallas_call(
        first_kernel,
        out_shape=(
            message,
            message,
            jax.ShapeDtypeStruct((kept + PAD, width), BF16),
            jax.ShapeDtypeStruct((rows, width), BF16),
            jax.ShapeDtypeStruct((rows + 2 * size, rows), BF16),
        ),
        in_specs=[smem, smem, smem, vmem, vmem, vmem, hbm, hbm, hbm],
        out_specs=(vmem,) * 5,
        scratch_shapes=[
            pltpu.VMEM((rows, width), BF16),
            pltpu.VMEM((slots, size, size), BF16),
            pltpu.VMEM((table_rows, width), F32),
            pltpu.VMEM((rows + 2 * size, rows), F32),
            pltpu.SemaphoreType.DMA((3,)),
        ],
        compiler_params=pltpu.CompilerParams(vmem_limit_bytes=16 * 2**20),
        name="messages",
    )(tile_rows, tile_cols, tile_live, labels, label_table, gains, features, tiles, weights)

    beside = [(i, i ^ 1) for i in range(shard_count)]
    apart = [(i, i + 1) for i in range(1, shard_count - 1, 2)]
    apart += [(b, a) for a, b in apart]
    crossed = lax.ppermute(crossing, "section", [(0, 1), (1, 0)])
    far = lax.ppermute(far, "shard", apart)
    near = lax.ppermute(near, "shard", beside)
    relayed = lax.ppermute(crossed, "shard", beside)

    return pl.pallas_call(
        second_kernel,
        out_shape=jax.ShapeDtypeStruct((1, rows), F32),
        in_specs=[vmem, vmem] + [hbm] * 7,
        out_specs=vmem,
        scratch_shapes=[
            pltpu.VMEM((rows + 2 * size, rows), BF16),
            pltpu.VMEM((rows + 2 * size, width), BF16),
            pltpu.VMEM(message.shape, BF16),
            pltpu.VMEM(message.shape, BF16),
            pltpu.VMEM((2, depth, width), BF16),
            pltpu.VMEM((PAD, width), BF16),
            pltpu.VMEM((rows, rows + 2 * size), BF16),
            pltpu.VMEM((rows + 2 * size, width), BF16),
            pltpu.VMEM((PAD, width), F32),
            pltpu.SemaphoreType.DMA((8,)),
        ],
        compiler_params=pltpu.CompilerParams(vmem_limit_bytes=32 * 2**20),
        name="layers",
    )(head_weight.reshape(1, width), gains, adjacency, state, near, far, crossed, relayed, weights)


def extended_2(block, sides, width):
    for axis, dim in sides:
        count = lax.axis_size(axis)
        forward = [(i, i + 1) for i in range(count - 1)]
        backward = [(target, source) for source, target in forward]
        low = lax.ppermute(
            lax.slice_in_dim(block, block.shape[dim] - width, None, axis=dim), axis, forward
        )
        high = lax.ppermute(lax.slice_in_dim(block, 0, width, axis=dim), axis, backward)
        block = jnp.concatenate([low, block, high], axis=dim)
    return block


def body(
    features,
    labels,
    label_table,
    tiles,
    tile_rows,
    tile_cols,
    tile_live,
    weights,
    gains,
    head_weight,
):
    section_count = lax.axis_size("section")
    section_index = lax.axis_index("section")
    shard_index = lax.axis_index("shard")
    batch_count = features.shape[0]
    row_count = features.shape[1]
    feature_width = features.shape[2]
    tile_size = tiles.shape[2]
    slot_count = tiles.shape[1]
    label_count = label_table.shape[0]
    per_rows = row_count // tile_size
    per_section = batch_count // section_count
    slot_ids = jnp.arange(slot_count, dtype=jnp.int32)
    place_ids = jnp.arange(per_rows + 2, dtype=jnp.int32)

    def apply_layer(state, parts, layer_weight, layer_gain):
        group_tiles, col_local, placing, from_below, from_above = parts
        block_view = state.reshape(per_rows, tile_size, feature_width)
        chosen_blocks = jnp.take(block_view, col_local, axis=0)
        products = jnp.einsum(
            "kab,kbd->kad", group_tiles, chosen_blocks, preferred_element_type=jnp.float32
        )
        partial_value = jnp.einsum(
            "kp,kad->pad", placing, products, precision=lax.Precision.HIGHEST
        )
        edge_states = jnp.concatenate([state[:tile_size], state[row_count - tile_size :]], axis=0)
        extended = extended_2(edge_states, (("shard", 0),), tile_size)
        below_block = extended[:tile_size].astype(jnp.float32)
        above_block = extended[extended.shape[0] - tile_size :].astype(jnp.float32)
        own_rows = partial_value.reshape(row_count, feature_width)
        own_rows = own_rows.at[:tile_size].add(
            jnp.dot(from_below, below_block, precision=lax.Precision.HIGHEST)
        )
        own_rows = own_rows.at[row_count - tile_size :].add(
            jnp.dot(from_above, above_block, precision=lax.Precision.HIGHEST)
        )
        aggregate = own_rows.astype(jnp.bfloat16)
        projected = jnp.dot(aggregate, layer_weight, preferred_element_type=jnp.float32)
        scale = lax.rsqrt(jnp.mean(projected * projected, axis=-1, keepdims=True) + 1e-06)
        normed = projected * scale * layer_gain.astype(jnp.float32)
        return (state.astype(jnp.float32) + jax.nn.gelu(normed)).astype(jnp.bfloat16)

    layer_mats, layer_gains = (
        lax.all_gather(weights, "section", axis=0, tiled=True),
        lax.all_gather(gains, "section", axis=0, tiled=True),
    )
    batch_index = section_index * per_section + 0
    group_tiles = lax.dynamic_index_in_dim(tiles, batch_index, 0, keepdims=False)
    group_rows = lax.dynamic_index_in_dim(tile_rows, batch_index, 0, keepdims=False)
    group_cols = lax.dynamic_index_in_dim(tile_cols, batch_index, 0, keepdims=False)
    group_live = lax.dynamic_index_in_dim(tile_live, batch_index, 0, keepdims=False)
    col_local = group_cols - shard_index * per_rows
    slot_local = group_rows - (shard_index * per_rows - 1)
    live_mask = (slot_ids < group_live[0]).astype(jnp.float32)
    placing = (slot_local[:, None] == place_ids[None, :]).astype(jnp.float32) * live_mask[:, None]
    edge_pick = jnp.stack([placing[:, 0], placing[:, per_rows + 1]], axis=1)
    edge_tiles = jnp.einsum(
        "kp,kab->pab", edge_pick, group_tiles.astype(jnp.float32), precision=lax.Precision.HIGHEST
    )
    received = extended_2(edge_tiles, (("shard", 0),), 1)
    parts = (group_tiles, col_local, placing[:, 1 : per_rows + 1], received[0], received[3])

    def through(layer_index, state):
        return apply_layer(state, parts, layer_mats[layer_index], layer_gains[layer_index])

    group_labels = lax.dynamic_index_in_dim(labels, batch_index, 0, keepdims=False)
    group_features = lax.dynamic_index_in_dim(features, batch_index, 0, keepdims=False)
    labels_hot = (
        group_labels[:, None] == jnp.arange(label_count, dtype=jnp.int32)[None, :]
    ).astype(jnp.float32)
    embedded = jnp.dot(labels_hot, label_table, precision=lax.Precision.HIGHEST)
    state = lax.fori_loop(
        0,
        section_count,
        through,
        (group_features.astype(jnp.float32) + embedded).astype(jnp.bfloat16),
    )
    results = [jnp.dot(state.astype(jnp.float32), head_weight, precision=lax.Precision.HIGHEST)]
    return jnp.stack(results)


def solution(mesh):
    return jax.shard_map(
        paired if mesh.shape["section"] == 2 else body,
        mesh=mesh,
        in_specs=(
            P(None, "shard", None),
            P(None, "shard"),
            P(),
            P(None, "shard", None, None),
            P(None, "shard"),
            P(None, "shard"),
            P(None, "shard"),
            P("section", None, None),
            P("section", None),
            P(),
        ),
        out_specs=P("section", "shard"),
        check_vma=False,
    )
```

```python
import jax
import jax.numpy as jnp
from jax import lax
from jax.experimental import pallas as pl
from jax.experimental.pallas import tpu as pltpu
from jax.sharding import PartitionSpec as P

BF16 = jnp.bfloat16
F32 = jnp.float32
PAD = 16


def split3(value):
    high = value.astype(BF16).astype(F32)
    rest = value - high
    mid = rest.astype(BF16).astype(F32)
    return high, mid, rest - mid


def dot(a, b, dims=((1,), (0,))):
    return lax.dot_general(a, b, (dims, ((), ())), preferred_element_type=F32)


def in_hbm(*arrays):
    return [pltpu.with_memory_space_constraint(array, pltpu.HBM) for array in arrays]


def layer(aggregate, weight, gain, state):
    projected = dot(aggregate, weight)
    scale = lax.rsqrt(jnp.mean(projected * projected, axis=-1, keepdims=True) + 1e-06)
    normed = projected * scale * gain
    return (state.astype(F32) + jax.nn.gelu(normed)).astype(BF16)


def first_kernel(
    tile_rows, tile_cols, tile_live, labels, label_table, gains, features, tiles, weights,
    near, far, crossing, state_out, adjacency_out,
    rows_buf, cols_buf, live_buf, labels_buf, classes_buf, gains_buf, features_buf, tiles_buf, table_buf, sums, sems,
):
    section = lax.axis_index("section")
    shard = lax.axis_index("shard")
    parity = lax.rem(shard, 2)
    rows, width = features_buf.shape
    slots, size, _ = tiles_buf.shape
    blocks = rows // size
    kept = crossing.shape[0] - PAD
    group = section

    half = weights.at[0, pl.ds(pl.multiple_of(parity * kept, kept), kept)]
    copies = [
        pltpu.make_async_copy(source, target, sems.at[index])
        for index, (source, target) in enumerate((
            (tile_rows, rows_buf),
            (tile_cols, cols_buf),
            (tile_live, live_buf),
            (tiles.at[group], tiles_buf),
            (labels, labels_buf),
            (label_table, classes_buf),
            (features.at[group], features_buf),
            (gains, gains_buf),
            (half, crossing.at[pl.ds(0, kept)]),
        ))
    ]
    for copy in copies:
        copy.start()
    sums[...] = jnp.zeros_like(sums)
    table_buf[...] = jnp.zeros_like(table_buf)

    for copy in copies[:4]:
        copy.wait()
    for slot in range(slots):
        @pl.when(slot < live_buf[0, group])
        def _():
            row = rows_buf[group, slot] - (shard * blocks - 1)
            col = cols_buf[group, slot] - shard * blocks
            place = (pl.ds(pl.multiple_of(row * size, size), size), pl.ds(pl.multiple_of(col * size, size), size))
            sums[place] += tiles_buf[slot].astype(F32)
    adjacency = sums[...].astype(BF16)
    adjacency_out[...] = adjacency

    copies[4].wait()
    copies[5].wait()
    classes = classes_buf.shape[0]
    for part, value in enumerate(split3(classes_buf[...])):
        table_buf[pl.ds(part * classes, classes), :] = value
    depth = table_buf.shape[0]
    index = lax.broadcasted_iota(jnp.int32, (depth, rows), 0)
    wanted = jnp.where(
        index < classes, index,
        jnp.where(index < 2 * classes, index - classes, jnp.where(index < 3 * classes, index - 2 * classes, -1)),
    )
    hot = (wanted == labels_buf[pl.ds(group, 1), :]).astype(F32).astype(BF16)
    embedded = dot(hot, table_buf[...].astype(BF16), ((0,), (0,)))

    copies[6].wait()
    state = (features_buf[...].astype(F32) + embedded).astype(BF16)
    state_out[...] = state
    partial = dot(adjacency[size : size + rows], state).astype(BF16)

    def write(target, block, edge):
        target[:, pl.ds(0, width)] = partial[block * size : (block + 1) * size]
        target[:, pl.ds(width, width)] = state[block * size : (block + 1) * size]
        target[:, pl.ds(2 * width, size)] = edge

    upper = adjacency[rows + size :, rows - size :]
    lower = adjacency[:size, :size]

    @pl.when(parity == 0)
    def _():
        write(near, blocks - 1, upper)
        write(far, 0, lower)

    @pl.when(parity == 1)
    def _():
        write(far, blocks - 1, upper)
        write(near, 0, lower)

    copies[7].wait()
    crossing[pl.ds(kept, PAD), :] = jnp.broadcast_to(gains_buf[...].astype(F32), (PAD, width)).astype(BF16)
    copies[8].wait()


def second_kernel(
    adjacency, state_own, near, far, crossed, relayed, head, gains, weights,
    outcome,
    ext_state, mats, wide, next_state, head_buf, gains_buf, split_buf, sems,
):
    section = lax.axis_index("section")
    parity = lax.rem(lax.axis_index("shard"), 2)
    rows, width = state_own.shape
    size = near.shape[0]
    kept = mats.shape[1] // 2
    other = 1 - section
    copies = [
        pltpu.make_async_copy(source, target, sems.at[index])
        for index, (source, target) in enumerate((
            (weights.at[0], mats.at[section]),
            (gains, gains_buf),
            (head, head_buf),
            (crossed.at[pl.ds(0, kept)], mats.at[other, pl.ds(pl.multiple_of(parity * kept, kept), kept)]),
            (relayed.at[pl.ds(0, kept)], mats.at[other, pl.ds(pl.multiple_of((1 - parity) * kept, kept), kept)]),
        ))
    ]
    for copy in copies:
        copy.start()

    even = parity == 0

    def sides(columns):
        one, two = near[:, columns], far[:, columns]
        return jnp.where(even, two, one), jnp.where(even, one, two)

    low_partial, high_partial = sides(pl.ds(0, width))
    low_state, high_state = sides(pl.ds(width, width))
    low_tile, high_tile = sides(pl.ds(2 * width, size))
    wide[...] = jnp.zeros_like(wide)
    wide[pl.ds(0, size), pl.ds(0, size)] = low_tile
    wide[pl.ds(rows - size, size), pl.ds(size + rows, size)] = high_tile
    wide[:, pl.ds(size, rows)] = adjacency[pl.ds(size, rows), :]
    own = state_own[...]
    ext_state[pl.ds(0, size), :] = low_state
    ext_state[pl.ds(size, rows), :] = own
    ext_state[pl.ds(size + rows, size), :] = high_state

    low_aggregate = (dot(adjacency[pl.ds(0, size), :], own) + low_partial.astype(F32)).astype(BF16)
    high_aggregate = (dot(adjacency[pl.ds(size + rows, size), :], own) + high_partial.astype(F32)).astype(BF16)
    aggregate = dot(wide[...], ext_state[...]).astype(BF16)

    copies[1].wait()
    own_gain = gains_buf[...].astype(F32)
    got_gain = crossed[pl.ds(kept, PAD), :].astype(F32)[0:1]
    first = section == 0
    gain = (jnp.where(first, own_gain, got_gain), jnp.where(first, got_gain, own_gain))

    copies[0].wait()
    copies[3].wait()
    copies[4].wait()
    weight = mats[0]
    next_state[pl.ds(0, size), :] = layer(low_aggregate, weight, gain[0], low_state)
    next_state[pl.ds(size, rows), :] = layer(aggregate, weight, gain[0], own)
    next_state[pl.ds(size + rows, size), :] = layer(high_aggregate, weight, gain[0], high_state)

    aggregate = dot(wide[...], next_state[...]).astype(BF16)
    state = layer(aggregate, mats[1], gain[1], next_state[pl.ds(size, rows), :])
    copies[2].wait()
    split_buf[...] = jnp.zeros_like(split_buf)
    for part, value in enumerate(split3(head_buf[...])):
        split_buf[pl.ds(part, 1), :] = value
    scores = dot(split_buf[...].astype(BF16), state, ((1,), (1,)))
    outcome[...] = scores[0:1] + scores[1:2] + scores[2:3]


def paired(features, labels, label_table, tiles, tile_rows, tile_cols, tile_live, weights, gains, head_weight):
    shard_count = lax.axis_size("shard")
    groups, rows, width = features.shape
    _, slots, size, _ = tiles.shape
    depth = weights.shape[1]
    kept = depth // 2
    classes = label_table.shape[0]
    message = jax.ShapeDtypeStruct((size, 2 * width + size), BF16)
    vmem = pl.BlockSpec(memory_space=pltpu.VMEM)
    hbm = pl.BlockSpec(memory_space=pltpu.HBM)
    table_rows = -(-3 * classes // PAD) * PAD

    near, far, crossing, state, adjacency = pl.pallas_call(
        first_kernel,
        out_shape=(
            message,
            message,
            jax.ShapeDtypeStruct((kept + PAD, width), BF16),
            jax.ShapeDtypeStruct((rows, width), BF16),
            jax.ShapeDtypeStruct((rows + 2 * size, rows), BF16),
        ),
        in_specs=[hbm] * 9,
        out_specs=(vmem,) * 5,
        scratch_shapes=[
            pltpu.SMEM((groups, slots), jnp.int32),
            pltpu.SMEM((groups, slots), jnp.int32),
            pltpu.SMEM((1, groups), jnp.int32),
            pltpu.VMEM((groups, rows), jnp.int32),
            pltpu.VMEM((classes, width), F32),
            pltpu.VMEM((1, width), BF16),
            pltpu.VMEM((rows, width), BF16),
            pltpu.VMEM((slots, size, size), BF16),
            pltpu.VMEM((table_rows, width), F32),
            pltpu.VMEM((rows + 2 * size, rows), F32),
            pltpu.SemaphoreType.DMA((9,)),
        ],
        compiler_params=pltpu.CompilerParams(vmem_limit_bytes=16 * 2**20),
        name="messages",
    )(*in_hbm(tile_rows, tile_cols, tile_live.T, labels, label_table, gains, features, tiles, weights))

    beside = [(i, i ^ 1) for i in range(shard_count)]
    apart = [(i, (i + 1) % shard_count) for i in range(1, shard_count, 2)]
    apart += [(b, a) for a, b in apart]
    far = lax.ppermute(far, "shard", apart)
    crossed = lax.ppermute(crossing, "section", [(0, 1), (1, 0)])
    near = lax.ppermute(near, "shard", beside)
    relayed = lax.ppermute(crossed, "shard", beside)

    return pl.pallas_call(
        second_kernel,
        out_shape=jax.ShapeDtypeStruct((1, rows), F32),
        in_specs=[vmem] * 6 + [hbm] * 3,
        out_specs=vmem,
        scratch_shapes=[
            pltpu.VMEM((rows + 2 * size, width), BF16),
            pltpu.VMEM((2, depth, width), BF16),
            pltpu.VMEM((rows, rows + 2 * size), BF16),
            pltpu.VMEM((rows + 2 * size, width), BF16),
            pltpu.VMEM((1, width), F32),
            pltpu.VMEM((1, width), BF16),
            pltpu.VMEM((PAD, width), F32),
            pltpu.SemaphoreType.DMA((5,)),
        ],
        compiler_params=pltpu.CompilerParams(vmem_limit_bytes=32 * 2**20),
        name="layers",
    )(adjacency, state, near, far, crossed, relayed, *in_hbm(head_weight.reshape(1, width), gains, weights))


def extended_2(block, sides, width):
    for axis, dim in sides:
        count = lax.axis_size(axis)
        forward = [(i, i + 1) for i in range(count - 1)]
        backward = [(target, source) for source, target in forward]
        low = lax.ppermute(
            lax.slice_in_dim(block, block.shape[dim] - width, None, axis=dim), axis, forward
        )
        high = lax.ppermute(lax.slice_in_dim(block, 0, width, axis=dim), axis, backward)
        block = jnp.concatenate([low, block, high], axis=dim)
    return block


def body(
    features,
    labels,
    label_table,
    tiles,
    tile_rows,
    tile_cols,
    tile_live,
    weights,
    gains,
    head_weight,
):
    section_count = lax.axis_size("section")
    section_index = lax.axis_index("section")
    shard_index = lax.axis_index("shard")
    batch_count = features.shape[0]
    row_count = features.shape[1]
    feature_width = features.shape[2]
    tile_size = tiles.shape[2]
    slot_count = tiles.shape[1]
    label_count = label_table.shape[0]
    per_rows = row_count // tile_size
    per_section = batch_count // section_count
    slot_ids = jnp.arange(slot_count, dtype=jnp.int32)
    place_ids = jnp.arange(per_rows + 2, dtype=jnp.int32)

    def apply_layer(state, parts, layer_weight, layer_gain):
        group_tiles, col_local, placing, from_below, from_above = parts
        block_view = state.reshape(per_rows, tile_size, feature_width)
        chosen_blocks = jnp.take(block_view, col_local, axis=0)
        products = jnp.einsum(
            "kab,kbd->kad", group_tiles, chosen_blocks, preferred_element_type=jnp.float32
        )
        partial_value = jnp.einsum(
            "kp,kad->pad", placing, products, precision=lax.Precision.HIGHEST
        )
        edge_states = jnp.concatenate([state[:tile_size], state[row_count - tile_size :]], axis=0)
        extended = extended_2(edge_states, (("shard", 0),), tile_size)
        below_block = extended[:tile_size].astype(jnp.float32)
        above_block = extended[extended.shape[0] - tile_size :].astype(jnp.float32)
        own_rows = partial_value.reshape(row_count, feature_width)
        own_rows = own_rows.at[:tile_size].add(
            jnp.dot(from_below, below_block, precision=lax.Precision.HIGHEST)
        )
        own_rows = own_rows.at[row_count - tile_size :].add(
            jnp.dot(from_above, above_block, precision=lax.Precision.HIGHEST)
        )
        aggregate = own_rows.astype(jnp.bfloat16)
        projected = jnp.dot(aggregate, layer_weight, preferred_element_type=jnp.float32)
        scale = lax.rsqrt(jnp.mean(projected * projected, axis=-1, keepdims=True) + 1e-06)
        normed = projected * scale * layer_gain.astype(jnp.float32)
        return (state.astype(jnp.float32) + jax.nn.gelu(normed)).astype(jnp.bfloat16)

    layer_mats, layer_gains = (
        lax.all_gather(weights, "section", axis=0, tiled=True),
        lax.all_gather(gains, "section", axis=0, tiled=True),
    )
    batch_index = section_index * per_section + 0
    group_tiles = lax.dynamic_index_in_dim(tiles, batch_index, 0, keepdims=False)
    group_rows = lax.dynamic_index_in_dim(tile_rows, batch_index, 0, keepdims=False)
    group_cols = lax.dynamic_index_in_dim(tile_cols, batch_index, 0, keepdims=False)
    group_live = lax.dynamic_index_in_dim(tile_live, batch_index, 0, keepdims=False)
    col_local = group_cols - shard_index * per_rows
    slot_local = group_rows - (shard_index * per_rows - 1)
    live_mask = (slot_ids < group_live[0]).astype(jnp.float32)
    placing = (slot_local[:, None] == place_ids[None, :]).astype(jnp.float32) * live_mask[:, None]
    edge_pick = jnp.stack([placing[:, 0], placing[:, per_rows + 1]], axis=1)
    edge_tiles = jnp.einsum(
        "kp,kab->pab", edge_pick, group_tiles.astype(jnp.float32), precision=lax.Precision.HIGHEST
    )
    received = extended_2(edge_tiles, (("shard", 0),), 1)
    parts = (group_tiles, col_local, placing[:, 1 : per_rows + 1], received[0], received[3])

    def through(layer_index, state):
        return apply_layer(state, parts, layer_mats[layer_index], layer_gains[layer_index])

    group_labels = lax.dynamic_index_in_dim(labels, batch_index, 0, keepdims=False)
    group_features = lax.dynamic_index_in_dim(features, batch_index, 0, keepdims=False)
    labels_hot = (
        group_labels[:, None] == jnp.arange(label_count, dtype=jnp.int32)[None, :]
    ).astype(jnp.float32)
    embedded = jnp.dot(labels_hot, label_table, precision=lax.Precision.HIGHEST)
    state = lax.fori_loop(
        0,
        section_count,
        through,
        (group_features.astype(jnp.float32) + embedded).astype(jnp.bfloat16),
    )
    results = [jnp.dot(state.astype(jnp.float32), head_weight, precision=lax.Precision.HIGHEST)]
    return jnp.stack(results)


def solution(mesh):
    return jax.shard_map(
        paired if mesh.shape["section"] == 2 else body,
        mesh=mesh,
        in_specs=(
            P(None, "shard", None),
            P(None, "shard"),
            P(),
            P(None, "shard", None, None),
            P(None, "shard"),
            P(None, "shard"),
            P(None, "shard"),
            P("section", None, None),
            P("section", None),
            P(),
        ),
        out_specs=P("section", "shard"),
        check_vma=False,
    )
```

```python
import jax
import jax.numpy as jnp
from jax import lax
from jax.experimental import pallas as pl
from jax.experimental.pallas import tpu as pltpu
from jax.sharding import PartitionSpec as P

BF16 = jnp.bfloat16
F32 = jnp.float32
PAD = 16
GELU_LINEAR = (2.0 / 3.141592653589793) ** 0.5
GELU_CUBIC = GELU_LINEAR * 0.044715


def split3(value):
    high = value.astype(BF16).astype(F32)
    rest = value - high
    mid = rest.astype(BF16).astype(F32)
    return high, mid, rest - mid


def dot(a, b, dims=((1,), (0,))):
    return lax.dot_general(a, b, (dims, ((), ())), preferred_element_type=F32)


def in_hbm(*arrays):
    return [pltpu.with_memory_space_constraint(array, pltpu.HBM) for array in arrays]


def layer(aggregate, weight, gain, state):
    projected = dot(aggregate, weight)
    scale = lax.rsqrt(jnp.mean(projected * projected, axis=-1, keepdims=True) + 1e-06)
    normed = projected * scale * gain
    inner = normed * (GELU_LINEAR + GELU_CUBIC * (normed * normed))
    half = 0.5 * normed
    return (state.astype(F32) + (half + half * jnp.tanh(inner))).astype(BF16)


def first_kernel(
    tile_rows, tile_cols, tile_live, labels, label_table, gains, features, tiles, weights,
    far, near, crossing, state_out, adjacency_out,
    rows_buf, cols_buf, live_buf, labels_buf, classes_buf, gains_buf, features_buf, tiles_buf, table_buf, sums, sems,
):
    section = lax.axis_index("section")
    shard = lax.axis_index("shard")
    parity = lax.rem(shard, 2)
    rows, width = features_buf.shape
    slots, size, _ = tiles_buf.shape
    blocks = rows // size
    kept = crossing.shape[0] - PAD
    group = section

    half = weights.at[0, pl.ds(pl.multiple_of(parity * kept, kept), kept)]
    copies = [
        pltpu.make_async_copy(source, target, sems.at[index])
        for index, (source, target) in enumerate((
            (tile_rows, rows_buf),
            (tile_cols, cols_buf),
            (tile_live, live_buf),
            (tiles.at[group], tiles_buf),
            (labels, labels_buf),
            (label_table, classes_buf),
            (features.at[group], features_buf),
            (gains, gains_buf),
            (half, crossing.at[pl.ds(0, kept)]),
        ))
    ]
    for copy in copies:
        copy.start()
    sums[...] = jnp.zeros_like(sums)
    table_buf[...] = jnp.zeros_like(table_buf)

    for copy in copies[:4]:
        copy.wait()
    for slot in range(slots):
        @pl.when(slot < live_buf[0, group])
        def _():
            row = rows_buf[group, slot] - (shard * blocks - 1)
            col = cols_buf[group, slot] - shard * blocks
            place = (pl.ds(pl.multiple_of(row * size, size), size), pl.ds(pl.multiple_of(col * size, size), size))
            sums[place] += tiles_buf[slot].astype(F32)
    adjacency = sums[...].astype(BF16)
    adjacency_out[...] = adjacency

    copies[4].wait()
    copies[5].wait()
    classes = classes_buf.shape[0]
    for part, value in enumerate(split3(classes_buf[...])):
        table_buf[pl.ds(part * classes, classes), :] = value
    depth = table_buf.shape[0]
    index = lax.broadcasted_iota(jnp.int32, (depth, rows), 0)
    wanted = jnp.where(
        index < classes, index,
        jnp.where(index < 2 * classes, index - classes, jnp.where(index < 3 * classes, index - 2 * classes, -1)),
    )
    hot = (wanted == labels_buf[pl.ds(group, 1), :]).astype(F32).astype(BF16)
    embedded = dot(hot, table_buf[...].astype(BF16), ((0,), (0,)))

    copies[6].wait()
    state = (features_buf[...].astype(F32) + embedded).astype(BF16)
    state_out[...] = state
    partial = dot(adjacency[size : size + rows], state).astype(BF16)

    def write(target, block, edge):
        target[:, pl.ds(0, width)] = partial[block * size : (block + 1) * size]
        target[:, pl.ds(width, width)] = state[block * size : (block + 1) * size]
        target[:, pl.ds(2 * width, size)] = edge

    upper = adjacency[rows + size :, rows - size :]
    lower = adjacency[:size, :size]

    @pl.when(parity == 0)
    def _():
        write(near, blocks - 1, upper)
        write(far, 0, lower)

    @pl.when(parity == 1)
    def _():
        write(far, blocks - 1, upper)
        write(near, 0, lower)

    copies[7].wait()
    crossing[pl.ds(kept, PAD), :] = jnp.broadcast_to(gains_buf[...].astype(F32), (PAD, width)).astype(BF16)
    copies[8].wait()


def waiting_kernel(
    adjacency, state, head, gains, weights,
    aggregate, weight, own_gain, head_parts,
    head_buf, gains_buf, parts_buf, sems,
):
    copies = [
        pltpu.make_async_copy(source, target, sems.at[index])
        for index, (source, target) in enumerate(((weights.at[0], weight), (head, head_buf), (gains, gains_buf)))
    ]
    for copy in copies:
        copy.start()
    aggregate[...] = dot(adjacency[...], state[...])
    parts_buf[...] = jnp.zeros_like(parts_buf)
    for copy in copies[1:]:
        copy.wait()
    for part, value in enumerate(split3(head_buf[...])):
        parts_buf[pl.ds(part, 1), :] = value
    head_parts[...] = parts_buf[...].astype(BF16)
    own_gain[...] = gains_buf[...].astype(F32)
    copies[0].wait()


def second_kernel(
    adjacency, state_own, far, near, crossed, relayed, aggregate, own_weight, own_gain, head_parts,
    outcome,
    mats, next_state,
):
    first = lax.axis_index("section") == 0
    even = lax.rem(lax.axis_index("shard"), 2) == 0
    rows, width = state_own.shape
    size = near.shape[0]
    kept = mats.shape[1] // 2

    for place, (one, two) in enumerate(((crossed, relayed), (relayed, crossed))):
        span = pl.ds(place * kept, kept)
        own = own_weight[span, :]
        got = jnp.where(even, one[pl.ds(0, kept), :], two[pl.ds(0, kept), :])
        mats[0, span, :] = jnp.where(first, own, got)
        mats[1, span, :] = jnp.where(first, got, own)
    got_gain = crossed[pl.ds(kept, PAD), :].astype(F32)[0:1]
    gain = (jnp.where(first, own_gain[...], got_gain), jnp.where(first, got_gain, own_gain[...]))

    def sides(columns):
        one, two = near[:, columns], far[:, columns]
        return jnp.where(even, two, one), jnp.where(even, one, two)

    low_partial, high_partial = sides(pl.ds(0, width))
    low_state, high_state = sides(pl.ds(width, width))
    low_tile, high_tile = sides(pl.ds(2 * width, size))

    def halo(partial, start):
        return (aggregate[pl.ds(start, size), :] + partial.astype(F32)).astype(BF16)

    def inner(low, high, start):
        parts = [aggregate[pl.ds(start, rows), :]] if start is not None else [dot(adjacency[pl.ds(size, rows), :], next_state[pl.ds(size, rows), :])]
        return parts[0], dot(low_tile, low), dot(high_tile, high)

    def joined(total, low, high):
        middle = [total[size : rows - size]] if rows > 2 * size else []
        return jnp.concatenate([total[:size] + low, *middle, total[rows - size :] + high], axis=0).astype(BF16)

    weight = mats[0]
    next_state[pl.ds(0, size), :] = layer(halo(low_partial, 0), weight, gain[0], low_state)
    next_state[pl.ds(size + rows, size), :] = layer(halo(high_partial, size + rows), weight, gain[0], high_state)
    next_state[pl.ds(size, rows), :] = layer(joined(*inner(low_state, high_state, size)), weight, gain[0], state_own[...])

    low, high = next_state[pl.ds(0, size), :], next_state[pl.ds(size + rows, size), :]
    state = layer(joined(*inner(low, high, None)), mats[1], gain[1], next_state[pl.ds(size, rows), :])
    scores = dot(head_parts[...], state, ((1,), (1,)))
    outcome[...] = scores[0:1] + scores[1:2] + scores[2:3]


def paired(features, labels, label_table, tiles, tile_rows, tile_cols, tile_live, weights, gains, head_weight):
    shard_count = lax.axis_size("shard")
    groups, rows, width = features.shape
    _, slots, size, _ = tiles.shape
    depth = weights.shape[1]
    kept = depth // 2
    classes = label_table.shape[0]
    message = jax.ShapeDtypeStruct((size, 2 * width + size), BF16)
    vmem = pl.BlockSpec(memory_space=pltpu.VMEM)
    hbm = pl.BlockSpec(memory_space=pltpu.HBM)
    table_rows = -(-3 * classes // PAD) * PAD

    far, near, crossing, state, adjacency = pl.pallas_call(
        first_kernel,
        out_shape=(
            message,
            message,
            jax.ShapeDtypeStruct((kept + PAD, width), BF16),
            jax.ShapeDtypeStruct((rows, width), BF16),
            jax.ShapeDtypeStruct((rows + 2 * size, rows), BF16),
        ),
        in_specs=[hbm] * 9,
        out_specs=(vmem,) * 5,
        scratch_shapes=[
            pltpu.SMEM((groups, slots), jnp.int32),
            pltpu.SMEM((groups, slots), jnp.int32),
            pltpu.SMEM((1, groups), jnp.int32),
            pltpu.VMEM((groups, rows), jnp.int32),
            pltpu.VMEM((classes, width), F32),
            pltpu.VMEM((1, width), BF16),
            pltpu.VMEM((rows, width), BF16),
            pltpu.VMEM((slots, size, size), BF16),
            pltpu.VMEM((table_rows, width), F32),
            pltpu.VMEM((rows + 2 * size, rows), F32),
            pltpu.SemaphoreType.DMA((9,)),
        ],
        compiler_params=pltpu.CompilerParams(vmem_limit_bytes=16 * 2**20),
        name="messages",
    )(*in_hbm(tile_rows, tile_cols, tile_live.T, labels, label_table, gains, features, tiles, weights))

    beside = [(i, i ^ 1) for i in range(shard_count)]
    apart = [(i, (i + 1) % shard_count) for i in range(1, shard_count, 2)]
    apart += [(b, a) for a, b in apart]
    far = lax.ppermute(far, "shard", apart)
    crossed = lax.ppermute(crossing, "section", [(0, 1), (1, 0)])
    near = lax.ppermute(near, "shard", beside)
    relayed = lax.ppermute(crossed, "shard", beside)

    aggregate, own_weight, own_gain, head_parts = pl.pallas_call(
        waiting_kernel,
        out_shape=(
            jax.ShapeDtypeStruct((rows + 2 * size, width), F32),
            jax.ShapeDtypeStruct((depth, width), BF16),
            jax.ShapeDtypeStruct((1, width), F32),
            jax.ShapeDtypeStruct((PAD, width), BF16),
        ),
        in_specs=[vmem] * 2 + [hbm] * 3,
        out_specs=(vmem,) * 4,
        scratch_shapes=[
            pltpu.VMEM((1, width), F32),
            pltpu.VMEM((1, width), BF16),
            pltpu.VMEM((PAD, width), F32),
            pltpu.SemaphoreType.DMA((3,)),
        ],
        compiler_params=pltpu.CompilerParams(vmem_limit_bytes=16 * 2**20),
        name="waiting",
    )(adjacency, state, *in_hbm(head_weight.reshape(1, width), gains, weights))

    return pl.pallas_call(
        second_kernel,
        out_shape=jax.ShapeDtypeStruct((1, rows), F32),
        in_specs=[vmem] * 10,
        out_specs=vmem,
        scratch_shapes=[
            pltpu.VMEM((2, depth, width), BF16),
            pltpu.VMEM((rows + 2 * size, width), BF16),
        ],
        compiler_params=pltpu.CompilerParams(vmem_limit_bytes=32 * 2**20),
        name="layers",
    )(adjacency, state, far, near, crossed, relayed, aggregate, own_weight, own_gain, head_parts)


def extended_2(block, sides, width):
    for axis, dim in sides:
        count = lax.axis_size(axis)
        forward = [(i, i + 1) for i in range(count - 1)]
        backward = [(target, source) for source, target in forward]
        low = lax.ppermute(
            lax.slice_in_dim(block, block.shape[dim] - width, None, axis=dim), axis, forward
        )
        high = lax.ppermute(lax.slice_in_dim(block, 0, width, axis=dim), axis, backward)
        block = jnp.concatenate([low, block, high], axis=dim)
    return block


def body(
    features,
    labels,
    label_table,
    tiles,
    tile_rows,
    tile_cols,
    tile_live,
    weights,
    gains,
    head_weight,
):
    section_count = lax.axis_size("section")
    section_index = lax.axis_index("section")
    shard_index = lax.axis_index("shard")
    batch_count = features.shape[0]
    row_count = features.shape[1]
    feature_width = features.shape[2]
    tile_size = tiles.shape[2]
    slot_count = tiles.shape[1]
    label_count = label_table.shape[0]
    per_rows = row_count // tile_size
    per_section = batch_count // section_count
    slot_ids = jnp.arange(slot_count, dtype=jnp.int32)
    place_ids = jnp.arange(per_rows + 2, dtype=jnp.int32)

    def apply_layer(state, parts, layer_weight, layer_gain):
        group_tiles, col_local, placing, from_below, from_above = parts
        block_view = state.reshape(per_rows, tile_size, feature_width)
        chosen_blocks = jnp.take(block_view, col_local, axis=0)
        products = jnp.einsum(
            "kab,kbd->kad", group_tiles, chosen_blocks, preferred_element_type=jnp.float32
        )
        partial_value = jnp.einsum(
            "kp,kad->pad", placing, products, precision=lax.Precision.HIGHEST
        )
        edge_states = jnp.concatenate([state[:tile_size], state[row_count - tile_size :]], axis=0)
        extended = extended_2(edge_states, (("shard", 0),), tile_size)
        below_block = extended[:tile_size].astype(jnp.float32)
        above_block = extended[extended.shape[0] - tile_size :].astype(jnp.float32)
        own_rows = partial_value.reshape(row_count, feature_width)
        own_rows = own_rows.at[:tile_size].add(
            jnp.dot(from_below, below_block, precision=lax.Precision.HIGHEST)
        )
        own_rows = own_rows.at[row_count - tile_size :].add(
            jnp.dot(from_above, above_block, precision=lax.Precision.HIGHEST)
        )
        aggregate = own_rows.astype(jnp.bfloat16)
        projected = jnp.dot(aggregate, layer_weight, preferred_element_type=jnp.float32)
        scale = lax.rsqrt(jnp.mean(projected * projected, axis=-1, keepdims=True) + 1e-06)
        normed = projected * scale * layer_gain.astype(jnp.float32)
        return (state.astype(jnp.float32) + jax.nn.gelu(normed)).astype(jnp.bfloat16)

    layer_mats, layer_gains = (
        lax.all_gather(weights, "section", axis=0, tiled=True),
        lax.all_gather(gains, "section", axis=0, tiled=True),
    )
    batch_index = section_index * per_section + 0
    group_tiles = lax.dynamic_index_in_dim(tiles, batch_index, 0, keepdims=False)
    group_rows = lax.dynamic_index_in_dim(tile_rows, batch_index, 0, keepdims=False)
    group_cols = lax.dynamic_index_in_dim(tile_cols, batch_index, 0, keepdims=False)
    group_live = lax.dynamic_index_in_dim(tile_live, batch_index, 0, keepdims=False)
    col_local = group_cols - shard_index * per_rows
    slot_local = group_rows - (shard_index * per_rows - 1)
    live_mask = (slot_ids < group_live[0]).astype(jnp.float32)
    placing = (slot_local[:, None] == place_ids[None, :]).astype(jnp.float32) * live_mask[:, None]
    edge_pick = jnp.stack([placing[:, 0], placing[:, per_rows + 1]], axis=1)
    edge_tiles = jnp.einsum(
        "kp,kab->pab", edge_pick, group_tiles.astype(jnp.float32), precision=lax.Precision.HIGHEST
    )
    received = extended_2(edge_tiles, (("shard", 0),), 1)
    parts = (group_tiles, col_local, placing[:, 1 : per_rows + 1], received[0], received[3])

    def through(layer_index, state):
        return apply_layer(state, parts, layer_mats[layer_index], layer_gains[layer_index])

    group_labels = lax.dynamic_index_in_dim(labels, batch_index, 0, keepdims=False)
    group_features = lax.dynamic_index_in_dim(features, batch_index, 0, keepdims=False)
    labels_hot = (
        group_labels[:, None] == jnp.arange(label_count, dtype=jnp.int32)[None, :]
    ).astype(jnp.float32)
    embedded = jnp.dot(labels_hot, label_table, precision=lax.Precision.HIGHEST)
    state = lax.fori_loop(
        0,
        section_count,
        through,
        (group_features.astype(jnp.float32) + embedded).astype(jnp.bfloat16),
    )
    results = [jnp.dot(state.astype(jnp.float32), head_weight, precision=lax.Precision.HIGHEST)]
    return jnp.stack(results)


def solution(mesh):
    return jax.shard_map(
        paired if mesh.shape["section"] == 2 else body,
        mesh=mesh,
        in_specs=(
            P(None, "shard", None),
            P(None, "shard"),
            P(),
            P(None, "shard", None, None),
            P(None, "shard"),
            P(None, "shard"),
            P(None, "shard"),
            P("section", None, None),
            P("section", None),
            P(),
        ),
        out_specs=P("section", "shard"),
        check_vma=False,
    )
```

```python
import jax
import jax.numpy as jnp
from jax import lax
from jax.experimental import pallas as pl
from jax.experimental.pallas import tpu as pltpu
from jax.sharding import PartitionSpec as P

BF16 = jnp.bfloat16
F32 = jnp.float32
PAD = 16
GELU_LINEAR = 2.0 * (2.0 / 3.141592653589793) ** 0.5
GELU_CUBIC = 4.0 * GELU_LINEAR * 0.044715


def split3(value):
    high = value.astype(BF16).astype(F32)
    rest = value - high
    mid = rest.astype(BF16).astype(F32)
    return high, mid, rest - mid


def dot(a, b, dims=((1,), (0,))):
    return lax.dot_general(a, b, (dims, ((), ())), preferred_element_type=F32)


def in_hbm(*arrays):
    return [pltpu.with_memory_space_constraint(array, pltpu.HBM) for array in arrays]


def layer(aggregate, weight, half_gain, state):
    projected = dot(aggregate, weight)
    scale = lax.rsqrt(jnp.mean(projected * projected, axis=-1, keepdims=True) + 1e-06)
    half = projected * scale * half_gain
    inner = half * (GELU_LINEAR + GELU_CUBIC * (half * half))
    return (state.astype(F32) + (half + half * jnp.tanh(inner))).astype(BF16)


def first_kernel(
    tile_rows, tile_cols, tile_live, labels, label_table, tiles, features, weights, gains,
    far, near, crossing, gain_out, state_out, adjacency_out,
    rows_buf, cols_buf, live_buf, labels_buf, classes_buf, tiles_buf, features_buf, table_buf, sums, sems,
):
    section = lax.axis_index("section")
    shard = lax.axis_index("shard")
    parity = lax.rem(shard, 2)
    rows, width = features_buf.shape
    slots, size, _ = tiles_buf.shape
    blocks = rows // size
    kept = crossing.shape[0]
    group = section

    copies = [
        pltpu.make_async_copy(source, target, sems.at[index])
        for index, (source, target) in enumerate((
            (tile_rows, rows_buf),
            (tile_cols, cols_buf),
            (tile_live, live_buf),
            (labels, labels_buf),
            (label_table, classes_buf),
            (tiles.at[group], tiles_buf),
            (features.at[group], features_buf),
            (weights.at[0, pl.ds(pl.multiple_of(parity * kept, kept), kept)], crossing),
            (gains, gain_out),
        ))
    ]
    for copy in copies:
        copy.start()
    sums[...] = jnp.zeros_like(sums)
    table_buf[...] = jnp.zeros_like(table_buf)

    for copy in copies[3:5]:
        copy.wait()
    classes = classes_buf.shape[0]
    for part, value in enumerate(split3(classes_buf[...])):
        table_buf[pl.ds(part * classes, classes), :] = value
    depth = table_buf.shape[0]
    index = lax.broadcasted_iota(jnp.int32, (depth, rows), 0)
    wanted = jnp.where(
        index < classes, index,
        jnp.where(index < 2 * classes, index - classes, jnp.where(index < 3 * classes, index - 2 * classes, -1)),
    )
    hot = (wanted == labels_buf[pl.ds(group, 1), :]).astype(F32).astype(BF16)
    embedded = dot(hot, table_buf[...].astype(BF16), ((0,), (0,)))

    for copy in copies[:3] + copies[5:6]:
        copy.wait()
    for slot in range(slots):
        @pl.when(slot < live_buf[0, group])
        def _():
            row = rows_buf[group, slot] - (shard * blocks - 1)
            col = cols_buf[group, slot] - shard * blocks
            place = (pl.ds(pl.multiple_of(row * size, size), size), pl.ds(pl.multiple_of(col * size, size), size))
            sums[place] += tiles_buf[slot].astype(F32)
    adjacency = sums[...].astype(BF16)
    adjacency_out[...] = adjacency

    copies[6].wait()
    state = (features_buf[...].astype(F32) + embedded).astype(BF16)
    state_out[...] = state
    partial = dot(adjacency[size : size + rows], state).astype(BF16)

    def write(target, upward):
        target[:, pl.ds(0, width)] = jnp.where(upward, partial[rows - size :], partial[:size])
        target[:, pl.ds(width, width)] = jnp.where(upward, state[rows - size :], state[:size])
        target[:, pl.ds(2 * width, size)] = jnp.where(
            upward, adjacency[rows + size :, rows - size :], adjacency[:size, :size]
        )

    write(far, parity == 1)
    write(near, parity == 0)
    for copy in copies[7:]:
        copy.wait()


def waiting_kernel(
    adjacency, state, head, gains, weights,
    aggregate, weight, half_gain, head_parts,
    head_buf, gains_buf, parts_buf, sems,
):
    copies = [
        pltpu.make_async_copy(source, target, sems.at[index])
        for index, (source, target) in enumerate(((weights.at[0], weight), (head, head_buf), (gains, gains_buf)))
    ]
    for copy in copies:
        copy.start()
    aggregate[...] = dot(adjacency[...], state[...])
    parts_buf[...] = jnp.zeros_like(parts_buf)
    for copy in copies[1:]:
        copy.wait()
    for part, value in enumerate(split3(head_buf[...])):
        parts_buf[pl.ds(part, 1), :] = value
    head_parts[...] = parts_buf[...].astype(BF16)
    half_gain[...] = 0.5 * gains_buf[...].astype(F32)
    copies[0].wait()


def second_kernel(
    adjacency, state_own, far, near, other_gain, crossed, relayed, aggregate, own_weight, half_gain, head_parts,
    outcome,
    mats, aggregates, states, next_states,
):
    first = lax.axis_index("section") == 0
    even = lax.rem(lax.axis_index("shard"), 2) == 0
    rows, width = state_own.shape
    size = near.shape[0]
    kept = crossed.shape[0]
    total = rows + 2 * size
    inside = pl.ds(size, rows)
    low, high = pl.ds(0, size), pl.ds(size + rows, size)

    for place, (one, two) in enumerate(((crossed, relayed), (relayed, crossed))):
        span = pl.ds(place * kept, kept)
        own = own_weight[span, :]
        got = jnp.where(even, one[...], two[...])
        mats[0, span, :] = jnp.where(first, own, got)
        mats[1, span, :] = jnp.where(first, got, own)
    got = 0.5 * other_gain[...].astype(F32)
    gain = (jnp.where(first, half_gain[...], got), jnp.where(first, got, half_gain[...]))

    def sides(columns):
        one, two = near[:, columns], far[:, columns]
        return jnp.where(even, two, one), jnp.where(even, one, two)

    low_partial, high_partial = sides(pl.ds(0, width))
    low_state, high_state = sides(pl.ds(width, width))
    low_tile, high_tile = sides(pl.ds(2 * width, size))
    states[low, :] = low_state
    states[high, :] = high_state
    states[inside, :] = state_own[...]
    aggregates[low, :] = (aggregate[low, :] + low_partial.astype(F32)).astype(BF16)
    aggregates[high, :] = (aggregate[high, :] + high_partial.astype(F32)).astype(BF16)
    if rows > 2 * size:
        between = pl.ds(2 * size, rows - 2 * size)
        aggregates[between, :] = aggregate[between, :].astype(BF16)
    edge = pl.ds(size, size)
    aggregates[edge, :] = (aggregate[edge, :] + dot(low_tile, low_state)).astype(BF16)
    edge = pl.ds(rows, size)
    aggregates[edge, :] = (aggregate[edge, :] + dot(high_tile, high_state)).astype(BF16)

    for start in range(0, total, size):
        span = pl.ds(start, size)
        next_states[span, :] = layer(aggregates[span, :], mats[0], gain[0], states[span, :])

    inner = dot(adjacency[inside, :], next_states[inside, :])
    inner = jnp.concatenate(
        [
            inner[:size] + dot(low_tile, next_states[low, :]),
            *([inner[size : rows - size]] if rows > 2 * size else []),
            inner[rows - size :] + dot(high_tile, next_states[high, :]),
        ],
        axis=0,
    ).astype(BF16)
    state = jnp.concatenate(
        [
            layer(inner[start : start + size], mats[1], gain[1], next_states[pl.ds(size + start, size), :])
            for start in range(0, rows, size)
        ],
        axis=0,
    )
    scores = dot(head_parts[...], state, ((1,), (1,)))
    outcome[...] = scores[0:1] + scores[1:2] + scores[2:3]


def paired(features, labels, label_table, tiles, tile_rows, tile_cols, tile_live, weights, gains, head_weight):
    shard_count = lax.axis_size("shard")
    groups, rows, width = features.shape
    _, slots, size, _ = tiles.shape
    depth = weights.shape[1]
    kept = depth // 2
    classes = label_table.shape[0]
    message = jax.ShapeDtypeStruct((size, 2 * width + size), BF16)
    vmem = pl.BlockSpec(memory_space=pltpu.VMEM)
    hbm = pl.BlockSpec(memory_space=pltpu.HBM)
    table_rows = -(-3 * classes // PAD) * PAD

    far, near, crossing, gain, state, adjacency = pl.pallas_call(
        first_kernel,
        out_shape=(
            message,
            message,
            jax.ShapeDtypeStruct((kept, width), BF16),
            jax.ShapeDtypeStruct((1, width), BF16),
            jax.ShapeDtypeStruct((rows, width), BF16),
            jax.ShapeDtypeStruct((rows + 2 * size, rows), BF16),
        ),
        in_specs=[hbm] * 9,
        out_specs=(vmem,) * 6,
        scratch_shapes=[
            pltpu.SMEM((groups, slots), jnp.int32),
            pltpu.SMEM((groups, slots), jnp.int32),
            pltpu.SMEM((1, groups), jnp.int32),
            pltpu.VMEM((groups, rows), jnp.int32),
            pltpu.VMEM((classes, width), F32),
            pltpu.VMEM((slots, size, size), BF16),
            pltpu.VMEM((rows, width), BF16),
            pltpu.VMEM((table_rows, width), F32),
            pltpu.VMEM((rows + 2 * size, rows), F32),
            pltpu.SemaphoreType.DMA((9,)),
        ],
        compiler_params=pltpu.CompilerParams(vmem_limit_bytes=16 * 2**20),
        name="messages",
    )(*in_hbm(tile_rows, tile_cols, tile_live.T, labels, label_table, tiles, features, weights, gains))

    aggregate, own_weight, half_gain, head_parts = pl.pallas_call(
        waiting_kernel,
        out_shape=(
            jax.ShapeDtypeStruct((rows + 2 * size, width), F32),
            jax.ShapeDtypeStruct((depth, width), BF16),
            jax.ShapeDtypeStruct((1, width), F32),
            jax.ShapeDtypeStruct((PAD, width), BF16),
        ),
        in_specs=[vmem] * 2 + [hbm] * 3,
        out_specs=(vmem,) * 4,
        scratch_shapes=[
            pltpu.VMEM((1, width), F32),
            pltpu.VMEM((1, width), BF16),
            pltpu.VMEM((PAD, width), F32),
            pltpu.SemaphoreType.DMA((3,)),
        ],
        compiler_params=pltpu.CompilerParams(vmem_limit_bytes=16 * 2**20),
        name="waiting",
    )(adjacency, state, *in_hbm(head_weight.reshape(1, width), gains, weights))

    beside = [(i, i ^ 1) for i in range(shard_count)]
    apart = [(i, (i + 1) % shard_count) for i in range(1, shard_count, 2)]
    apart += [(b, a) for a, b in apart]
    across = [(0, 1), (1, 0)]
    crossed = lax.ppermute(crossing, "section", across)
    far = lax.ppermute(far, "shard", apart)
    near = lax.ppermute(near, "shard", beside)
    other_gain = lax.ppermute(gain, "section", across)
    crossed, aggregate, other_gain = lax.optimization_barrier((crossed, aggregate, other_gain))
    relayed = lax.ppermute(crossed, "shard", beside)

    return pl.pallas_call(
        second_kernel,
        out_shape=jax.ShapeDtypeStruct((1, rows), F32),
        in_specs=[vmem] * 11,
        out_specs=vmem,
        scratch_shapes=[
            pltpu.VMEM((2, depth, width), BF16),
            pltpu.VMEM((rows + 2 * size, width), BF16),
            pltpu.VMEM((rows + 2 * size, width), BF16),
            pltpu.VMEM((rows + 2 * size, width), BF16),
        ],
        compiler_params=pltpu.CompilerParams(vmem_limit_bytes=32 * 2**20),
        name="layers",
    )(adjacency, state, far, near, other_gain, crossed, relayed, aggregate, own_weight, half_gain, head_parts)


def extended_2(block, sides, width):
    for axis, dim in sides:
        count = lax.axis_size(axis)
        forward = [(i, i + 1) for i in range(count - 1)]
        backward = [(target, source) for source, target in forward]
        low = lax.ppermute(
            lax.slice_in_dim(block, block.shape[dim] - width, None, axis=dim), axis, forward
        )
        high = lax.ppermute(lax.slice_in_dim(block, 0, width, axis=dim), axis, backward)
        block = jnp.concatenate([low, block, high], axis=dim)
    return block


def body(
    features,
    labels,
    label_table,
    tiles,
    tile_rows,
    tile_cols,
    tile_live,
    weights,
    gains,
    head_weight,
):
    section_count = lax.axis_size("section")
    section_index = lax.axis_index("section")
    shard_index = lax.axis_index("shard")
    batch_count = features.shape[0]
    row_count = features.shape[1]
    feature_width = features.shape[2]
    tile_size = tiles.shape[2]
    slot_count = tiles.shape[1]
    label_count = label_table.shape[0]
    per_rows = row_count // tile_size
    per_section = batch_count // section_count
    slot_ids = jnp.arange(slot_count, dtype=jnp.int32)
    place_ids = jnp.arange(per_rows + 2, dtype=jnp.int32)

    def apply_layer(state, parts, layer_weight, layer_gain):
        group_tiles, col_local, placing, from_below, from_above = parts
        block_view = state.reshape(per_rows, tile_size, feature_width)
        chosen_blocks = jnp.take(block_view, col_local, axis=0)
        products = jnp.einsum(
            "kab,kbd->kad", group_tiles, chosen_blocks, preferred_element_type=jnp.float32
        )
        partial_value = jnp.einsum(
            "kp,kad->pad", placing, products, precision=lax.Precision.HIGHEST
        )
        edge_states = jnp.concatenate([state[:tile_size], state[row_count - tile_size :]], axis=0)
        extended = extended_2(edge_states, (("shard", 0),), tile_size)
        below_block = extended[:tile_size].astype(jnp.float32)
        above_block = extended[extended.shape[0] - tile_size :].astype(jnp.float32)
        own_rows = partial_value.reshape(row_count, feature_width)
        own_rows = own_rows.at[:tile_size].add(
            jnp.dot(from_below, below_block, precision=lax.Precision.HIGHEST)
        )
        own_rows = own_rows.at[row_count - tile_size :].add(
            jnp.dot(from_above, above_block, precision=lax.Precision.HIGHEST)
        )
        aggregate = own_rows.astype(jnp.bfloat16)
        projected = jnp.dot(aggregate, layer_weight, preferred_element_type=jnp.float32)
        scale = lax.rsqrt(jnp.mean(projected * projected, axis=-1, keepdims=True) + 1e-06)
        normed = projected * scale * layer_gain.astype(jnp.float32)
        return (state.astype(jnp.float32) + jax.nn.gelu(normed)).astype(jnp.bfloat16)

    layer_mats, layer_gains = (
        lax.all_gather(weights, "section", axis=0, tiled=True),
        lax.all_gather(gains, "section", axis=0, tiled=True),
    )
    batch_index = section_index * per_section + 0
    group_tiles = lax.dynamic_index_in_dim(tiles, batch_index, 0, keepdims=False)
    group_rows = lax.dynamic_index_in_dim(tile_rows, batch_index, 0, keepdims=False)
    group_cols = lax.dynamic_index_in_dim(tile_cols, batch_index, 0, keepdims=False)
    group_live = lax.dynamic_index_in_dim(tile_live, batch_index, 0, keepdims=False)
    col_local = group_cols - shard_index * per_rows
    slot_local = group_rows - (shard_index * per_rows - 1)
    live_mask = (slot_ids < group_live[0]).astype(jnp.float32)
    placing = (slot_local[:, None] == place_ids[None, :]).astype(jnp.float32) * live_mask[:, None]
    edge_pick = jnp.stack([placing[:, 0], placing[:, per_rows + 1]], axis=1)
    edge_tiles = jnp.einsum(
        "kp,kab->pab", edge_pick, group_tiles.astype(jnp.float32), precision=lax.Precision.HIGHEST
    )
    received = extended_2(edge_tiles, (("shard", 0),), 1)
    parts = (group_tiles, col_local, placing[:, 1 : per_rows + 1], received[0], received[3])

    def through(layer_index, state):
        return apply_layer(state, parts, layer_mats[layer_index], layer_gains[layer_index])

    group_labels = lax.dynamic_index_in_dim(labels, batch_index, 0, keepdims=False)
    group_features = lax.dynamic_index_in_dim(features, batch_index, 0, keepdims=False)
    labels_hot = (
        group_labels[:, None] == jnp.arange(label_count, dtype=jnp.int32)[None, :]
    ).astype(jnp.float32)
    embedded = jnp.dot(labels_hot, label_table, precision=lax.Precision.HIGHEST)
    state = lax.fori_loop(
        0,
        section_count,
        through,
        (group_features.astype(jnp.float32) + embedded).astype(jnp.bfloat16),
    )
    results = [jnp.dot(state.astype(jnp.float32), head_weight, precision=lax.Precision.HIGHEST)]
    return jnp.stack(results)


def solution(mesh):
    return jax.shard_map(
        paired if mesh.shape["section"] == 2 else body,
        mesh=mesh,
        in_specs=(
            P(None, "shard", None),
            P(None, "shard"),
            P(),
            P(None, "shard", None, None),
            P(None, "shard"),
            P(None, "shard"),
            P(None, "shard"),
            P("section", None, None),
            P("section", None),
            P(),
        ),
        out_specs=P("section", "shard"),
        check_vma=False,
    )
```

```python
import jax
import jax.numpy as jnp
from jax import lax
from jax.experimental import pallas as pl
from jax.experimental.pallas import tpu as pltpu
from jax.sharding import PartitionSpec as P

BF16 = jnp.bfloat16
F32 = jnp.float32
PAD = 16
GELU_LINEAR = 2.0 * (2.0 / 3.141592653589793) ** 0.5
GELU_CUBIC = 4.0 * GELU_LINEAR * 0.044715


def split3(value):
    high = value.astype(BF16).astype(F32)
    rest = value - high
    mid = rest.astype(BF16).astype(F32)
    return high, mid, rest - mid


def dot(a, b, dims=((1,), (0,))):
    return lax.dot_general(a, b, (dims, ((), ())), preferred_element_type=F32)


def in_hbm(*arrays):
    return [pltpu.with_memory_space_constraint(array, pltpu.HBM) for array in arrays]


def layer(aggregate, weight, half_gain, state):
    projected = dot(aggregate, weight)
    scale = lax.rsqrt(jnp.mean(projected * projected, axis=-1, keepdims=True) + 1e-06)
    half = (projected * scale * half_gain).astype(BF16)
    inner = half * (BF16(GELU_LINEAR) + BF16(GELU_CUBIC) * (half * half))
    return state + (half + half * jnp.tanh(inner))


def placed(block, blocks, shard, size):
    mirrored = 1 - lax.rem(shard, 2)
    return pl.ds(pl.multiple_of((block + mirrored * (blocks - 1 - 2 * block)) * size, size), size)


def first_kernel(
    tile_rows, tile_cols, tile_live, labels, label_table, tiles, features, weights,
    far, near, crossing, state_out, adjacency_out,
    rows_buf, cols_buf, live_buf, labels_buf, classes_buf, tiles_buf, features_buf, table_buf, sums, sems,
):
    section = lax.axis_index("section")
    shard = lax.axis_index("shard")
    rows, width = features_buf.shape
    slots, size, _ = tiles_buf.shape
    blocks = rows // size
    kept = crossing.shape[0]
    group = section

    small = [(tile_rows, rows_buf), (tile_cols, cols_buf), (tile_live, live_buf)]
    named = [(label_table, classes_buf)]
    spread = []
    for block in range(blocks):
        span, place = pl.ds(block * size, size), placed(block, blocks, shard, size)
        named.append((labels.at[:, span], labels_buf.at[:, place]))
        spread.append((features.at[group, span], features_buf.at[place]))
    half = pl.ds(pl.multiple_of(lax.rem(shard, 2) * kept, kept), kept)
    sent = [(weights.at[0, half], crossing)]
    batches, count = [], 0
    for batch in (small, named, [(tiles.at[group], tiles_buf)], spread, sent):
        batches.append([
            pltpu.make_async_copy(source, target, sems.at[count + index])
            for index, (source, target) in enumerate(batch)
        ])
        count += len(batch)
    for batch in batches:
        for copy in batch:
            copy.start()
    sums[...] = jnp.zeros_like(sums)
    table_buf[...] = jnp.zeros_like(table_buf)

    for copy in batches[1]:
        copy.wait()
    classes = classes_buf.shape[0]
    for part, value in enumerate(split3(classes_buf[...])):
        table_buf[pl.ds(part * classes, classes), :] = value
    depth = table_buf.shape[0]
    index = lax.broadcasted_iota(jnp.int32, (depth, rows), 0)
    wanted = jnp.where(
        index < classes, index,
        jnp.where(index < 2 * classes, index - classes, jnp.where(index < 3 * classes, index - 2 * classes, -1)),
    )
    hot = (wanted == labels_buf[pl.ds(group, 1), :]).astype(F32).astype(BF16)
    embedded = dot(hot, table_buf[...].astype(BF16), ((0,), (0,)))

    for copy in batches[0] + batches[2]:
        copy.wait()
    for slot in range(slots):
        @pl.when(slot < live_buf[0, group])
        def _():
            row = rows_buf[group, slot] - (shard * blocks - 1)
            col = cols_buf[group, slot] - shard * blocks
            sums[placed(row, blocks + 2, shard, size), placed(col, blocks, shard, size)] += tiles_buf[slot].astype(F32)
    adjacency = sums[...].astype(BF16)
    adjacency_out[...] = adjacency

    for copy in batches[3]:
        copy.wait()
    state = (features_buf[...].astype(F32) + embedded).astype(BF16)
    state_out[...] = state
    partial = dot(adjacency[size : size + rows], state).astype(BF16)
    near[:, pl.ds(0, width)] = partial[:size]
    near[:, pl.ds(width, width)] = state[:size]
    near[:, pl.ds(2 * width, size)] = adjacency[:size, :size]
    far[:, pl.ds(0, width)] = partial[rows - size :]
    far[:, pl.ds(width, width)] = state[rows - size :]
    far[:, pl.ds(2 * width, size)] = adjacency[rows + size :, rows - size :]
    for copy in batches[4]:
        copy.wait()


def waiting_kernel(
    adjacency, state, head, gains, weights,
    aggregate, weight, gain, half_gain, head_parts,
    head_buf, parts_buf, sems,
):
    copies = [
        pltpu.make_async_copy(source, target, sems.at[index])
        for index, (source, target) in enumerate(((weights.at[0], weight), (head, head_buf), (gains, gain)))
    ]
    for copy in copies:
        copy.start()
    aggregate[...] = dot(adjacency[...], state[...])
    parts_buf[...] = jnp.zeros_like(parts_buf)
    for copy in copies[1:]:
        copy.wait()
    for part, value in enumerate(split3(head_buf[...])):
        parts_buf[pl.ds(part, 1), :] = value
    head_parts[...] = parts_buf[...].astype(BF16)
    half_gain[...] = 0.5 * gain[...].astype(F32)
    copies[0].wait()


def near_kernel(state, near, aggregate, weight, half_gain, near_blocks):
    size, width = near.shape[0], state.shape[1]
    near_state = near[:, pl.ds(width, width)]
    first_sum = aggregate[pl.ds(0, size), :] + near[:, pl.ds(0, width)].astype(F32)
    next_sum = aggregate[pl.ds(size, size), :] + dot(near[:, pl.ds(2 * width, size)], near_state)
    near_blocks[pl.ds(0, size), :] = first_sum.astype(BF16)
    near_blocks[pl.ds(size, size), :] = next_sum.astype(BF16)

    @pl.when(lax.axis_index("section") == 0)
    def _():
        for place, block in enumerate((near_state, state[pl.ds(0, size), :])):
            span = pl.ds(place * size, size)
            near_blocks[span, :] = layer(near_blocks[span, :], weight[...], half_gain[...], block)


def second_kernel(
    adjacency, state, far, near, other_gain, crossed, relayed, near_blocks, aggregate, own_weight, half_gain, head_parts,
    outcome,
    mats, aggregates, states, next_states,
):
    first = lax.axis_index("section") == 0
    shard = lax.axis_index("shard")
    even = lax.rem(shard, 2) == 0
    rows, width = state.shape
    size = near.shape[0]
    kept = crossed.shape[0]
    total = rows + 2 * size
    inside, last = pl.ds(size, rows), pl.ds(size + rows, size)

    for place, (one, two) in enumerate(((crossed, relayed), (relayed, crossed))):
        span = pl.ds(place * kept, kept)
        own = own_weight[span, :]
        got = jnp.where(even, one[...], two[...])
        mats[0, span, :] = jnp.where(first, own, got)
        mats[1, span, :] = jnp.where(first, got, own)
    got = 0.5 * other_gain[...].astype(F32)
    gain = (jnp.where(first, half_gain[...], got), jnp.where(first, got, half_gain[...]))

    near_tile, far_tile = near[:, pl.ds(2 * width, size)], far[:, pl.ds(2 * width, size)]
    far_state = far[:, pl.ds(width, width)]
    states[inside, :] = state[...]
    states[last, :] = far_state
    for start in range(2 * size, rows, size):
        aggregates[pl.ds(start, size), :] = aggregate[pl.ds(start, size), :].astype(BF16)
    edge = pl.ds(rows, size)
    aggregates[edge, :] = (aggregate[edge, :] + dot(far_tile, far_state)).astype(BF16)
    aggregates[last, :] = (
        aggregate[last, :] + far[:, pl.ds(0, width)].astype(F32)
    ).astype(BF16)

    def step(start, source):
        span = pl.ds(start, size)
        next_states[span, :] = layer(source[span, :], mats[0], gain[0], states[span, :])

    @pl.when(first)
    def _():
        next_states[pl.ds(0, 2 * size), :] = near_blocks[...]

    @pl.when(jnp.logical_not(first))
    def _():
        states[pl.ds(0, size), :] = near[:, pl.ds(width, width)]
        step(0, near_blocks)
        step(size, near_blocks)

    for start in range(2 * size, total, size):
        step(start, aggregates)

    inner = dot(adjacency[inside, :], next_states[inside, :])
    inner = jnp.concatenate(
        [
            inner[:size] + dot(near_tile, next_states[pl.ds(0, size), :]),
            *([inner[size : rows - size]] if rows > 2 * size else []),
            inner[rows - size :] + dot(far_tile, next_states[last, :]),
        ],
        axis=0,
    ).astype(BF16)
    state = jnp.concatenate(
        [
            layer(inner[start : start + size], mats[1], gain[1], next_states[pl.ds(size + start, size), :])
            for start in range(0, rows, size)
        ],
        axis=0,
    )
    scores = dot(head_parts[...], state, ((1,), (1,)))
    scores = scores[0:1] + scores[1:2] + scores[2:3]
    for block in range(rows // size):
        outcome[:, placed(block, rows // size, shard, size)] = scores[:, block * size : (block + 1) * size]


def paired(features, labels, label_table, tiles, tile_rows, tile_cols, tile_live, weights, gains, head_weight):
    shard_count = lax.axis_size("shard")
    groups, rows, width = features.shape
    _, slots, size, _ = tiles.shape
    depth = weights.shape[1]
    kept = depth // 2
    classes = label_table.shape[0]
    message = jax.ShapeDtypeStruct((size, 2 * width + size), BF16)
    vmem = pl.BlockSpec(memory_space=pltpu.VMEM)
    hbm = pl.BlockSpec(memory_space=pltpu.HBM)
    table_rows = -(-3 * classes // PAD) * PAD

    far, near, crossing, state, adjacency = pl.pallas_call(
        first_kernel,
        out_shape=(
            message,
            message,
            jax.ShapeDtypeStruct((kept, width), BF16),
            jax.ShapeDtypeStruct((rows, width), BF16),
            jax.ShapeDtypeStruct((rows + 2 * size, rows), BF16),
        ),
        in_specs=[hbm] * 8,
        out_specs=(vmem,) * 5,
        scratch_shapes=[
            pltpu.SMEM((groups, slots), jnp.int32),
            pltpu.SMEM((groups, slots), jnp.int32),
            pltpu.SMEM((1, groups), jnp.int32),
            pltpu.VMEM((groups, rows), jnp.int32),
            pltpu.VMEM((classes, width), F32),
            pltpu.VMEM((slots, size, size), BF16),
            pltpu.VMEM((rows, width), BF16),
            pltpu.VMEM((table_rows, width), F32),
            pltpu.VMEM((rows + 2 * size, rows), F32),
            pltpu.SemaphoreType.DMA((6 + 2 * (rows // size),)),
        ],
        compiler_params=pltpu.CompilerParams(vmem_limit_bytes=16 * 2**20),
        name="messages",
    )(*in_hbm(tile_rows, tile_cols, tile_live.T, labels, label_table, tiles, features, weights))

    beside = [(i, i ^ 1) for i in range(shard_count)]
    apart = [(i, (i + 1) % shard_count) for i in range(1, shard_count, 2)]
    apart += [(b, a) for a, b in apart]
    across = [(0, 1), (1, 0)]
    crossed = lax.ppermute(crossing, "section", across)
    far = lax.ppermute(far, "shard", apart)
    near = lax.ppermute(near, "shard", beside)

    aggregate, own_weight, gain, half_gain, head_parts = pl.pallas_call(
        waiting_kernel,
        out_shape=(
            jax.ShapeDtypeStruct((rows + 2 * size, width), F32),
            jax.ShapeDtypeStruct((depth, width), BF16),
            jax.ShapeDtypeStruct((1, width), BF16),
            jax.ShapeDtypeStruct((1, width), F32),
            jax.ShapeDtypeStruct((PAD, width), BF16),
        ),
        in_specs=[vmem] * 2 + [hbm] * 3,
        out_specs=(vmem,) * 5,
        scratch_shapes=[
            pltpu.VMEM((1, width), F32),
            pltpu.VMEM((PAD, width), F32),
            pltpu.SemaphoreType.DMA((3,)),
        ],
        compiler_params=pltpu.CompilerParams(vmem_limit_bytes=16 * 2**20),
        cost_estimate=pl.CostEstimate(flops=4 * 10**9, bytes_accessed=2**20, transcendentals=0),
        name="waiting",
    )(adjacency, state, *in_hbm(head_weight.reshape(1, width), gains, weights))

    other_gain = lax.ppermute(gain, "section", across)
    near_blocks = pl.pallas_call(
        near_kernel,
        out_shape=jax.ShapeDtypeStruct((2 * size, width), BF16),
        in_specs=[vmem] * 5,
        out_specs=vmem,
        compiler_params=pltpu.CompilerParams(vmem_limit_bytes=16 * 2**20),
        name="beside",
    )(state, near, aggregate, own_weight, half_gain)

    crossed, near_blocks, other_gain = lax.optimization_barrier((crossed, near_blocks, other_gain))
    relayed = lax.ppermute(crossed, "shard", beside)

    return pl.pallas_call(
        second_kernel,
        out_shape=jax.ShapeDtypeStruct((1, rows), F32),
        in_specs=[vmem] * 12,
        out_specs=vmem,
        scratch_shapes=[
            pltpu.VMEM((2, depth, width), BF16),
            pltpu.VMEM((rows + 2 * size, width), BF16),
            pltpu.VMEM((rows + 2 * size, width), BF16),
            pltpu.VMEM((rows + 2 * size, width), BF16),
        ],
        compiler_params=pltpu.CompilerParams(vmem_limit_bytes=32 * 2**20),
        name="layers",
    )(
        adjacency, state, far, near, other_gain, crossed, relayed,
        near_blocks, aggregate, own_weight, half_gain, head_parts,
    )


def extended_2(block, sides, width):
    for axis, dim in sides:
        count = lax.axis_size(axis)
        forward = [(i, i + 1) for i in range(count - 1)]
        backward = [(target, source) for source, target in forward]
        low = lax.ppermute(
            lax.slice_in_dim(block, block.shape[dim] - width, None, axis=dim), axis, forward
        )
        high = lax.ppermute(lax.slice_in_dim(block, 0, width, axis=dim), axis, backward)
        block = jnp.concatenate([low, block, high], axis=dim)
    return block


def body(
    features,
    labels,
    label_table,
    tiles,
    tile_rows,
    tile_cols,
    tile_live,
    weights,
    gains,
    head_weight,
):
    section_count = lax.axis_size("section")
    section_index = lax.axis_index("section")
    shard_index = lax.axis_index("shard")
    batch_count = features.shape[0]
    row_count = features.shape[1]
    feature_width = features.shape[2]
    tile_size = tiles.shape[2]
    slot_count = tiles.shape[1]
    label_count = label_table.shape[0]
    per_rows = row_count // tile_size
    per_section = batch_count // section_count
    slot_ids = jnp.arange(slot_count, dtype=jnp.int32)
    place_ids = jnp.arange(per_rows + 2, dtype=jnp.int32)

    def apply_layer(state, parts, layer_weight, layer_gain):
        group_tiles, col_local, placing, from_below, from_above = parts
        block_view = state.reshape(per_rows, tile_size, feature_width)
        chosen_blocks = jnp.take(block_view, col_local, axis=0)
        products = jnp.einsum(
            "kab,kbd->kad", group_tiles, chosen_blocks, preferred_element_type=jnp.float32
        )
        partial_value = jnp.einsum(
            "kp,kad->pad", placing, products, precision=lax.Precision.HIGHEST
        )
        edge_states = jnp.concatenate([state[:tile_size], state[row_count - tile_size :]], axis=0)
        extended = extended_2(edge_states, (("shard", 0),), tile_size)
        below_block = extended[:tile_size].astype(jnp.float32)
        above_block = extended[extended.shape[0] - tile_size :].astype(jnp.float32)
        own_rows = partial_value.reshape(row_count, feature_width)
        own_rows = own_rows.at[:tile_size].add(
            jnp.dot(from_below, below_block, precision=lax.Precision.HIGHEST)
        )
        own_rows = own_rows.at[row_count - tile_size :].add(
            jnp.dot(from_above, above_block, precision=lax.Precision.HIGHEST)
        )
        aggregate = own_rows.astype(jnp.bfloat16)
        projected = jnp.dot(aggregate, layer_weight, preferred_element_type=jnp.float32)
        scale = lax.rsqrt(jnp.mean(projected * projected, axis=-1, keepdims=True) + 1e-06)
        normed = projected * scale * layer_gain.astype(jnp.float32)
        return (state.astype(jnp.float32) + jax.nn.gelu(normed)).astype(jnp.bfloat16)

    layer_mats, layer_gains = (
        lax.all_gather(weights, "section", axis=0, tiled=True),
        lax.all_gather(gains, "section", axis=0, tiled=True),
    )
    batch_index = section_index * per_section + 0
    group_tiles = lax.dynamic_index_in_dim(tiles, batch_index, 0, keepdims=False)
    group_rows = lax.dynamic_index_in_dim(tile_rows, batch_index, 0, keepdims=False)
    group_cols = lax.dynamic_index_in_dim(tile_cols, batch_index, 0, keepdims=False)
    group_live = lax.dynamic_index_in_dim(tile_live, batch_index, 0, keepdims=False)
    col_local = group_cols - shard_index * per_rows
    slot_local = group_rows - (shard_index * per_rows - 1)
    live_mask = (slot_ids < group_live[0]).astype(jnp.float32)
    placing = (slot_local[:, None] == place_ids[None, :]).astype(jnp.float32) * live_mask[:, None]
    edge_pick = jnp.stack([placing[:, 0], placing[:, per_rows + 1]], axis=1)
    edge_tiles = jnp.einsum(
        "kp,kab->pab", edge_pick, group_tiles.astype(jnp.float32), precision=lax.Precision.HIGHEST
    )
    received = extended_2(edge_tiles, (("shard", 0),), 1)
    parts = (group_tiles, col_local, placing[:, 1 : per_rows + 1], received[0], received[3])

    def through(layer_index, state):
        return apply_layer(state, parts, layer_mats[layer_index], layer_gains[layer_index])

    group_labels = lax.dynamic_index_in_dim(labels, batch_index, 0, keepdims=False)
    group_features = lax.dynamic_index_in_dim(features, batch_index, 0, keepdims=False)
    labels_hot = (
        group_labels[:, None] == jnp.arange(label_count, dtype=jnp.int32)[None, :]
    ).astype(jnp.float32)
    embedded = jnp.dot(labels_hot, label_table, precision=lax.Precision.HIGHEST)
    state = lax.fori_loop(
        0,
        section_count,
        through,
        (group_features.astype(jnp.float32) + embedded).astype(jnp.bfloat16),
    )
    results = [jnp.dot(state.astype(jnp.float32), head_weight, precision=lax.Precision.HIGHEST)]
    return jnp.stack(results)


def solution(mesh):
    return jax.shard_map(
        paired if mesh.shape["section"] == 2 else body,
        mesh=mesh,
        in_specs=(
            P(None, "shard", None),
            P(None, "shard"),
            P(),
            P(None, "shard", None, None),
            P(None, "shard"),
            P(None, "shard"),
            P(None, "shard"),
            P("section", None, None),
            P("section", None),
            P(),
        ),
        out_specs=P("section", "shard"),
        check_vma=False,
    )
```

```python
import jax
import jax.numpy as jnp
from jax import lax
from jax.experimental import pallas as pl
from jax.experimental.pallas import tpu as pltpu
from jax.sharding import PartitionSpec as P

BF16 = jnp.bfloat16
F32 = jnp.float32
PAD = 16
EXTRA = 8
GELU_LINEAR = 2.0 * (2.0 / 3.141592653589793) ** 0.5
GELU_CUBIC = 4.0 * GELU_LINEAR * 0.044715


def split3(value):
    high = value.astype(BF16).astype(F32)
    rest = value - high
    mid = rest.astype(BF16).astype(F32)
    return high, mid, rest - mid


def dot(a, b, dims=((1,), (0,))):
    return lax.dot_general(a, b, (dims, ((), ())), preferred_element_type=F32)


def in_hbm(*arrays):
    return [pltpu.with_memory_space_constraint(array, pltpu.HBM) for array in arrays]


def layer(aggregate, weight, half_gain, state):
    projected = dot(aggregate, weight)
    scale = lax.rsqrt(jnp.mean(projected * projected, axis=-1, keepdims=True) + 1e-06)
    half = (projected * scale * half_gain).astype(BF16)
    inner = half * (BF16(GELU_LINEAR) + BF16(GELU_CUBIC) * (half * half))
    return state + (half + half * jnp.tanh(inner))


def placed(block, blocks, shard, size):
    mirrored = 1 - lax.rem(shard, 2)
    return pl.ds(pl.multiple_of((block + mirrored * (blocks - 1 - 2 * block)) * size, size), size)


def first_kernel(
    tile_rows, tile_cols, tile_live, labels, label_table, tiles, features, gains, weights,
    far, near, crossing, state_out, adjacency_out,
    rows_buf, cols_buf, live_buf, labels_buf, classes_buf, tiles_buf, features_buf, gains_buf, table_buf, sums, sems,
):
    section = lax.axis_index("section")
    shard = lax.axis_index("shard")
    rows, width = features_buf.shape
    slots, size, _ = tiles_buf.shape
    blocks = rows // size
    kept = crossing.shape[0] - EXTRA
    group = section

    small = [(tile_rows, rows_buf), (tile_cols, cols_buf), (tile_live, live_buf)]
    named = [(label_table, classes_buf)]
    spread = []
    for block in range(blocks):
        span, place = pl.ds(block * size, size), placed(block, blocks, shard, size)
        named.append((labels.at[:, span], labels_buf.at[:, place]))
        spread.append((features.at[group, span], features_buf.at[place]))
    half = pl.ds(pl.multiple_of(lax.rem(shard, 2) * kept, kept), kept)
    sent = [(gains, gains_buf), (weights.at[0, half], crossing.at[pl.ds(0, kept)])]
    batches, count = [], 0
    for batch in (small, named, [(tiles.at[group], tiles_buf)], spread, sent):
        batches.append([
            pltpu.make_async_copy(source, target, sems.at[count + index])
            for index, (source, target) in enumerate(batch)
        ])
        count += len(batch)
    for batch in batches:
        for copy in batch:
            copy.start()
    sums[...] = jnp.zeros_like(sums)
    table_buf[...] = jnp.zeros_like(table_buf)

    for copy in batches[1]:
        copy.wait()
    classes = classes_buf.shape[0]
    for part, value in enumerate(split3(classes_buf[...])):
        table_buf[pl.ds(part * classes, classes), :] = value
    depth = table_buf.shape[0]
    index = lax.broadcasted_iota(jnp.int32, (depth, rows), 0)
    wanted = jnp.where(
        index < classes, index,
        jnp.where(index < 2 * classes, index - classes, jnp.where(index < 3 * classes, index - 2 * classes, -1)),
    )
    hot = (wanted == labels_buf[pl.ds(group, 1), :]).astype(F32).astype(BF16)
    embedded = dot(hot, table_buf[...].astype(BF16), ((0,), (0,)))

    for copy in batches[0] + batches[2]:
        copy.wait()
    for slot in range(slots):
        @pl.when(slot < live_buf[0, group])
        def _():
            row = rows_buf[group, slot] - (shard * blocks - 1)
            col = cols_buf[group, slot] - shard * blocks
            sums[placed(row, blocks + 2, shard, size), placed(col, blocks, shard, size)] += tiles_buf[slot].astype(F32)
    adjacency = sums[...].astype(BF16)
    adjacency_out[...] = adjacency

    for copy in batches[3]:
        copy.wait()
    state = (features_buf[...].astype(F32) + embedded).astype(BF16)
    state_out[...] = state
    partial = dot(adjacency[size : size + rows], state).astype(BF16)
    near[:, pl.ds(0, width)] = partial[:size]
    near[:, pl.ds(width, width)] = state[:size]
    near[:, pl.ds(2 * width, size)] = adjacency[:size, :size]
    far[:, pl.ds(0, width)] = partial[rows - size :]
    far[:, pl.ds(width, width)] = state[rows - size :]
    far[:, pl.ds(2 * width, size)] = adjacency[rows + size :, rows - size :]
    batches[4][0].wait()
    crossing[pl.ds(kept, EXTRA), :] = jnp.broadcast_to(gains_buf[...].astype(F32), (EXTRA, width)).astype(BF16)
    batches[4][1].wait()


def waiting_kernel(
    adjacency, state, head, gains, weights,
    aggregate, weight, half_gain, head_parts,
    head_buf, gains_buf, parts_buf, sems,
):
    copies = [
        pltpu.make_async_copy(source, target, sems.at[index])
        for index, (source, target) in enumerate(((weights.at[0], weight), (head, head_buf), (gains, gains_buf)))
    ]
    for copy in copies:
        copy.start()
    aggregate[...] = dot(adjacency[...], state[...])
    parts_buf[...] = jnp.zeros_like(parts_buf)
    for copy in copies[1:]:
        copy.wait()
    for part, value in enumerate(split3(head_buf[...])):
        parts_buf[pl.ds(part, 1), :] = value
    head_parts[...] = parts_buf[...].astype(BF16)
    half_gain[...] = 0.5 * gains_buf[...].astype(F32)
    copies[0].wait()


def near_kernel(near, aggregate, near_aggregate):
    size, width = near.shape[0], aggregate.shape[1]
    first, second = pl.ds(0, size), pl.ds(size, size)
    near_aggregate[first, :] = (aggregate[first, :] + near[:, pl.ds(0, width)].astype(F32)).astype(BF16)
    near_aggregate[second, :] = (
        aggregate[second, :] + dot(near[:, pl.ds(2 * width, size)], near[:, pl.ds(width, width)])
    ).astype(BF16)


def second_kernel(
    adjacency, state, far, near, crossed, relayed, near_aggregate, aggregate, own_weight, half_gain, head_parts,
    outcome,
    mats, aggregates, next_states,
):
    first = lax.axis_index("section") == 0
    shard = lax.axis_index("shard")
    even = lax.rem(shard, 2) == 0
    rows, width = state.shape
    size = near.shape[0]
    kept = crossed.shape[0] - EXTRA
    total = rows + 2 * size
    inside, last = pl.ds(size, rows), pl.ds(size + rows, size)

    for place, (one, two) in enumerate(((crossed, relayed), (relayed, crossed))):
        span = pl.ds(place * kept, kept)
        own = own_weight[span, :]
        got = jnp.where(even, one[pl.ds(0, kept), :], two[pl.ds(0, kept), :])
        mats[0, span, :] = jnp.where(first, own, got)
        mats[1, span, :] = jnp.where(first, got, own)
    got = 0.5 * crossed[pl.ds(kept, EXTRA), :].astype(F32)[0:1]
    gain = (jnp.where(first, half_gain[...], got), jnp.where(first, got, half_gain[...]))

    near_tile, far_tile = near[:, pl.ds(2 * width, size)], far[:, pl.ds(2 * width, size)]
    edge = pl.ds(rows, size)
    for start in range(2 * size, rows, size):
        aggregates[pl.ds(start, size), :] = aggregate[pl.ds(start, size), :].astype(BF16)
    aggregates[edge, :] = (aggregate[edge, :] + dot(far_tile, far[:, pl.ds(width, width)])).astype(BF16)
    aggregates[last, :] = (aggregate[last, :] + far[:, pl.ds(0, width)].astype(F32)).astype(BF16)

    for start in range(0, total, size):
        span = pl.ds(start, size)
        source = near_aggregate if start < 2 * size else aggregates
        if start == 0:
            before = near[:, pl.ds(width, width)]
        elif start < total - size:
            before = state[pl.ds(start - size, size), :]
        else:
            before = far[:, pl.ds(width, width)]
        next_states[span, :] = layer(source[span, :], mats[0], gain[0], before)

    inner = dot(adjacency[inside, :], next_states[inside, :])
    inner = jnp.concatenate(
        [
            inner[:size] + dot(near_tile, next_states[pl.ds(0, size), :]),
            *([inner[size : rows - size]] if rows > 2 * size else []),
            inner[rows - size :] + dot(far_tile, next_states[last, :]),
        ],
        axis=0,
    ).astype(BF16)
    state = jnp.concatenate(
        [
            layer(inner[start : start + size], mats[1], gain[1], next_states[pl.ds(size + start, size), :])
            for start in range(0, rows, size)
        ],
        axis=0,
    )
    scores = dot(head_parts[...], state, ((1,), (1,)))
    scores = scores[0:1] + scores[1:2] + scores[2:3]
    for block in range(rows // size):
        outcome[:, placed(block, rows // size, shard, size)] = scores[:, block * size : (block + 1) * size]


def paired(features, labels, label_table, tiles, tile_rows, tile_cols, tile_live, weights, gains, head_weight):
    shard_count = lax.axis_size("shard")
    groups, rows, width = features.shape
    _, slots, size, _ = tiles.shape
    depth = weights.shape[1]
    kept = depth // 2
    classes = label_table.shape[0]
    message = jax.ShapeDtypeStruct((size, 2 * width + size), BF16)
    vmem = pl.BlockSpec(memory_space=pltpu.VMEM)
    hbm = pl.BlockSpec(memory_space=pltpu.HBM)
    table_rows = -(-3 * classes // PAD) * PAD

    far, near, crossing, state, adjacency = pl.pallas_call(
        first_kernel,
        out_shape=(
            message,
            message,
            jax.ShapeDtypeStruct((kept + EXTRA, width), BF16),
            jax.ShapeDtypeStruct((rows, width), BF16),
            jax.ShapeDtypeStruct((rows + 2 * size, rows), BF16),
        ),
        in_specs=[hbm] * 9,
        out_specs=(vmem,) * 5,
        scratch_shapes=[
            pltpu.SMEM((groups, slots), jnp.int32),
            pltpu.SMEM((groups, slots), jnp.int32),
            pltpu.SMEM((1, groups), jnp.int32),
            pltpu.VMEM((groups, rows), jnp.int32),
            pltpu.VMEM((classes, width), F32),
            pltpu.VMEM((slots, size, size), BF16),
            pltpu.VMEM((rows, width), BF16),
            pltpu.VMEM((1, width), BF16),
            pltpu.VMEM((table_rows, width), F32),
            pltpu.VMEM((rows + 2 * size, rows), F32),
            pltpu.SemaphoreType.DMA((7 + 2 * (rows // size),)),
        ],
        compiler_params=pltpu.CompilerParams(vmem_limit_bytes=16 * 2**20),
        name="messages",
    )(*in_hbm(tile_rows, tile_cols, tile_live.T, labels, label_table, tiles, features, gains, weights))

    beside = [(i, i ^ 1) for i in range(shard_count)]
    apart = [(i, (i + 1) % shard_count) for i in range(1, shard_count, 2)]
    apart += [(b, a) for a, b in apart]
    across = [(0, 1), (1, 0)]
    crossed = lax.ppermute(crossing, "section", across)
    far = lax.ppermute(far, "shard", apart)
    near = lax.ppermute(near, "shard", beside)

    aggregate, own_weight, half_gain, head_parts = pl.pallas_call(
        waiting_kernel,
        out_shape=(
            jax.ShapeDtypeStruct((rows + 2 * size, width), F32),
            jax.ShapeDtypeStruct((depth, width), BF16),
            jax.ShapeDtypeStruct((1, width), F32),
            jax.ShapeDtypeStruct((PAD, width), BF16),
        ),
        in_specs=[vmem] * 2 + [hbm] * 3,
        out_specs=(vmem,) * 4,
        scratch_shapes=[
            pltpu.VMEM((1, width), F32),
            pltpu.VMEM((1, width), BF16),
            pltpu.VMEM((PAD, width), F32),
            pltpu.SemaphoreType.DMA((3,)),
        ],
        compiler_params=pltpu.CompilerParams(vmem_limit_bytes=16 * 2**20),
        cost_estimate=pl.CostEstimate(flops=4 * 10**9, bytes_accessed=2**20, transcendentals=0),
        name="waiting",
    )(adjacency, state, *in_hbm(head_weight.reshape(1, width), gains, weights))

    near_aggregate = pl.pallas_call(
        near_kernel,
        out_shape=jax.ShapeDtypeStruct((2 * size, width), BF16),
        in_specs=[vmem] * 2,
        out_specs=vmem,
        compiler_params=pltpu.CompilerParams(vmem_limit_bytes=16 * 2**20),
        name="beside",
    )(near, aggregate)

    crossed, near_aggregate = lax.optimization_barrier((crossed, near_aggregate))
    relayed = lax.ppermute(crossed, "shard", beside)

    return pl.pallas_call(
        second_kernel,
        out_shape=jax.ShapeDtypeStruct((1, rows), F32),
        in_specs=[vmem] * 11,
        out_specs=vmem,
        scratch_shapes=[
            pltpu.VMEM((2, depth, width), BF16),
            pltpu.VMEM((rows + 2 * size, width), BF16),
            pltpu.VMEM((rows + 2 * size, width), BF16),
        ],
        compiler_params=pltpu.CompilerParams(vmem_limit_bytes=32 * 2**20),
        name="layers",
    )(
        adjacency, state, far, near, crossed, relayed, near_aggregate, aggregate, own_weight, half_gain, head_parts,
    )


def extended_2(block, sides, width):
    for axis, dim in sides:
        count = lax.axis_size(axis)
        forward = [(i, i + 1) for i in range(count - 1)]
        backward = [(target, source) for source, target in forward]
        low = lax.ppermute(
            lax.slice_in_dim(block, block.shape[dim] - width, None, axis=dim), axis, forward
        )
        high = lax.ppermute(lax.slice_in_dim(block, 0, width, axis=dim), axis, backward)
        block = jnp.concatenate([low, block, high], axis=dim)
    return block


def body(
    features,
    labels,
    label_table,
    tiles,
    tile_rows,
    tile_cols,
    tile_live,
    weights,
    gains,
    head_weight,
):
    section_count = lax.axis_size("section")
    section_index = lax.axis_index("section")
    shard_index = lax.axis_index("shard")
    batch_count = features.shape[0]
    row_count = features.shape[1]
    feature_width = features.shape[2]
    tile_size = tiles.shape[2]
    slot_count = tiles.shape[1]
    label_count = label_table.shape[0]
    per_rows = row_count // tile_size
    per_section = batch_count // section_count
    slot_ids = jnp.arange(slot_count, dtype=jnp.int32)
    place_ids = jnp.arange(per_rows + 2, dtype=jnp.int32)

    def apply_layer(state, parts, layer_weight, layer_gain):
        group_tiles, col_local, placing, from_below, from_above = parts
        block_view = state.reshape(per_rows, tile_size, feature_width)
        chosen_blocks = jnp.take(block_view, col_local, axis=0)
        products = jnp.einsum(
            "kab,kbd->kad", group_tiles, chosen_blocks, preferred_element_type=jnp.float32
        )
        partial_value = jnp.einsum(
            "kp,kad->pad", placing, products, precision=lax.Precision.HIGHEST
        )
        edge_states = jnp.concatenate([state[:tile_size], state[row_count - tile_size :]], axis=0)
        extended = extended_2(edge_states, (("shard", 0),), tile_size)
        below_block = extended[:tile_size].astype(jnp.float32)
        above_block = extended[extended.shape[0] - tile_size :].astype(jnp.float32)
        own_rows = partial_value.reshape(row_count, feature_width)
        own_rows = own_rows.at[:tile_size].add(
            jnp.dot(from_below, below_block, precision=lax.Precision.HIGHEST)
        )
        own_rows = own_rows.at[row_count - tile_size :].add(
            jnp.dot(from_above, above_block, precision=lax.Precision.HIGHEST)
        )
        aggregate = own_rows.astype(jnp.bfloat16)
        projected = jnp.dot(aggregate, layer_weight, preferred_element_type=jnp.float32)
        scale = lax.rsqrt(jnp.mean(projected * projected, axis=-1, keepdims=True) + 1e-06)
        normed = projected * scale * layer_gain.astype(jnp.float32)
        return (state.astype(jnp.float32) + jax.nn.gelu(normed)).astype(jnp.bfloat16)

    layer_mats, layer_gains = (
        lax.all_gather(weights, "section", axis=0, tiled=True),
        lax.all_gather(gains, "section", axis=0, tiled=True),
    )
    batch_index = section_index * per_section + 0
    group_tiles = lax.dynamic_index_in_dim(tiles, batch_index, 0, keepdims=False)
    group_rows = lax.dynamic_index_in_dim(tile_rows, batch_index, 0, keepdims=False)
    group_cols = lax.dynamic_index_in_dim(tile_cols, batch_index, 0, keepdims=False)
    group_live = lax.dynamic_index_in_dim(tile_live, batch_index, 0, keepdims=False)
    col_local = group_cols - shard_index * per_rows
    slot_local = group_rows - (shard_index * per_rows - 1)
    live_mask = (slot_ids < group_live[0]).astype(jnp.float32)
    placing = (slot_local[:, None] == place_ids[None, :]).astype(jnp.float32) * live_mask[:, None]
    edge_pick = jnp.stack([placing[:, 0], placing[:, per_rows + 1]], axis=1)
    edge_tiles = jnp.einsum(
        "kp,kab->pab", edge_pick, group_tiles.astype(jnp.float32), precision=lax.Precision.HIGHEST
    )
    received = extended_2(edge_tiles, (("shard", 0),), 1)
    parts = (group_tiles, col_local, placing[:, 1 : per_rows + 1], received[0], received[3])

    def through(layer_index, state):
        return apply_layer(state, parts, layer_mats[layer_index], layer_gains[layer_index])

    group_labels = lax.dynamic_index_in_dim(labels, batch_index, 0, keepdims=False)
    group_features = lax.dynamic_index_in_dim(features, batch_index, 0, keepdims=False)
    labels_hot = (
        group_labels[:, None] == jnp.arange(label_count, dtype=jnp.int32)[None, :]
    ).astype(jnp.float32)
    embedded = jnp.dot(labels_hot, label_table, precision=lax.Precision.HIGHEST)
    state = lax.fori_loop(
        0,
        section_count,
        through,
        (group_features.astype(jnp.float32) + embedded).astype(jnp.bfloat16),
    )
    results = [jnp.dot(state.astype(jnp.float32), head_weight, precision=lax.Precision.HIGHEST)]
    return jnp.stack(results)


def solution(mesh):
    return jax.shard_map(
        paired if mesh.shape["section"] == 2 else body,
        mesh=mesh,
        in_specs=(
            P(None, "shard", None),
            P(None, "shard"),
            P(),
            P(None, "shard", None, None),
            P(None, "shard"),
            P(None, "shard"),
            P(None, "shard"),
            P("section", None, None),
            P("section", None),
            P(),
        ),
        out_specs=P("section", "shard"),
        check_vma=False,
    )
```

```python
import jax
import jax.numpy as jnp
from jax import lax
from jax.experimental import pallas as pl
from jax.experimental.pallas import tpu as pltpu
from jax.sharding import PartitionSpec as P

BF16 = jnp.bfloat16
F32 = jnp.float32
PAD = 16
EXTRA = 8
GELU_LINEAR = 2.0 * (2.0 / 3.141592653589793) ** 0.5
GELU_CUBIC = 4.0 * GELU_LINEAR * 0.044715


def split3(value):
    high = value.astype(BF16).astype(F32)
    rest = value - high
    mid = rest.astype(BF16).astype(F32)
    return high, mid, rest - mid


def dot(a, b, dims=((1,), (0,))):
    return lax.dot_general(a, b, (dims, ((), ())), preferred_element_type=F32)


def in_hbm(*arrays):
    return [pltpu.with_memory_space_constraint(array, pltpu.HBM) for array in arrays]


def layer(aggregate, weight, half_gain, state):
    projected = dot(aggregate, weight)
    scale = lax.rsqrt(jnp.mean(projected * projected, axis=-1, keepdims=True) + 1e-06)
    half = (projected * scale * half_gain).astype(BF16)
    inner = half * (BF16(GELU_LINEAR) + BF16(GELU_CUBIC) * (half * half))
    return state + (half + half * jnp.tanh(inner))


def placed(block, blocks, shard, size):
    mirrored = 1 - lax.rem(shard, 2)
    return pl.ds(pl.multiple_of((block + mirrored * (blocks - 1 - 2 * block)) * size, size), size)


def first_kernel(
    tile_rows, tile_cols, tile_live, labels, label_table, tiles, features, gains, weights,
    far, near, crossing, state_out, adjacency_out,
    rows_buf, cols_buf, live_buf, labels_buf, classes_buf, tiles_buf, features_buf, gains_buf, table_buf, sums, sems,
):
    section = lax.axis_index("section")
    shard = lax.axis_index("shard")
    rows, width = features_buf.shape
    slots, size, _ = tiles_buf.shape
    blocks = rows // size
    kept = crossing.shape[0] - EXTRA
    group = section

    small = [(tile_rows, rows_buf), (tile_cols, cols_buf), (tile_live, live_buf)]
    named = [(label_table, classes_buf)]
    spread = []
    for block in range(blocks):
        span, place = pl.ds(block * size, size), placed(block, blocks, shard, size)
        named.append((labels.at[:, span], labels_buf.at[:, place]))
        spread.append((features.at[group, span], features_buf.at[place]))
    half = pl.ds(pl.multiple_of(lax.rem(shard, 2) * kept, kept), kept)
    sent = [(gains, gains_buf), (weights.at[0, half], crossing.at[pl.ds(0, kept)])]
    batches, count = [], 0
    for batch in (small, named, [(tiles.at[group], tiles_buf)], spread, sent):
        batches.append([
            pltpu.make_async_copy(source, target, sems.at[count + index])
            for index, (source, target) in enumerate(batch)
        ])
        count += len(batch)
    for batch in batches:
        for copy in batch:
            copy.start()
    sums[...] = jnp.zeros_like(sums)
    table_buf[...] = jnp.zeros_like(table_buf)

    for copy in batches[1]:
        copy.wait()
    classes = classes_buf.shape[0]
    for part, value in enumerate(split3(classes_buf[...])):
        table_buf[pl.ds(part * classes, classes), :] = value
    depth = table_buf.shape[0]
    index = lax.broadcasted_iota(jnp.int32, (depth, rows), 0)
    wanted = jnp.where(
        index < classes, index,
        jnp.where(index < 2 * classes, index - classes, jnp.where(index < 3 * classes, index - 2 * classes, -1)),
    )
    hot = (wanted == labels_buf[pl.ds(group, 1), :]).astype(F32).astype(BF16)
    embedded = dot(hot, table_buf[...].astype(BF16), ((0,), (0,)))

    for copy in batches[0] + batches[2]:
        copy.wait()
    for slot in range(slots):
        @pl.when(slot < live_buf[0, group])
        def _():
            row = rows_buf[group, slot] - (shard * blocks - 1)
            col = cols_buf[group, slot] - shard * blocks
            sums[placed(row, blocks + 2, shard, size), placed(col, blocks, shard, size)] += tiles_buf[slot].astype(F32)
    adjacency = sums[...].astype(BF16)
    adjacency_out[...] = adjacency

    for copy in batches[3]:
        copy.wait()
    state = (features_buf[...].astype(F32) + embedded).astype(BF16)
    state_out[...] = state
    partial = dot(adjacency[size : size + rows], state).astype(BF16)
    near[:, pl.ds(0, width)] = partial[:size]
    near[:, pl.ds(width, width)] = state[:size]
    near[:, pl.ds(2 * width, size)] = adjacency[:size, :size]
    far[:, pl.ds(0, width)] = partial[rows - size :]
    far[:, pl.ds(width, width)] = state[rows - size :]
    far[:, pl.ds(2 * width, size)] = adjacency[rows + size :, rows - size :]
    batches[4][0].wait()
    crossing[pl.ds(kept, EXTRA), :] = jnp.broadcast_to(gains_buf[...].astype(F32), (EXTRA, width)).astype(BF16)
    batches[4][1].wait()


def waiting_kernel(
    adjacency, state, head, gains, weights,
    aggregate, weight, half_gain, head_row,
    gains_buf, sems,
):
    copies = [
        pltpu.make_async_copy(source, target, sems.at[index])
        for index, (source, target) in enumerate(((weights.at[0], weight), (head, head_row), (gains, gains_buf)))
    ]
    for copy in copies:
        copy.start()
    aggregate[...] = dot(adjacency[...], state[...])
    copies[2].wait()
    half_gain[...] = 0.5 * gains_buf[...].astype(F32)
    copies[0].wait()
    copies[1].wait()


def near_kernel(near, aggregate, near_aggregate):
    size, width = near.shape[0], aggregate.shape[1]
    first, second = pl.ds(0, size), pl.ds(size, size)
    near_aggregate[first, :] = (aggregate[first, :] + near[:, pl.ds(0, width)].astype(F32)).astype(BF16)
    near_aggregate[second, :] = (
        aggregate[second, :] + dot(near[:, pl.ds(2 * width, size)], near[:, pl.ds(width, width)])
    ).astype(BF16)


def second_kernel(
    adjacency, state, far, near, crossed, relayed, near_aggregate, aggregate, own_weight, half_gain, head_row,
    outcome,
    mats, aggregates, next_states,
):
    first = lax.axis_index("section") == 0
    shard = lax.axis_index("shard")
    even = lax.rem(shard, 2) == 0
    rows, width = state.shape
    size = near.shape[0]
    kept = crossed.shape[0] - EXTRA
    total = rows + 2 * size
    inside, last = pl.ds(size, rows), pl.ds(size + rows, size)

    for place, (one, two) in enumerate(((crossed, relayed), (relayed, crossed))):
        span = pl.ds(place * kept, kept)
        own = own_weight[span, :]
        got = jnp.where(even, one[pl.ds(0, kept), :], two[pl.ds(0, kept), :])
        mats[0, span, :] = jnp.where(first, own, got)
        mats[1, span, :] = jnp.where(first, got, own)
    got = 0.5 * crossed[pl.ds(kept, EXTRA), :].astype(F32)[0:1]
    gain = (jnp.where(first, half_gain[...], got), jnp.where(first, got, half_gain[...]))

    near_tile, far_tile = near[:, pl.ds(2 * width, size)], far[:, pl.ds(2 * width, size)]
    edge = pl.ds(rows, size)
    for start in range(2 * size, rows, size):
        aggregates[pl.ds(start, size), :] = aggregate[pl.ds(start, size), :].astype(BF16)
    aggregates[edge, :] = (aggregate[edge, :] + dot(far_tile, far[:, pl.ds(width, width)])).astype(BF16)
    aggregates[last, :] = (aggregate[last, :] + far[:, pl.ds(0, width)].astype(F32)).astype(BF16)

    for start in (*range(size, rows + size, size), 0, total - size):
        span = pl.ds(start, size)
        source = near_aggregate if start < 2 * size else aggregates
        if start == 0:
            before = near[:, pl.ds(width, width)]
        elif start < total - size:
            before = state[pl.ds(start - size, size), :]
        else:
            before = far[:, pl.ds(width, width)]
        next_states[span, :] = layer(source[span, :], mats[0], gain[0], before)

    inner = dot(adjacency[inside, :], next_states[inside, :])
    inner = jnp.concatenate(
        [
            inner[:size] + dot(near_tile, next_states[pl.ds(0, size), :]),
            *([inner[size : rows - size]] if rows > 2 * size else []),
            inner[rows - size :] + dot(far_tile, next_states[last, :]),
        ],
        axis=0,
    ).astype(BF16)
    for block in range(rows // size):
        start = block * size
        after = layer(inner[start : start + size], mats[1], gain[1], next_states[pl.ds(size + start, size), :])
        weighted = after.astype(F32) * head_row[...]
        folded = weighted[:, :size]
        for at in range(size, width, size):
            folded = folded + weighted[:, at : at + size]
        outcome[:, placed(block, rows // size, shard, size)] = jnp.sum(folded.T, axis=0, keepdims=True)


def paired(features, labels, label_table, tiles, tile_rows, tile_cols, tile_live, weights, gains, head_weight):
    shard_count = lax.axis_size("shard")
    groups, rows, width = features.shape
    _, slots, size, _ = tiles.shape
    depth = weights.shape[1]
    kept = depth // 2
    classes = label_table.shape[0]
    message = jax.ShapeDtypeStruct((size, 2 * width + size), BF16)
    vmem = pl.BlockSpec(memory_space=pltpu.VMEM)
    hbm = pl.BlockSpec(memory_space=pltpu.HBM)
    table_rows = -(-3 * classes // PAD) * PAD

    far, near, crossing, state, adjacency = pl.pallas_call(
        first_kernel,
        out_shape=(
            message,
            message,
            jax.ShapeDtypeStruct((kept + EXTRA, width), BF16),
            jax.ShapeDtypeStruct((rows, width), BF16),
            jax.ShapeDtypeStruct((rows + 2 * size, rows), BF16),
        ),
        in_specs=[hbm] * 9,
        out_specs=(vmem,) * 5,
        scratch_shapes=[
            pltpu.SMEM((groups, slots), jnp.int32),
            pltpu.SMEM((groups, slots), jnp.int32),
            pltpu.SMEM((1, groups), jnp.int32),
            pltpu.VMEM((groups, rows), jnp.int32),
            pltpu.VMEM((classes, width), F32),
            pltpu.VMEM((slots, size, size), BF16),
            pltpu.VMEM((rows, width), BF16),
            pltpu.VMEM((1, width), BF16),
            pltpu.VMEM((table_rows, width), F32),
            pltpu.VMEM((rows + 2 * size, rows), F32),
            pltpu.SemaphoreType.DMA((7 + 2 * (rows // size),)),
        ],
        compiler_params=pltpu.CompilerParams(vmem_limit_bytes=16 * 2**20),
        name="messages",
    )(*in_hbm(tile_rows, tile_cols, tile_live.T, labels, label_table, tiles, features, gains, weights))

    beside = [(i, i ^ 1) for i in range(shard_count)]
    apart = [(i, (i + 1) % shard_count) for i in range(1, shard_count, 2)]
    apart += [(b, a) for a, b in apart]
    across = [(0, 1), (1, 0)]
    crossed = lax.ppermute(crossing, "section", across)
    far = lax.ppermute(far, "shard", apart)
    near = lax.ppermute(near, "shard", beside)

    aggregate, own_weight, half_gain, head_row = pl.pallas_call(
        waiting_kernel,
        out_shape=(
            jax.ShapeDtypeStruct((rows + 2 * size, width), F32),
            jax.ShapeDtypeStruct((depth, width), BF16),
            jax.ShapeDtypeStruct((1, width), F32),
            jax.ShapeDtypeStruct((1, width), F32),
        ),
        in_specs=[vmem] * 2 + [hbm] * 3,
        out_specs=(vmem,) * 4,
        scratch_shapes=[
            pltpu.VMEM((1, width), BF16),
            pltpu.SemaphoreType.DMA((3,)),
        ],
        compiler_params=pltpu.CompilerParams(vmem_limit_bytes=16 * 2**20),
        cost_estimate=pl.CostEstimate(flops=4 * 10**9, bytes_accessed=2**20, transcendentals=0),
        name="waiting",
    )(adjacency, state, *in_hbm(head_weight.reshape(1, width), gains, weights))

    near_aggregate = pl.pallas_call(
        near_kernel,
        out_shape=jax.ShapeDtypeStruct((2 * size, width), BF16),
        in_specs=[vmem] * 2,
        out_specs=vmem,
        compiler_params=pltpu.CompilerParams(vmem_limit_bytes=16 * 2**20),
        name="beside",
    )(near, aggregate)

    crossed, near_aggregate = lax.optimization_barrier((crossed, near_aggregate))
    relayed = lax.ppermute(crossed, "shard", beside)

    return pl.pallas_call(
        second_kernel,
        out_shape=jax.ShapeDtypeStruct((1, rows), F32),
        in_specs=[vmem] * 11,
        out_specs=vmem,
        scratch_shapes=[
            pltpu.VMEM((2, depth, width), BF16),
            pltpu.VMEM((rows + 2 * size, width), BF16),
            pltpu.VMEM((rows + 2 * size, width), BF16),
        ],
        compiler_params=pltpu.CompilerParams(vmem_limit_bytes=32 * 2**20),
        name="layers",
    )(
        adjacency, state, far, near, crossed, relayed, near_aggregate, aggregate, own_weight, half_gain, head_row,
    )


def extended_2(block, sides, width):
    for axis, dim in sides:
        count = lax.axis_size(axis)
        forward = [(i, i + 1) for i in range(count - 1)]
        backward = [(target, source) for source, target in forward]
        low = lax.ppermute(
            lax.slice_in_dim(block, block.shape[dim] - width, None, axis=dim), axis, forward
        )
        high = lax.ppermute(lax.slice_in_dim(block, 0, width, axis=dim), axis, backward)
        block = jnp.concatenate([low, block, high], axis=dim)
    return block


def body(
    features,
    labels,
    label_table,
    tiles,
    tile_rows,
    tile_cols,
    tile_live,
    weights,
    gains,
    head_weight,
):
    section_count = lax.axis_size("section")
    section_index = lax.axis_index("section")
    shard_index = lax.axis_index("shard")
    batch_count = features.shape[0]
    row_count = features.shape[1]
    feature_width = features.shape[2]
    tile_size = tiles.shape[2]
    slot_count = tiles.shape[1]
    label_count = label_table.shape[0]
    per_rows = row_count // tile_size
    per_section = batch_count // section_count
    slot_ids = jnp.arange(slot_count, dtype=jnp.int32)
    place_ids = jnp.arange(per_rows + 2, dtype=jnp.int32)

    def apply_layer(state, parts, layer_weight, layer_gain):
        group_tiles, col_local, placing, from_below, from_above = parts
        block_view = state.reshape(per_rows, tile_size, feature_width)
        chosen_blocks = jnp.take(block_view, col_local, axis=0)
        products = jnp.einsum(
            "kab,kbd->kad", group_tiles, chosen_blocks, preferred_element_type=jnp.float32
        )
        partial_value = jnp.einsum(
            "kp,kad->pad", placing, products, precision=lax.Precision.HIGHEST
        )
        edge_states = jnp.concatenate([state[:tile_size], state[row_count - tile_size :]], axis=0)
        extended = extended_2(edge_states, (("shard", 0),), tile_size)
        below_block = extended[:tile_size].astype(jnp.float32)
        above_block = extended[extended.shape[0] - tile_size :].astype(jnp.float32)
        own_rows = partial_value.reshape(row_count, feature_width)
        own_rows = own_rows.at[:tile_size].add(
            jnp.dot(from_below, below_block, precision=lax.Precision.HIGHEST)
        )
        own_rows = own_rows.at[row_count - tile_size :].add(
            jnp.dot(from_above, above_block, precision=lax.Precision.HIGHEST)
        )
        aggregate = own_rows.astype(jnp.bfloat16)
        projected = jnp.dot(aggregate, layer_weight, preferred_element_type=jnp.float32)
        scale = lax.rsqrt(jnp.mean(projected * projected, axis=-1, keepdims=True) + 1e-06)
        normed = projected * scale * layer_gain.astype(jnp.float32)
        return (state.astype(jnp.float32) + jax.nn.gelu(normed)).astype(jnp.bfloat16)

    layer_mats, layer_gains = (
        lax.all_gather(weights, "section", axis=0, tiled=True),
        lax.all_gather(gains, "section", axis=0, tiled=True),
    )
    batch_index = section_index * per_section + 0
    group_tiles = lax.dynamic_index_in_dim(tiles, batch_index, 0, keepdims=False)
    group_rows = lax.dynamic_index_in_dim(tile_rows, batch_index, 0, keepdims=False)
    group_cols = lax.dynamic_index_in_dim(tile_cols, batch_index, 0, keepdims=False)
    group_live = lax.dynamic_index_in_dim(tile_live, batch_index, 0, keepdims=False)
    col_local = group_cols - shard_index * per_rows
    slot_local = group_rows - (shard_index * per_rows - 1)
    live_mask = (slot_ids < group_live[0]).astype(jnp.float32)
    placing = (slot_local[:, None] == place_ids[None, :]).astype(jnp.float32) * live_mask[:, None]
    edge_pick = jnp.stack([placing[:, 0], placing[:, per_rows + 1]], axis=1)
    edge_tiles = jnp.einsum(
        "kp,kab->pab", edge_pick, group_tiles.astype(jnp.float32), precision=lax.Precision.HIGHEST
    )
    received = extended_2(edge_tiles, (("shard", 0),), 1)
    parts = (group_tiles, col_local, placing[:, 1 : per_rows + 1], received[0], received[3])

    def through(layer_index, state):
        return apply_layer(state, parts, layer_mats[layer_index], layer_gains[layer_index])

    group_labels = lax.dynamic_index_in_dim(labels, batch_index, 0, keepdims=False)
    group_features = lax.dynamic_index_in_dim(features, batch_index, 0, keepdims=False)
    labels_hot = (
        group_labels[:, None] == jnp.arange(label_count, dtype=jnp.int32)[None, :]
    ).astype(jnp.float32)
    embedded = jnp.dot(labels_hot, label_table, precision=lax.Precision.HIGHEST)
    state = lax.fori_loop(
        0,
        section_count,
        through,
        (group_features.astype(jnp.float32) + embedded).astype(jnp.bfloat16),
    )
    results = [jnp.dot(state.astype(jnp.float32), head_weight, precision=lax.Precision.HIGHEST)]
    return jnp.stack(results)


def solution(mesh):
    return jax.shard_map(
        paired if mesh.shape["section"] == 2 else body,
        mesh=mesh,
        in_specs=(
            P(None, "shard", None),
            P(None, "shard"),
            P(),
            P(None, "shard", None, None),
            P(None, "shard"),
            P(None, "shard"),
            P(None, "shard"),
            P("section", None, None),
            P("section", None),
            P(),
        ),
        out_specs=P("section", "shard"),
        check_vma=False,
    )
```

```python
import jax
import jax.numpy as jnp
from jax import lax
from jax.experimental import pallas as pl
from jax.experimental.pallas import tpu as pltpu
from jax.sharding import PartitionSpec as P

BF16 = jnp.bfloat16
F32 = jnp.float32
PAD = 16
EXTRA = 8
GELU_LINEAR = 2.0 * (2.0 / 3.141592653589793) ** 0.5
GELU_CUBIC = 4.0 * GELU_LINEAR * 0.044715


def split3(value):
    high = value.astype(BF16).astype(F32)
    rest = value - high
    mid = rest.astype(BF16).astype(F32)
    return high, mid, rest - mid


def dot(a, b, dims=((1,), (0,))):
    return lax.dot_general(a, b, (dims, ((), ())), preferred_element_type=F32)


def in_hbm(*arrays):
    return [pltpu.with_memory_space_constraint(array, pltpu.HBM) for array in arrays]


def layer(aggregate, weight, half_gain, state):
    projected = dot(aggregate, weight)
    scale = lax.rsqrt(jnp.mean(projected * projected, axis=-1, keepdims=True) + 1e-06)
    half = (projected * scale * half_gain).astype(BF16)
    inner = half * (BF16(GELU_LINEAR) + BF16(GELU_CUBIC) * (half * half))
    return state + (half + half * jnp.tanh(inner))


def placed(block, blocks, shard, size):
    mirrored = 1 - lax.rem(shard, 2)
    return pl.ds(pl.multiple_of((block + mirrored * (blocks - 1 - 2 * block)) * size, size), size)


def first_kernel(
    tile_rows, tile_cols, tile_live, labels, label_table, tiles, features, gains, weights,
    far, near, crossing, state_out, adjacency_out,
    rows_buf, cols_buf, live_buf, labels_buf, classes_buf, tiles_buf, features_buf, gains_buf, table_buf, sums, sems,
):
    section = lax.axis_index("section")
    shard = lax.axis_index("shard")
    rows, width = features_buf.shape
    slots, size, _ = tiles_buf.shape
    blocks = rows // size
    kept = crossing.shape[0] - EXTRA
    group = section

    small = [(tile_rows, rows_buf), (tile_cols, cols_buf), (tile_live, live_buf)]
    named = [(label_table, classes_buf)]
    spread = []
    for block in range(blocks):
        span, place = pl.ds(block * size, size), placed(block, blocks, shard, size)
        named.append((labels.at[:, span], labels_buf.at[:, place]))
        spread.append((features.at[group, span], features_buf.at[place]))
    half = pl.ds(pl.multiple_of(lax.rem(shard, 2) * kept, kept), kept)
    sent = [(gains, gains_buf), (weights.at[0, half], crossing.at[pl.ds(0, kept)])]
    batches, count = [], 0
    for batch in (small, named, [(tiles.at[group], tiles_buf)], spread, sent):
        batches.append([
            pltpu.make_async_copy(source, target, sems.at[count + index])
            for index, (source, target) in enumerate(batch)
        ])
        count += len(batch)
    for batch in batches:
        for copy in batch:
            copy.start()
    sums[...] = jnp.zeros_like(sums)
    table_buf[...] = jnp.zeros_like(table_buf)

    for copy in batches[1]:
        copy.wait()
    classes = classes_buf.shape[0]
    for part, value in enumerate(split3(classes_buf[...])):
        table_buf[pl.ds(part * classes, classes), :] = value
    depth = table_buf.shape[0]
    index = lax.broadcasted_iota(jnp.int32, (depth, rows), 0)
    wanted = jnp.where(
        index < classes, index,
        jnp.where(index < 2 * classes, index - classes, jnp.where(index < 3 * classes, index - 2 * classes, -1)),
    )
    hot = (wanted == labels_buf[pl.ds(group, 1), :]).astype(F32).astype(BF16)
    embedded = dot(hot, table_buf[...].astype(BF16), ((0,), (0,)))

    for copy in batches[0] + batches[2]:
        copy.wait()
    for slot in range(slots):
        @pl.when(slot < live_buf[0, group])
        def _():
            row = rows_buf[group, slot] - (shard * blocks - 1)
            col = cols_buf[group, slot] - shard * blocks
            sums[placed(row, blocks + 2, shard, size), placed(col, blocks, shard, size)] += tiles_buf[slot].astype(F32)
    adjacency = sums[...].astype(BF16)
    adjacency_out[...] = adjacency

    for copy in batches[3]:
        copy.wait()
    state = (features_buf[...].astype(F32) + embedded).astype(BF16)
    state_out[...] = state
    partial = dot(adjacency[size : size + rows], state).astype(BF16)
    near[:, pl.ds(0, width)] = partial[:size]
    near[:, pl.ds(width, width)] = state[:size]
    near[:, pl.ds(2 * width, size)] = adjacency[:size, :size]
    far[:, pl.ds(0, width)] = partial[rows - size :]
    far[:, pl.ds(width, width)] = state[rows - size :]
    far[:, pl.ds(2 * width, size)] = adjacency[rows + size :, rows - size :]
    batches[4][0].wait()
    crossing[pl.ds(kept, EXTRA), :] = jnp.broadcast_to(gains_buf[...].astype(F32), (EXTRA, width)).astype(BF16)
    batches[4][1].wait()


def waiting_kernel(
    adjacency, state, head, gains, weights,
    aggregate, weight, half_gain, head_row,
    gains_buf, sems,
):
    copies = [
        pltpu.make_async_copy(source, target, sems.at[index])
        for index, (source, target) in enumerate(((weights.at[0], weight), (head, head_row), (gains, gains_buf)))
    ]
    for copy in copies:
        copy.start()
    aggregate[...] = dot(adjacency[...], state[...])
    copies[2].wait()
    half_gain[...] = 0.5 * gains_buf[...].astype(F32)
    copies[0].wait()
    copies[1].wait()


def near_kernel(near, aggregate, state, weight, half_gain, near_blocks):
    size, width = near.shape[0], aggregate.shape[1]
    near_state = near[:, pl.ds(width, width)]
    first, second = pl.ds(0, size), pl.ds(size, size)
    near_blocks[first, :] = (aggregate[first, :] + near[:, pl.ds(0, width)].astype(F32)).astype(BF16)
    near_blocks[second, :] = (aggregate[second, :] + dot(near[:, pl.ds(2 * width, size)], near_state)).astype(BF16)

    @pl.when(lax.axis_index("section") == 0)
    def _():
        for span, before in ((first, near_state), (second, state[pl.ds(0, size), :])):
            near_blocks[span, :] = layer(near_blocks[span, :], weight[...], half_gain[...], before)


def second_kernel(*refs):
    first = lax.axis_index("section") == 0

    @pl.when(first)
    def _():
        both_layers(True, *refs)

    @pl.when(jnp.logical_not(first))
    def _():
        both_layers(False, *refs)


def both_layers(
    own_first, adjacency, state, far, near, crossed, relayed, near_blocks, aggregate, own_weight, half_gain, head_row,
    outcome,
    got_weight, aggregates, next_states,
):
    shard = lax.axis_index("shard")
    even = lax.rem(shard, 2) == 0
    rows, width = state.shape
    size = near.shape[0]
    kept = crossed.shape[0] - EXTRA
    total = rows + 2 * size
    inside, last = pl.ds(size, rows), pl.ds(size + rows, size)

    for place, (one, two) in enumerate(((crossed, relayed), (relayed, crossed))):
        got_weight[pl.ds(place * kept, kept), :] = jnp.where(even, one[pl.ds(0, kept), :], two[pl.ds(0, kept), :])
    got_gain = 0.5 * crossed[pl.ds(kept, EXTRA), :].astype(F32)[0:1]
    used = ((own_weight, half_gain[...]), (got_weight, got_gain))
    (weight, gain), (last_weight, last_gain) = used if own_first else used[::-1]

    near_tile, far_tile = near[:, pl.ds(2 * width, size)], far[:, pl.ds(2 * width, size)]
    edge = pl.ds(rows, size)
    for start in range(2 * size, rows, size):
        aggregates[pl.ds(start, size), :] = aggregate[pl.ds(start, size), :].astype(BF16)
    aggregates[edge, :] = (aggregate[edge, :] + dot(far_tile, far[:, pl.ds(width, width)])).astype(BF16)
    aggregates[last, :] = (aggregate[last, :] + far[:, pl.ds(0, width)].astype(F32)).astype(BF16)

    def step(source, start, before):
        span = pl.ds(start, size)
        next_states[span, :] = layer(source[span, :], weight[...], gain, before)

    if own_first:
        next_states[pl.ds(0, 2 * size), :] = near_blocks[...]
    else:
        step(near_blocks, size, state[pl.ds(0, size), :])
    for start in range(2 * size, rows + size, size):
        step(aggregates, start, state[pl.ds(start - size, size), :])
    if not own_first:
        step(near_blocks, 0, near[:, pl.ds(width, width)])
    step(aggregates, total - size, far[:, pl.ds(width, width)])

    inner = dot(adjacency[inside, :], next_states[inside, :])
    inner = jnp.concatenate(
        [
            inner[:size] + dot(near_tile, next_states[pl.ds(0, size), :]),
            *([inner[size : rows - size]] if rows > 2 * size else []),
            inner[rows - size :] + dot(far_tile, next_states[last, :]),
        ],
        axis=0,
    ).astype(BF16)
    for block in range(rows // size):
        start = block * size
        before = next_states[pl.ds(size + start, size), :]
        after = layer(inner[start : start + size], last_weight[...], last_gain, before)
        weighted = after.astype(F32) * head_row[...]
        folded = weighted[:, :size]
        for at in range(size, width, size):
            folded = folded + weighted[:, at : at + size]
        outcome[:, placed(block, rows // size, shard, size)] = jnp.sum(folded.T, axis=0, keepdims=True)


def paired(features, labels, label_table, tiles, tile_rows, tile_cols, tile_live, weights, gains, head_weight):
    shard_count = lax.axis_size("shard")
    groups, rows, width = features.shape
    _, slots, size, _ = tiles.shape
    depth = weights.shape[1]
    kept = depth // 2
    classes = label_table.shape[0]
    message = jax.ShapeDtypeStruct((size, 2 * width + size), BF16)
    vmem = pl.BlockSpec(memory_space=pltpu.VMEM)
    hbm = pl.BlockSpec(memory_space=pltpu.HBM)
    table_rows = -(-3 * classes // PAD) * PAD

    far, near, crossing, state, adjacency = pl.pallas_call(
        first_kernel,
        out_shape=(
            message,
            message,
            jax.ShapeDtypeStruct((kept + EXTRA, width), BF16),
            jax.ShapeDtypeStruct((rows, width), BF16),
            jax.ShapeDtypeStruct((rows + 2 * size, rows), BF16),
        ),
        in_specs=[hbm] * 9,
        out_specs=(vmem,) * 5,
        scratch_shapes=[
            pltpu.SMEM((groups, slots), jnp.int32),
            pltpu.SMEM((groups, slots), jnp.int32),
            pltpu.SMEM((1, groups), jnp.int32),
            pltpu.VMEM((groups, rows), jnp.int32),
            pltpu.VMEM((classes, width), F32),
            pltpu.VMEM((slots, size, size), BF16),
            pltpu.VMEM((rows, width), BF16),
            pltpu.VMEM((1, width), BF16),
            pltpu.VMEM((table_rows, width), F32),
            pltpu.VMEM((rows + 2 * size, rows), F32),
            pltpu.SemaphoreType.DMA((7 + 2 * (rows // size),)),
        ],
        compiler_params=pltpu.CompilerParams(vmem_limit_bytes=16 * 2**20),
        name="messages",
    )(*in_hbm(tile_rows, tile_cols, tile_live.T, labels, label_table, tiles, features, gains, weights))

    beside = [(i, i ^ 1) for i in range(shard_count)]
    apart = [(i, (i + 1) % shard_count) for i in range(1, shard_count, 2)]
    apart += [(b, a) for a, b in apart]
    across = [(0, 1), (1, 0)]
    crossed = lax.ppermute(crossing, "section", across)
    far = lax.ppermute(far, "shard", apart)
    near = lax.ppermute(near, "shard", beside)

    aggregate, own_weight, half_gain, head_row = pl.pallas_call(
        waiting_kernel,
        out_shape=(
            jax.ShapeDtypeStruct((rows + 2 * size, width), F32),
            jax.ShapeDtypeStruct((depth, width), BF16),
            jax.ShapeDtypeStruct((1, width), F32),
            jax.ShapeDtypeStruct((1, width), F32),
        ),
        in_specs=[vmem] * 2 + [hbm] * 3,
        out_specs=(vmem,) * 4,
        scratch_shapes=[
            pltpu.VMEM((1, width), BF16),
            pltpu.SemaphoreType.DMA((3,)),
        ],
        compiler_params=pltpu.CompilerParams(vmem_limit_bytes=16 * 2**20),
        cost_estimate=pl.CostEstimate(flops=4 * 10**9, bytes_accessed=2**20, transcendentals=0),
        name="waiting",
    )(adjacency, state, *in_hbm(head_weight.reshape(1, width), gains, weights))

    near_blocks = pl.pallas_call(
        near_kernel,
        out_shape=jax.ShapeDtypeStruct((2 * size, width), BF16),
        in_specs=[vmem] * 5,
        out_specs=vmem,
        compiler_params=pltpu.CompilerParams(vmem_limit_bytes=16 * 2**20),
        name="beside",
    )(near, aggregate, state, own_weight, half_gain)

    crossed, near_blocks = lax.optimization_barrier((crossed, near_blocks))
    relayed = lax.ppermute(crossed, "shard", beside)

    return pl.pallas_call(
        second_kernel,
        out_shape=jax.ShapeDtypeStruct((1, rows), F32),
        in_specs=[vmem] * 11,
        out_specs=vmem,
        scratch_shapes=[
            pltpu.VMEM((depth, width), BF16),
            pltpu.VMEM((rows + 2 * size, width), BF16),
            pltpu.VMEM((rows + 2 * size, width), BF16),
        ],
        compiler_params=pltpu.CompilerParams(vmem_limit_bytes=32 * 2**20),
        name="layers",
    )(
        adjacency, state, far, near, crossed, relayed, near_blocks, aggregate, own_weight, half_gain, head_row,
    )


def extended_2(block, sides, width):
    for axis, dim in sides:
        count = lax.axis_size(axis)
        forward = [(i, i + 1) for i in range(count - 1)]
        backward = [(target, source) for source, target in forward]
        low = lax.ppermute(
            lax.slice_in_dim(block, block.shape[dim] - width, None, axis=dim), axis, forward
        )
        high = lax.ppermute(lax.slice_in_dim(block, 0, width, axis=dim), axis, backward)
        block = jnp.concatenate([low, block, high], axis=dim)
    return block


def body(
    features,
    labels,
    label_table,
    tiles,
    tile_rows,
    tile_cols,
    tile_live,
    weights,
    gains,
    head_weight,
):
    section_count = lax.axis_size("section")
    section_index = lax.axis_index("section")
    shard_index = lax.axis_index("shard")
    batch_count = features.shape[0]
    row_count = features.shape[1]
    feature_width = features.shape[2]
    tile_size = tiles.shape[2]
    slot_count = tiles.shape[1]
    label_count = label_table.shape[0]
    per_rows = row_count // tile_size
    per_section = batch_count // section_count
    slot_ids = jnp.arange(slot_count, dtype=jnp.int32)
    place_ids = jnp.arange(per_rows + 2, dtype=jnp.int32)

    def apply_layer(state, parts, layer_weight, layer_gain):
        group_tiles, col_local, placing, from_below, from_above = parts
        block_view = state.reshape(per_rows, tile_size, feature_width)
        chosen_blocks = jnp.take(block_view, col_local, axis=0)
        products = jnp.einsum(
            "kab,kbd->kad", group_tiles, chosen_blocks, preferred_element_type=jnp.float32
        )
        partial_value = jnp.einsum(
            "kp,kad->pad", placing, products, precision=lax.Precision.HIGHEST
        )
        edge_states = jnp.concatenate([state[:tile_size], state[row_count - tile_size :]], axis=0)
        extended = extended_2(edge_states, (("shard", 0),), tile_size)
        below_block = extended[:tile_size].astype(jnp.float32)
        above_block = extended[extended.shape[0] - tile_size :].astype(jnp.float32)
        own_rows = partial_value.reshape(row_count, feature_width)
        own_rows = own_rows.at[:tile_size].add(
            jnp.dot(from_below, below_block, precision=lax.Precision.HIGHEST)
        )
        own_rows = own_rows.at[row_count - tile_size :].add(
            jnp.dot(from_above, above_block, precision=lax.Precision.HIGHEST)
        )
        aggregate = own_rows.astype(jnp.bfloat16)
        projected = jnp.dot(aggregate, layer_weight, preferred_element_type=jnp.float32)
        scale = lax.rsqrt(jnp.mean(projected * projected, axis=-1, keepdims=True) + 1e-06)
        normed = projected * scale * layer_gain.astype(jnp.float32)
        return (state.astype(jnp.float32) + jax.nn.gelu(normed)).astype(jnp.bfloat16)

    layer_mats, layer_gains = (
        lax.all_gather(weights, "section", axis=0, tiled=True),
        lax.all_gather(gains, "section", axis=0, tiled=True),
    )
    batch_index = section_index * per_section + 0
    group_tiles = lax.dynamic_index_in_dim(tiles, batch_index, 0, keepdims=False)
    group_rows = lax.dynamic_index_in_dim(tile_rows, batch_index, 0, keepdims=False)
    group_cols = lax.dynamic_index_in_dim(tile_cols, batch_index, 0, keepdims=False)
    group_live = lax.dynamic_index_in_dim(tile_live, batch_index, 0, keepdims=False)
    col_local = group_cols - shard_index * per_rows
    slot_local = group_rows - (shard_index * per_rows - 1)
    live_mask = (slot_ids < group_live[0]).astype(jnp.float32)
    placing = (slot_local[:, None] == place_ids[None, :]).astype(jnp.float32) * live_mask[:, None]
    edge_pick = jnp.stack([placing[:, 0], placing[:, per_rows + 1]], axis=1)
    edge_tiles = jnp.einsum(
        "kp,kab->pab", edge_pick, group_tiles.astype(jnp.float32), precision=lax.Precision.HIGHEST
    )
    received = extended_2(edge_tiles, (("shard", 0),), 1)
    parts = (group_tiles, col_local, placing[:, 1 : per_rows + 1], received[0], received[3])

    def through(layer_index, state):
        return apply_layer(state, parts, layer_mats[layer_index], layer_gains[layer_index])

    group_labels = lax.dynamic_index_in_dim(labels, batch_index, 0, keepdims=False)
    group_features = lax.dynamic_index_in_dim(features, batch_index, 0, keepdims=False)
    labels_hot = (
        group_labels[:, None] == jnp.arange(label_count, dtype=jnp.int32)[None, :]
    ).astype(jnp.float32)
    embedded = jnp.dot(labels_hot, label_table, precision=lax.Precision.HIGHEST)
    state = lax.fori_loop(
        0,
        section_count,
        through,
        (group_features.astype(jnp.float32) + embedded).astype(jnp.bfloat16),
    )
    results = [jnp.dot(state.astype(jnp.float32), head_weight, precision=lax.Precision.HIGHEST)]
    return jnp.stack(results)


def solution(mesh):
    return jax.shard_map(
        paired if mesh.shape["section"] == 2 else body,
        mesh=mesh,
        in_specs=(
            P(None, "shard", None),
            P(None, "shard"),
            P(),
            P(None, "shard", None, None),
            P(None, "shard"),
            P(None, "shard"),
            P(None, "shard"),
            P("section", None, None),
            P("section", None),
            P(),
        ),
        out_specs=P("section", "shard"),
        check_vma=False,
    )
```

```python
import jax
import jax.numpy as jnp
from jax import lax
from jax.experimental import pallas as pl
from jax.experimental.pallas import tpu as pltpu
from jax.sharding import PartitionSpec as P

BF16 = jnp.bfloat16
F32 = jnp.float32
PAD = 16
EXTRA = 8
GELU_LINEAR = 2.0 * (2.0 / 3.141592653589793) ** 0.5
GELU_CUBIC = 4.0 * GELU_LINEAR * 0.044715


def split3(value):
    high = value.astype(BF16).astype(F32)
    rest = value - high
    mid = rest.astype(BF16).astype(F32)
    return high, mid, rest - mid


def dot(a, b, dims=((1,), (0,))):
    return lax.dot_general(a, b, (dims, ((), ())), preferred_element_type=F32)


def in_hbm(*arrays):
    return [pltpu.with_memory_space_constraint(array, pltpu.HBM) for array in arrays]


def layer(aggregate, weight, half_gain, state):
    projected = dot(aggregate, weight)
    scale = lax.rsqrt(jnp.mean(projected * projected, axis=-1, keepdims=True) + 1e-06)
    half = (projected * scale * half_gain).astype(BF16)
    inner = half * (BF16(GELU_LINEAR) + BF16(GELU_CUBIC) * (half * half))
    return state + (half + half * jnp.tanh(inner))


def placed(block, blocks, shard, size):
    mirrored = 1 - lax.rem(shard, 2)
    return pl.ds(pl.multiple_of((block + mirrored * (blocks - 1 - 2 * block)) * size, size), size)


def first_kernel(
    tile_rows, tile_cols, tile_live, labels, label_table, tiles, features, gains, weights,
    far, far_sum, near, crossing, state_out, adjacency_out,
    rows_buf, cols_buf, live_buf, labels_buf, classes_buf, tiles_buf, features_buf, gains_buf, table_buf, sums, sems,
):
    section = lax.axis_index("section")
    shard = lax.axis_index("shard")
    rows, width = features_buf.shape
    slots, size, _ = tiles_buf.shape
    blocks = rows // size
    kept = crossing.shape[0] - EXTRA
    group = section

    small = [(tile_rows, rows_buf), (tile_cols, cols_buf), (tile_live, live_buf)]
    named = [(label_table, classes_buf)]
    spread = []
    for block in range(blocks):
        span, place = pl.ds(block * size, size), placed(block, blocks, shard, size)
        named.append((labels.at[:, span], labels_buf.at[:, place]))
        spread.append((features.at[group, span], features_buf.at[place]))
    half = pl.ds(pl.multiple_of(lax.rem(shard, 2) * kept, kept), kept)
    sent = [(gains, gains_buf), (weights.at[0, half], crossing.at[pl.ds(0, kept)])]
    batches, count = [], 0
    for batch in (small, named, [(tiles.at[group], tiles_buf)], spread, sent):
        batches.append([
            pltpu.make_async_copy(source, target, sems.at[count + index])
            for index, (source, target) in enumerate(batch)
        ])
        count += len(batch)
    for batch in batches:
        for copy in batch:
            copy.start()
    sums[...] = jnp.zeros_like(sums)
    table_buf[...] = jnp.zeros_like(table_buf)

    for copy in batches[1]:
        copy.wait()
    classes = classes_buf.shape[0]
    for part, value in enumerate(split3(classes_buf[...])):
        table_buf[pl.ds(part * classes, classes), :] = value
    depth = table_buf.shape[0]
    index = lax.broadcasted_iota(jnp.int32, (depth, rows), 0)
    wanted = jnp.where(
        index < classes, index,
        jnp.where(index < 2 * classes, index - classes, jnp.where(index < 3 * classes, index - 2 * classes, -1)),
    )
    hot = (wanted == labels_buf[pl.ds(group, 1), :]).astype(F32).astype(BF16)
    embedded = dot(hot, table_buf[...].astype(BF16), ((0,), (0,)))

    for copy in batches[0] + batches[2]:
        copy.wait()
    for slot in range(slots):
        @pl.when(slot < live_buf[0, group])
        def _():
            row = rows_buf[group, slot] - (shard * blocks - 1)
            col = cols_buf[group, slot] - shard * blocks
            sums[placed(row, blocks + 2, shard, size), placed(col, blocks, shard, size)] += tiles_buf[slot].astype(F32)
    adjacency = sums[...].astype(BF16)
    adjacency_out[...] = adjacency

    for copy in batches[3]:
        copy.wait()
    state = (features_buf[...].astype(F32) + embedded).astype(BF16)
    state_out[...] = state
    partial = dot(adjacency[size : size + rows], state).astype(BF16)
    near[:, pl.ds(0, width)] = partial[:size]
    near[:, pl.ds(width, width)] = state[:size]
    near[:, pl.ds(2 * width, size)] = adjacency[:size, :size]
    far_sum[...] = partial[rows - size :]
    far[:, pl.ds(0, width)] = state[rows - size :]
    far[:, pl.ds(width, size)] = adjacency[rows + size :, rows - size :]
    batches[4][0].wait()
    crossing[pl.ds(kept, EXTRA), :] = jnp.broadcast_to(gains_buf[...].astype(F32), (EXTRA, width)).astype(BF16)
    batches[4][1].wait()


def waiting_kernel(
    adjacency, state, head, gains, weights,
    aggregate, weight, half_gain, head_row,
    gains_buf, sems,
):
    copies = [
        pltpu.make_async_copy(source, target, sems.at[index])
        for index, (source, target) in enumerate(((weights.at[0], weight), (head, head_row), (gains, gains_buf)))
    ]
    for copy in copies:
        copy.start()
    aggregate[...] = dot(adjacency[...], state[...])
    copies[2].wait()
    half_gain[...] = 0.5 * gains_buf[...].astype(F32)
    copies[0].wait()
    copies[1].wait()


def near_kernel(near, aggregate, state, weight, half_gain, near_blocks):
    size, width = near.shape[0], aggregate.shape[1]
    near_state = near[:, pl.ds(width, width)]
    first, second = pl.ds(0, size), pl.ds(size, size)
    near_blocks[first, :] = (aggregate[first, :] + near[:, pl.ds(0, width)].astype(F32)).astype(BF16)
    near_blocks[second, :] = (aggregate[second, :] + dot(near[:, pl.ds(2 * width, size)], near_state)).astype(BF16)

    @pl.when(lax.axis_index("section") == 0)
    def _():
        for span, before in ((first, near_state), (second, state[pl.ds(0, size), :])):
            near_blocks[span, :] = layer(near_blocks[span, :], weight[...], half_gain[...], before)


def far_kernel(far, near, near_blocks, aggregate, adjacency, state, weight, half_gain, far_blocks, inner, states):
    size = far.shape[0]
    rows, width = state.shape
    for start in range(0, rows - 2 * size, size):
        far_blocks[pl.ds(start, size), :] = aggregate[pl.ds(2 * size + start, size), :].astype(BF16)
    far_blocks[pl.ds(rows - 2 * size, size), :] = (
        aggregate[pl.ds(rows, size), :] + dot(far[:, pl.ds(width, size)], far[:, pl.ds(0, width)])
    ).astype(BF16)

    @pl.when(lax.axis_index("section") == 0)
    def _():
        for start in range(0, rows - size, size):
            span = pl.ds(start, size)
            far_blocks[span, :] = layer(
                far_blocks[span, :], weight[...], half_gain[...], state[pl.ds(size + start, size), :]
            )
        states[pl.ds(0, size), :] = near_blocks[pl.ds(size, size), :]
        states[pl.ds(size, rows - size), :] = far_blocks[...]
        inner[...] = dot(adjacency[pl.ds(size, rows), :], states[...])
        inner[pl.ds(0, size), :] += dot(near[:, pl.ds(2 * width, size)], near_blocks[pl.ds(0, size), :])


def second_kernel(*refs):
    first = lax.axis_index("section") == 0

    @pl.when(first)
    def _():
        both_layers(True, *refs)

    @pl.when(jnp.logical_not(first))
    def _():
        both_layers(False, *refs)


def both_layers(
    own_first,
    adjacency, state, far, far_sum, near, crossed, relayed, near_blocks, far_blocks, known_inner, aggregate,
    own_weight, half_gain, head_row,
    outcome,
    got_weight, next_states,
):
    shard = lax.axis_index("shard")
    even = lax.rem(shard, 2) == 0
    rows, width = state.shape
    size = near.shape[0]
    kept = crossed.shape[0] - EXTRA
    inside, last = pl.ds(size, rows), pl.ds(size + rows, size)

    for place, (one, two) in enumerate(((crossed, relayed), (relayed, crossed))):
        got_weight[pl.ds(place * kept, kept), :] = jnp.where(even, one[pl.ds(0, kept), :], two[pl.ds(0, kept), :])
    got_gain = 0.5 * crossed[pl.ds(kept, EXTRA), :].astype(F32)[0:1]
    used = ((own_weight, half_gain[...]), (got_weight, got_gain))
    (weight, gain), (last_weight, last_gain) = used if own_first else used[::-1]
    far_tile = far[:, pl.ds(width, size)]
    halo = (aggregate[last, :] + far_sum[...].astype(F32)).astype(BF16)

    if own_first:
        next_states[pl.ds(0, 2 * size), :] = near_blocks[...]
        next_states[pl.ds(2 * size, rows - size), :] = far_blocks[...]
    else:
        for start in range(0, rows, size):
            span = pl.ds(start, size)
            source = near_blocks[pl.ds(size, size), :] if start == 0 else far_blocks[pl.ds(start - size, size), :]
            next_states[pl.ds(size + start, size), :] = layer(source, weight[...], gain, state[span, :])
        next_states[pl.ds(0, size), :] = layer(
            near_blocks[pl.ds(0, size), :], weight[...], gain, near[:, pl.ds(width, width)]
        )
    next_states[last, :] = layer(halo, weight[...], gain, far[:, pl.ds(0, width)])

    if own_first:
        inner = known_inner[...]
    else:
        inner = dot(adjacency[inside, :], next_states[inside, :])
    for block in range(rows // size):
        start = block * size
        summed = inner[start : start + size]
        if block == 0 and not own_first:
            summed = summed + dot(near[:, pl.ds(2 * width, size)], next_states[pl.ds(0, size), :])
        if block == rows // size - 1:
            summed = summed + dot(far_tile, next_states[last, :])
        before = next_states[pl.ds(size + start, size), :]
        after = layer(summed.astype(BF16), last_weight[...], last_gain, before)
        weighted = after.astype(F32) * head_row[...]
        folded = weighted[:, :size]
        for at in range(size, width, size):
            folded = folded + weighted[:, at : at + size]
        outcome[:, placed(block, rows // size, shard, size)] = jnp.sum(folded.T, axis=0, keepdims=True)


def paired(features, labels, label_table, tiles, tile_rows, tile_cols, tile_live, weights, gains, head_weight):
    shard_count = lax.axis_size("shard")
    groups, rows, width = features.shape
    _, slots, size, _ = tiles.shape
    depth = weights.shape[1]
    kept = depth // 2
    classes = label_table.shape[0]
    message = jax.ShapeDtypeStruct((size, 2 * width + size), BF16)
    vmem = pl.BlockSpec(memory_space=pltpu.VMEM)
    hbm = pl.BlockSpec(memory_space=pltpu.HBM)
    table_rows = -(-3 * classes // PAD) * PAD

    far, far_sum, near, crossing, state, adjacency = pl.pallas_call(
        first_kernel,
        out_shape=(
            jax.ShapeDtypeStruct((size, width + size), BF16),
            jax.ShapeDtypeStruct((size, width), BF16),
            message,
            jax.ShapeDtypeStruct((kept + EXTRA, width), BF16),
            jax.ShapeDtypeStruct((rows, width), BF16),
            jax.ShapeDtypeStruct((rows + 2 * size, rows), BF16),
        ),
        in_specs=[hbm] * 9,
        out_specs=(vmem,) * 6,
        scratch_shapes=[
            pltpu.SMEM((groups, slots), jnp.int32),
            pltpu.SMEM((groups, slots), jnp.int32),
            pltpu.SMEM((1, groups), jnp.int32),
            pltpu.VMEM((groups, rows), jnp.int32),
            pltpu.VMEM((classes, width), F32),
            pltpu.VMEM((slots, size, size), BF16),
            pltpu.VMEM((rows, width), BF16),
            pltpu.VMEM((1, width), BF16),
            pltpu.VMEM((table_rows, width), F32),
            pltpu.VMEM((rows + 2 * size, rows), F32),
            pltpu.SemaphoreType.DMA((7 + 2 * (rows // size),)),
        ],
        compiler_params=pltpu.CompilerParams(vmem_limit_bytes=16 * 2**20),
        name="messages",
    )(*in_hbm(tile_rows, tile_cols, tile_live.T, labels, label_table, tiles, features, gains, weights))

    beside = [(i, i ^ 1) for i in range(shard_count)]
    apart = [(i, (i + 1) % shard_count) for i in range(1, shard_count, 2)]
    apart += [(b, a) for a, b in apart]
    across = [(0, 1), (1, 0)]
    crossed = lax.ppermute(crossing, "section", across)
    far = lax.ppermute(far, "shard", apart)
    far_sum = lax.ppermute(far_sum, "shard", apart)
    near = lax.ppermute(near, "shard", beside)

    aggregate, own_weight, half_gain, head_row = pl.pallas_call(
        waiting_kernel,
        out_shape=(
            jax.ShapeDtypeStruct((rows + 2 * size, width), F32),
            jax.ShapeDtypeStruct((depth, width), BF16),
            jax.ShapeDtypeStruct((1, width), F32),
            jax.ShapeDtypeStruct((1, width), F32),
        ),
        in_specs=[vmem] * 2 + [hbm] * 3,
        out_specs=(vmem,) * 4,
        scratch_shapes=[
            pltpu.VMEM((1, width), BF16),
            pltpu.SemaphoreType.DMA((3,)),
        ],
        compiler_params=pltpu.CompilerParams(vmem_limit_bytes=16 * 2**20),
        cost_estimate=pl.CostEstimate(flops=15 * 10**8, bytes_accessed=2**20, transcendentals=0),
        name="waiting",
    )(adjacency, state, *in_hbm(head_weight.reshape(1, width), gains, weights))

    near_blocks = pl.pallas_call(
        near_kernel,
        out_shape=jax.ShapeDtypeStruct((2 * size, width), BF16),
        in_specs=[vmem] * 5,
        out_specs=vmem,
        compiler_params=pltpu.CompilerParams(vmem_limit_bytes=16 * 2**20),
        name="beside",
    )(near, aggregate, state, own_weight, half_gain)

    crossed, near_blocks = lax.optimization_barrier((crossed, near_blocks))
    relayed = lax.ppermute(crossed, "shard", beside)

    far_blocks, inner = pl.pallas_call(
        far_kernel,
        out_shape=(
            jax.ShapeDtypeStruct((rows - size, width), BF16),
            jax.ShapeDtypeStruct((rows, width), F32),
        ),
        in_specs=[vmem] * 8,
        out_specs=(vmem,) * 2,
        scratch_shapes=[pltpu.VMEM((rows, width), BF16)],
        compiler_params=pltpu.CompilerParams(vmem_limit_bytes=16 * 2**20),
        cost_estimate=pl.CostEstimate(flops=4 * 10**9, bytes_accessed=2**20, transcendentals=0),
        name="apart",
    )(far, near, near_blocks, aggregate, adjacency, state, own_weight, half_gain)

    return pl.pallas_call(
        second_kernel,
        out_shape=jax.ShapeDtypeStruct((1, rows), F32),
        in_specs=[vmem] * 14,
        out_specs=vmem,
        scratch_shapes=[
            pltpu.VMEM((depth, width), BF16),
            pltpu.VMEM((rows + 2 * size, width), BF16),
        ],
        compiler_params=pltpu.CompilerParams(vmem_limit_bytes=32 * 2**20),
        name="layers",
    )(
        adjacency, state, far, far_sum, near, crossed, relayed, near_blocks, far_blocks, inner, aggregate,
        own_weight, half_gain, head_row,
    )


def extended_2(block, sides, width):
    for axis, dim in sides:
        count = lax.axis_size(axis)
        forward = [(i, i + 1) for i in range(count - 1)]
        backward = [(target, source) for source, target in forward]
        low = lax.ppermute(
            lax.slice_in_dim(block, block.shape[dim] - width, None, axis=dim), axis, forward
        )
        high = lax.ppermute(lax.slice_in_dim(block, 0, width, axis=dim), axis, backward)
        block = jnp.concatenate([low, block, high], axis=dim)
    return block


def body(
    features,
    labels,
    label_table,
    tiles,
    tile_rows,
    tile_cols,
    tile_live,
    weights,
    gains,
    head_weight,
):
    section_count = lax.axis_size("section")
    section_index = lax.axis_index("section")
    shard_index = lax.axis_index("shard")
    batch_count = features.shape[0]
    row_count = features.shape[1]
    feature_width = features.shape[2]
    tile_size = tiles.shape[2]
    slot_count = tiles.shape[1]
    label_count = label_table.shape[0]
    per_rows = row_count // tile_size
    per_section = batch_count // section_count
    slot_ids = jnp.arange(slot_count, dtype=jnp.int32)
    place_ids = jnp.arange(per_rows + 2, dtype=jnp.int32)

    def apply_layer(state, parts, layer_weight, layer_gain):
        group_tiles, col_local, placing, from_below, from_above = parts
        block_view = state.reshape(per_rows, tile_size, feature_width)
        chosen_blocks = jnp.take(block_view, col_local, axis=0)
        products = jnp.einsum(
            "kab,kbd->kad", group_tiles, chosen_blocks, preferred_element_type=jnp.float32
        )
        partial_value = jnp.einsum(
            "kp,kad->pad", placing, products, precision=lax.Precision.HIGHEST
        )
        edge_states = jnp.concatenate([state[:tile_size], state[row_count - tile_size :]], axis=0)
        extended = extended_2(edge_states, (("shard", 0),), tile_size)
        below_block = extended[:tile_size].astype(jnp.float32)
        above_block = extended[extended.shape[0] - tile_size :].astype(jnp.float32)
        own_rows = partial_value.reshape(row_count, feature_width)
        own_rows = own_rows.at[:tile_size].add(
            jnp.dot(from_below, below_block, precision=lax.Precision.HIGHEST)
        )
        own_rows = own_rows.at[row_count - tile_size :].add(
            jnp.dot(from_above, above_block, precision=lax.Precision.HIGHEST)
        )
        aggregate = own_rows.astype(jnp.bfloat16)
        projected = jnp.dot(aggregate, layer_weight, preferred_element_type=jnp.float32)
        scale = lax.rsqrt(jnp.mean(projected * projected, axis=-1, keepdims=True) + 1e-06)
        normed = projected * scale * layer_gain.astype(jnp.float32)
        return (state.astype(jnp.float32) + jax.nn.gelu(normed)).astype(jnp.bfloat16)

    layer_mats, layer_gains = (
        lax.all_gather(weights, "section", axis=0, tiled=True),
        lax.all_gather(gains, "section", axis=0, tiled=True),
    )
    batch_index = section_index * per_section + 0
    group_tiles = lax.dynamic_index_in_dim(tiles, batch_index, 0, keepdims=False)
    group_rows = lax.dynamic_index_in_dim(tile_rows, batch_index, 0, keepdims=False)
    group_cols = lax.dynamic_index_in_dim(tile_cols, batch_index, 0, keepdims=False)
    group_live = lax.dynamic_index_in_dim(tile_live, batch_index, 0, keepdims=False)
    col_local = group_cols - shard_index * per_rows
    slot_local = group_rows - (shard_index * per_rows - 1)
    live_mask = (slot_ids < group_live[0]).astype(jnp.float32)
    placing = (slot_local[:, None] == place_ids[None, :]).astype(jnp.float32) * live_mask[:, None]
    edge_pick = jnp.stack([placing[:, 0], placing[:, per_rows + 1]], axis=1)
    edge_tiles = jnp.einsum(
        "kp,kab->pab", edge_pick, group_tiles.astype(jnp.float32), precision=lax.Precision.HIGHEST
    )
    received = extended_2(edge_tiles, (("shard", 0),), 1)
    parts = (group_tiles, col_local, placing[:, 1 : per_rows + 1], received[0], received[3])

    def through(layer_index, state):
        return apply_layer(state, parts, layer_mats[layer_index], layer_gains[layer_index])

    group_labels = lax.dynamic_index_in_dim(labels, batch_index, 0, keepdims=False)
    group_features = lax.dynamic_index_in_dim(features, batch_index, 0, keepdims=False)
    labels_hot = (
        group_labels[:, None] == jnp.arange(label_count, dtype=jnp.int32)[None, :]
    ).astype(jnp.float32)
    embedded = jnp.dot(labels_hot, label_table, precision=lax.Precision.HIGHEST)
    state = lax.fori_loop(
        0,
        section_count,
        through,
        (group_features.astype(jnp.float32) + embedded).astype(jnp.bfloat16),
    )
    results = [jnp.dot(state.astype(jnp.float32), head_weight, precision=lax.Precision.HIGHEST)]
    return jnp.stack(results)


def solution(mesh):
    return jax.shard_map(
        paired if mesh.shape["section"] == 2 else body,
        mesh=mesh,
        in_specs=(
            P(None, "shard", None),
            P(None, "shard"),
            P(),
            P(None, "shard", None, None),
            P(None, "shard"),
            P(None, "shard"),
            P(None, "shard"),
            P("section", None, None),
            P("section", None),
            P(),
        ),
        out_specs=P("section", "shard"),
        check_vma=False,
    )
```

```python
import jax
import jax.numpy as jnp
from jax import lax
from jax.experimental import pallas as pl
from jax.experimental.pallas import tpu as pltpu
from jax.sharding import PartitionSpec as P

BF16 = jnp.bfloat16
F32 = jnp.float32
PAD = 16
EXTRA = 8
GELU_LINEAR = 2.0 * (2.0 / 3.141592653589793) ** 0.5
GELU_CUBIC = 4.0 * GELU_LINEAR * 0.044715


def split3(value):
    high = value.astype(BF16).astype(F32)
    rest = value - high
    mid = rest.astype(BF16).astype(F32)
    return high, mid, rest - mid


def dot(a, b, dims=((1,), (0,))):
    return lax.dot_general(a, b, (dims, ((), ())), preferred_element_type=F32)


def in_hbm(*arrays):
    return [pltpu.with_memory_space_constraint(array, pltpu.HBM) for array in arrays]


def layer(aggregate, weight, half_gain, state):
    projected = dot(aggregate, weight)
    scale = lax.rsqrt(jnp.mean(projected * projected, axis=-1, keepdims=True) + 1e-06)
    half = (projected * scale * half_gain).astype(BF16)
    inner = half * (BF16(GELU_LINEAR) + BF16(GELU_CUBIC) * (half * half))
    return state + (half + half * jnp.tanh(inner))


def placed(block, blocks, shard, size):
    mirrored = 1 - lax.rem(shard, 2)
    return pl.ds(pl.multiple_of((block + mirrored * (blocks - 1 - 2 * block)) * size, size), size)


def first_kernel(
    tile_rows, tile_cols, tile_live, labels, label_table, tiles, features, gains, weights,
    far, far_sum, near, crossing, state_out, adjacency_out,
    rows_buf, cols_buf, live_buf, labels_buf, classes_buf, tiles_buf, features_buf, gains_buf, table_buf, sums, sems,
):
    section = lax.axis_index("section")
    shard = lax.axis_index("shard")
    rows, width = features_buf.shape
    slots, size, _ = tiles_buf.shape
    blocks = rows // size
    kept = crossing.shape[0] - EXTRA
    group = section

    small = [(tile_rows, rows_buf), (tile_cols, cols_buf), (tile_live, live_buf)]
    named = [(label_table, classes_buf)]
    spread = []
    for block in range(blocks):
        span, place = pl.ds(block * size, size), placed(block, blocks, shard, size)
        named.append((labels.at[:, span], labels_buf.at[:, place]))
        spread.append((features.at[group, span], features_buf.at[place]))
    half = pl.ds(pl.multiple_of(lax.rem(shard, 2) * kept, kept), kept)
    sent = [(gains, gains_buf), (weights.at[0, half], crossing.at[pl.ds(0, kept)])]
    batches, count = [], 0
    for batch in (small, named, [(tiles.at[group], tiles_buf)], spread, sent):
        batches.append([
            pltpu.make_async_copy(source, target, sems.at[count + index])
            for index, (source, target) in enumerate(batch)
        ])
        count += len(batch)
    for batch in batches:
        for copy in batch:
            copy.start()
    sums[...] = jnp.zeros_like(sums)
    table_buf[...] = jnp.zeros_like(table_buf)

    for copy in batches[1]:
        copy.wait()
    classes = classes_buf.shape[0]
    for part, value in enumerate(split3(classes_buf[...])):
        table_buf[pl.ds(part * classes, classes), :] = value
    depth = table_buf.shape[0]
    index = lax.broadcasted_iota(jnp.int32, (depth, rows), 0)
    wanted = jnp.where(
        index < classes, index,
        jnp.where(index < 2 * classes, index - classes, jnp.where(index < 3 * classes, index - 2 * classes, -1)),
    )
    hot = (wanted == labels_buf[pl.ds(group, 1), :]).astype(F32).astype(BF16)
    embedded = dot(hot, table_buf[...].astype(BF16), ((0,), (0,)))

    for copy in batches[0] + batches[2]:
        copy.wait()
    for slot in range(slots):
        @pl.when(slot < live_buf[0, group])
        def _():
            row = rows_buf[group, slot] - (shard * blocks - 1)
            col = cols_buf[group, slot] - shard * blocks
            sums[placed(row, blocks + 2, shard, size), placed(col, blocks, shard, size)] += tiles_buf[slot].astype(F32)
    adjacency = sums[...].astype(BF16)
    adjacency_out[...] = adjacency

    for copy in batches[3]:
        copy.wait()
    state = (features_buf[...].astype(F32) + embedded).astype(BF16)
    state_out[...] = state
    partial = dot(adjacency[size : size + rows], state).astype(BF16)
    near[:, pl.ds(0, width)] = partial[:size]
    near[:, pl.ds(width, width)] = state[:size]
    near[:, pl.ds(2 * width, size)] = adjacency[:size, :size]
    far_sum[...] = partial[rows - size :]
    far[:, pl.ds(0, width)] = state[rows - size :]
    far[:, pl.ds(width, size)] = adjacency[rows + size :, rows - size :]
    batches[4][0].wait()
    crossing[pl.ds(kept, EXTRA), :] = jnp.broadcast_to(gains_buf[...].astype(F32), (EXTRA, width)).astype(BF16)
    batches[4][1].wait()


def waiting_kernel(
    adjacency, state, head, gains, weights,
    aggregate, weight, half_gain, head_row,
    gains_buf, sems,
):
    copies = [
        pltpu.make_async_copy(source, target, sems.at[index])
        for index, (source, target) in enumerate(((weights.at[0], weight), (head, head_row), (gains, gains_buf)))
    ]
    for copy in copies:
        copy.start()
    aggregate[...] = dot(adjacency[...], state[...])
    copies[2].wait()
    half_gain[...] = 0.5 * gains_buf[...].astype(F32)
    copies[0].wait()
    copies[1].wait()


def near_kernel(near, aggregate, state, weight, half_gain, near_blocks):
    size, width = near.shape[0], aggregate.shape[1]
    near_state = near[:, pl.ds(width, width)]
    first, second = pl.ds(0, size), pl.ds(size, size)
    near_blocks[first, :] = (aggregate[first, :] + near[:, pl.ds(0, width)].astype(F32)).astype(BF16)
    near_blocks[second, :] = (aggregate[second, :] + dot(near[:, pl.ds(2 * width, size)], near_state)).astype(BF16)

    @pl.when(lax.axis_index("section") == 0)
    def _():
        for span, before in ((first, near_state), (second, state[pl.ds(0, size), :])):
            near_blocks[span, :] = layer(near_blocks[span, :], weight[...], half_gain[...], before)


def far_kernel(far, near, near_blocks, aggregate, adjacency, state, weight, half_gain, far_blocks, inner, states):
    size = far.shape[0]
    rows, width = state.shape
    for start in range(0, rows - 2 * size, size):
        far_blocks[pl.ds(start, size), :] = aggregate[pl.ds(2 * size + start, size), :].astype(BF16)
    far_blocks[pl.ds(rows - 2 * size, size), :] = (
        aggregate[pl.ds(rows, size), :] + dot(far[:, pl.ds(width, size)], far[:, pl.ds(0, width)])
    ).astype(BF16)

    @pl.when(lax.axis_index("section") == 0)
    def _():
        for start in range(0, rows - size, size):
            span = pl.ds(start, size)
            far_blocks[span, :] = layer(
                far_blocks[span, :], weight[...], half_gain[...], state[pl.ds(size + start, size), :]
            )
        states[pl.ds(0, size), :] = near_blocks[pl.ds(size, size), :]
        states[pl.ds(size, rows - size), :] = far_blocks[...]
        inner[...] = dot(adjacency[pl.ds(size, rows), :], states[...])
        inner[pl.ds(0, size), :] += dot(near[:, pl.ds(2 * width, size)], near_blocks[pl.ds(0, size), :])


def second_kernel(*refs):
    first = lax.axis_index("section") == 0

    @pl.when(first)
    def _():
        both_layers(True, *refs)

    @pl.when(jnp.logical_not(first))
    def _():
        both_layers(False, *refs)


def both_layers(
    own_first,
    adjacency, state, far, far_sum, near, crossed, relayed, near_blocks, far_blocks, known_inner, aggregate,
    own_weight, half_gain, head_row,
    outcome,
    got_weight, next_states,
):
    shard = lax.axis_index("shard")
    even = lax.rem(shard, 2) == 0
    rows, width = state.shape
    size = near.shape[0]
    kept = crossed.shape[0] - EXTRA
    inside, last = pl.ds(size, rows), pl.ds(size + rows, size)

    for place, (one, two) in enumerate(((crossed, relayed), (relayed, crossed))):
        got_weight[pl.ds(place * kept, kept), :] = jnp.where(even, one[pl.ds(0, kept), :], two[pl.ds(0, kept), :])
    got_gain = 0.5 * crossed[pl.ds(kept, EXTRA), :].astype(F32)[0:1]
    used = ((own_weight, half_gain[...]), (got_weight, got_gain))
    (weight, gain), (last_weight, last_gain) = used if own_first else used[::-1]
    far_tile = far[:, pl.ds(width, size)]
    halo = (aggregate[last, :] + far_sum[...].astype(F32)).astype(BF16)

    if own_first:
        next_states[pl.ds(0, 2 * size), :] = near_blocks[...]
        next_states[pl.ds(2 * size, rows - size), :] = far_blocks[...]
    else:
        for start in range(0, rows, size):
            span = pl.ds(start, size)
            source = near_blocks[pl.ds(size, size), :] if start == 0 else far_blocks[pl.ds(start - size, size), :]
            next_states[pl.ds(size + start, size), :] = layer(source, weight[...], gain, state[span, :])
        next_states[pl.ds(0, size), :] = layer(
            near_blocks[pl.ds(0, size), :], weight[...], gain, near[:, pl.ds(width, width)]
        )
    next_states[last, :] = layer(halo, weight[...], gain, far[:, pl.ds(0, width)])

    if own_first:
        inner = known_inner[...]
    else:
        inner = dot(adjacency[inside, :], next_states[inside, :])
    for block in range(rows // size):
        start = block * size
        summed = inner[start : start + size]
        if block == 0 and not own_first:
            summed = summed + dot(near[:, pl.ds(2 * width, size)], next_states[pl.ds(0, size), :])
        if block == rows // size - 1:
            summed = summed + dot(far_tile, next_states[last, :])
        before = next_states[pl.ds(size + start, size), :]
        after = layer(summed.astype(BF16), last_weight[...], last_gain, before)
        weighted = after.astype(F32) * head_row[...]
        folded = weighted[:, :size]
        for at in range(size, width, size):
            folded = folded + weighted[:, at : at + size]
        outcome[:, placed(block, rows // size, shard, size)] = jnp.sum(folded.T, axis=0, keepdims=True)


def paired(features, labels, label_table, tiles, tile_rows, tile_cols, tile_live, weights, gains, head_weight):
    shard_count = lax.axis_size("shard")
    groups, rows, width = features.shape
    _, slots, size, _ = tiles.shape
    depth = weights.shape[1]
    kept = depth // 2
    classes = label_table.shape[0]
    message = jax.ShapeDtypeStruct((size, 2 * width + size), BF16)
    vmem = pl.BlockSpec(memory_space=pltpu.VMEM)
    hbm = pl.BlockSpec(memory_space=pltpu.HBM)
    table_rows = -(-3 * classes // PAD) * PAD

    far, far_sum, near, crossing, state, adjacency = pl.pallas_call(
        first_kernel,
        out_shape=(
            jax.ShapeDtypeStruct((size, width + size), BF16),
            jax.ShapeDtypeStruct((size, width), BF16),
            message,
            jax.ShapeDtypeStruct((kept + EXTRA, width), BF16),
            jax.ShapeDtypeStruct((rows, width), BF16),
            jax.ShapeDtypeStruct((rows + 2 * size, rows), BF16),
        ),
        in_specs=[hbm] * 9,
        out_specs=(vmem,) * 6,
        scratch_shapes=[
            pltpu.SMEM((groups, slots), jnp.int32),
            pltpu.SMEM((groups, slots), jnp.int32),
            pltpu.SMEM((1, groups), jnp.int32),
            pltpu.VMEM((groups, rows), jnp.int32),
            pltpu.VMEM((classes, width), F32),
            pltpu.VMEM((slots, size, size), BF16),
            pltpu.VMEM((rows, width), BF16),
            pltpu.VMEM((1, width), BF16),
            pltpu.VMEM((table_rows, width), F32),
            pltpu.VMEM((rows + 2 * size, rows), F32),
            pltpu.SemaphoreType.DMA((7 + 2 * (rows // size),)),
        ],
        compiler_params=pltpu.CompilerParams(vmem_limit_bytes=16 * 2**20),
        name="messages",
    )(*in_hbm(tile_rows, tile_cols, tile_live.T, labels, label_table, tiles, features, gains, weights))

    beside = [(i, i ^ 1) for i in range(shard_count)]
    apart = [(i, (i + 1) % shard_count) for i in range(1, shard_count, 2)]
    apart += [(b, a) for a, b in apart]
    across = [(0, 1), (1, 0)]
    crossed = lax.ppermute(crossing, "section", across)
    far = lax.ppermute(far, "shard", apart)
    far_sum = lax.ppermute(far_sum, "shard", [pair for pair in apart if abs(pair[0] - pair[1]) == 1])
    near = lax.ppermute(near, "shard", beside)

    aggregate, own_weight, half_gain, head_row = pl.pallas_call(
        waiting_kernel,
        out_shape=(
            jax.ShapeDtypeStruct((rows + 2 * size, width), F32),
            jax.ShapeDtypeStruct((depth, width), BF16),
            jax.ShapeDtypeStruct((1, width), F32),
            jax.ShapeDtypeStruct((1, width), F32),
        ),
        in_specs=[vmem] * 2 + [hbm] * 3,
        out_specs=(vmem,) * 4,
        scratch_shapes=[
            pltpu.VMEM((1, width), BF16),
            pltpu.SemaphoreType.DMA((3,)),
        ],
        compiler_params=pltpu.CompilerParams(vmem_limit_bytes=16 * 2**20),
        cost_estimate=pl.CostEstimate(flops=15 * 10**8, bytes_accessed=2**20, transcendentals=0),
        name="waiting",
    )(adjacency, state, *in_hbm(head_weight.reshape(1, width), gains, weights))

    near_blocks = pl.pallas_call(
        near_kernel,
        out_shape=jax.ShapeDtypeStruct((2 * size, width), BF16),
        in_specs=[vmem] * 5,
        out_specs=vmem,
        compiler_params=pltpu.CompilerParams(vmem_limit_bytes=16 * 2**20),
        name="beside",
    )(near, aggregate, state, own_weight, half_gain)

    crossed, near_blocks = lax.optimization_barrier((crossed, near_blocks))
    relayed = lax.ppermute(crossed, "shard", beside)

    far_blocks, inner = pl.pallas_call(
        far_kernel,
        out_shape=(
            jax.ShapeDtypeStruct((rows - size, width), BF16),
            jax.ShapeDtypeStruct((rows, width), F32),
        ),
        in_specs=[vmem] * 8,
        out_specs=(vmem,) * 2,
        scratch_shapes=[pltpu.VMEM((rows, width), BF16)],
        compiler_params=pltpu.CompilerParams(vmem_limit_bytes=16 * 2**20),
        cost_estimate=pl.CostEstimate(flops=4 * 10**9, bytes_accessed=2**20, transcendentals=0),
        name="apart",
    )(far, near, near_blocks, aggregate, adjacency, state, own_weight, half_gain)

    return pl.pallas_call(
        second_kernel,
        out_shape=jax.ShapeDtypeStruct((1, rows), F32),
        in_specs=[vmem] * 14,
        out_specs=vmem,
        scratch_shapes=[
            pltpu.VMEM((depth, width), BF16),
            pltpu.VMEM((rows + 2 * size, width), BF16),
        ],
        compiler_params=pltpu.CompilerParams(vmem_limit_bytes=32 * 2**20),
        name="layers",
    )(
        adjacency, state, far, far_sum, near, crossed, relayed, near_blocks, far_blocks, inner, aggregate,
        own_weight, half_gain, head_row,
    )


def extended_2(block, sides, width):
    for axis, dim in sides:
        count = lax.axis_size(axis)
        forward = [(i, i + 1) for i in range(count - 1)]
        backward = [(target, source) for source, target in forward]
        low = lax.ppermute(
            lax.slice_in_dim(block, block.shape[dim] - width, None, axis=dim), axis, forward
        )
        high = lax.ppermute(lax.slice_in_dim(block, 0, width, axis=dim), axis, backward)
        block = jnp.concatenate([low, block, high], axis=dim)
    return block


def body(
    features,
    labels,
    label_table,
    tiles,
    tile_rows,
    tile_cols,
    tile_live,
    weights,
    gains,
    head_weight,
):
    section_count = lax.axis_size("section")
    section_index = lax.axis_index("section")
    shard_index = lax.axis_index("shard")
    batch_count = features.shape[0]
    row_count = features.shape[1]
    feature_width = features.shape[2]
    tile_size = tiles.shape[2]
    slot_count = tiles.shape[1]
    label_count = label_table.shape[0]
    per_rows = row_count // tile_size
    per_section = batch_count // section_count
    slot_ids = jnp.arange(slot_count, dtype=jnp.int32)
    place_ids = jnp.arange(per_rows + 2, dtype=jnp.int32)

    def apply_layer(state, parts, layer_weight, layer_gain):
        group_tiles, col_local, placing, from_below, from_above = parts
        block_view = state.reshape(per_rows, tile_size, feature_width)
        chosen_blocks = jnp.take(block_view, col_local, axis=0)
        products = jnp.einsum(
            "kab,kbd->kad", group_tiles, chosen_blocks, preferred_element_type=jnp.float32
        )
        partial_value = jnp.einsum(
            "kp,kad->pad", placing, products, precision=lax.Precision.HIGHEST
        )
        edge_states = jnp.concatenate([state[:tile_size], state[row_count - tile_size :]], axis=0)
        extended = extended_2(edge_states, (("shard", 0),), tile_size)
        below_block = extended[:tile_size].astype(jnp.float32)
        above_block = extended[extended.shape[0] - tile_size :].astype(jnp.float32)
        own_rows = partial_value.reshape(row_count, feature_width)
        own_rows = own_rows.at[:tile_size].add(
            jnp.dot(from_below, below_block, precision=lax.Precision.HIGHEST)
        )
        own_rows = own_rows.at[row_count - tile_size :].add(
            jnp.dot(from_above, above_block, precision=lax.Precision.HIGHEST)
        )
        aggregate = own_rows.astype(jnp.bfloat16)
        projected = jnp.dot(aggregate, layer_weight, preferred_element_type=jnp.float32)
        scale = lax.rsqrt(jnp.mean(projected * projected, axis=-1, keepdims=True) + 1e-06)
        normed = projected * scale * layer_gain.astype(jnp.float32)
        return (state.astype(jnp.float32) + jax.nn.gelu(normed)).astype(jnp.bfloat16)

    layer_mats, layer_gains = (
        lax.all_gather(weights, "section", axis=0, tiled=True),
        lax.all_gather(gains, "section", axis=0, tiled=True),
    )
    batch_index = section_index * per_section + 0
    group_tiles = lax.dynamic_index_in_dim(tiles, batch_index, 0, keepdims=False)
    group_rows = lax.dynamic_index_in_dim(tile_rows, batch_index, 0, keepdims=False)
    group_cols = lax.dynamic_index_in_dim(tile_cols, batch_index, 0, keepdims=False)
    group_live = lax.dynamic_index_in_dim(tile_live, batch_index, 0, keepdims=False)
    col_local = group_cols - shard_index * per_rows
    slot_local = group_rows - (shard_index * per_rows - 1)
    live_mask = (slot_ids < group_live[0]).astype(jnp.float32)
    placing = (slot_local[:, None] == place_ids[None, :]).astype(jnp.float32) * live_mask[:, None]
    edge_pick = jnp.stack([placing[:, 0], placing[:, per_rows + 1]], axis=1)
    edge_tiles = jnp.einsum(
        "kp,kab->pab", edge_pick, group_tiles.astype(jnp.float32), precision=lax.Precision.HIGHEST
    )
    received = extended_2(edge_tiles, (("shard", 0),), 1)
    parts = (group_tiles, col_local, placing[:, 1 : per_rows + 1], received[0], received[3])

    def through(layer_index, state):
        return apply_layer(state, parts, layer_mats[layer_index], layer_gains[layer_index])

    group_labels = lax.dynamic_index_in_dim(labels, batch_index, 0, keepdims=False)
    group_features = lax.dynamic_index_in_dim(features, batch_index, 0, keepdims=False)
    labels_hot = (
        group_labels[:, None] == jnp.arange(label_count, dtype=jnp.int32)[None, :]
    ).astype(jnp.float32)
    embedded = jnp.dot(labels_hot, label_table, precision=lax.Precision.HIGHEST)
    state = lax.fori_loop(
        0,
        section_count,
        through,
        (group_features.astype(jnp.float32) + embedded).astype(jnp.bfloat16),
    )
    results = [jnp.dot(state.astype(jnp.float32), head_weight, precision=lax.Precision.HIGHEST)]
    return jnp.stack(results)


def solution(mesh):
    return jax.shard_map(
        paired if mesh.shape["section"] == 2 else body,
        mesh=mesh,
        in_specs=(
            P(None, "shard", None),
            P(None, "shard"),
            P(),
            P(None, "shard", None, None),
            P(None, "shard"),
            P(None, "shard"),
            P(None, "shard"),
            P("section", None, None),
            P("section", None),
            P(),
        ),
        out_specs=P("section", "shard"),
        check_vma=False,
    )
```

```python
import jax
import jax.numpy as jnp
from jax import lax
from jax.experimental import pallas as pl
from jax.experimental.pallas import tpu as pltpu
from jax.sharding import PartitionSpec as P

BF16 = jnp.bfloat16
F32 = jnp.float32
PAD = 16
EXTRA = 8
GELU_LINEAR = 2.0 * (2.0 / 3.141592653589793) ** 0.5
GELU_CUBIC = 4.0 * GELU_LINEAR * 0.044715


def split3(value):
    high = value.astype(BF16).astype(F32)
    rest = value - high
    mid = rest.astype(BF16).astype(F32)
    return high, mid, rest - mid


def dot(a, b, dims=((1,), (0,))):
    return lax.dot_general(a, b, (dims, ((), ())), preferred_element_type=F32)


def in_hbm(*arrays):
    return [pltpu.with_memory_space_constraint(array, pltpu.HBM) for array in arrays]


def layer(aggregate, weight, half_gain, state):
    projected = dot(aggregate, weight)
    scale = lax.rsqrt(jnp.mean(projected * projected, axis=-1, keepdims=True) + 1e-06)
    half = (projected * scale * half_gain).astype(BF16)
    inner = half * (BF16(GELU_LINEAR) + BF16(GELU_CUBIC) * (half * half))
    return state + (half + half * jnp.tanh(inner))


def placed(block, blocks, shard, size):
    mirrored = 1 - lax.rem(shard, 2)
    return pl.ds(pl.multiple_of((block + mirrored * (blocks - 1 - 2 * block)) * size, size), size)


def first_kernel(
    tile_rows, tile_cols, tile_live, labels, label_table, tiles, features, gains, weights,
    far, far_sum, near, near_sum, crossing, state_out, adjacency_out,
    rows_buf, cols_buf, live_buf, labels_buf, classes_buf, tiles_buf, features_buf, gains_buf, table_buf, sums, sems,
):
    section = lax.axis_index("section")
    shard = lax.axis_index("shard")
    rows, width = features_buf.shape
    slots, size, _ = tiles_buf.shape
    blocks = rows // size
    kept = crossing.shape[0] - EXTRA
    group = section

    small = [(tile_rows, rows_buf), (tile_cols, cols_buf), (tile_live, live_buf)]
    named = [(label_table, classes_buf)]
    spread = []
    for block in range(blocks):
        span, place = pl.ds(block * size, size), placed(block, blocks, shard, size)
        named.append((labels.at[:, span], labels_buf.at[:, place]))
        spread.append((features.at[group, span], features_buf.at[place]))
    half = pl.ds(pl.multiple_of(lax.rem(shard, 2) * kept, kept), kept)
    sent = [(gains, gains_buf), (weights.at[0, half], crossing.at[pl.ds(0, kept)])]
    batches, count = [], 0
    for batch in (small, named, [(tiles.at[group], tiles_buf)], spread, sent):
        batches.append([
            pltpu.make_async_copy(source, target, sems.at[count + index])
            for index, (source, target) in enumerate(batch)
        ])
        count += len(batch)
    for batch in batches:
        for copy in batch:
            copy.start()
    sums[...] = jnp.zeros_like(sums)
    table_buf[...] = jnp.zeros_like(table_buf)

    for copy in batches[1]:
        copy.wait()
    classes = classes_buf.shape[0]
    for part, value in enumerate(split3(classes_buf[...])):
        table_buf[pl.ds(part * classes, classes), :] = value
    depth = table_buf.shape[0]
    index = lax.broadcasted_iota(jnp.int32, (depth, rows), 0)
    wanted = jnp.where(
        index < classes, index,
        jnp.where(index < 2 * classes, index - classes, jnp.where(index < 3 * classes, index - 2 * classes, -1)),
    )
    hot = (wanted == labels_buf[pl.ds(group, 1), :]).astype(F32).astype(BF16)
    embedded = dot(hot, table_buf[...].astype(BF16), ((0,), (0,)))

    for copy in batches[0] + batches[2]:
        copy.wait()
    for slot in range(slots):
        @pl.when(slot < live_buf[0, group])
        def _():
            row = rows_buf[group, slot] - (shard * blocks - 1)
            col = cols_buf[group, slot] - shard * blocks
            sums[placed(row, blocks + 2, shard, size), placed(col, blocks, shard, size)] += tiles_buf[slot].astype(F32)
    adjacency = sums[...].astype(BF16)
    adjacency_out[...] = adjacency

    for copy in batches[3]:
        copy.wait()
    state = (features_buf[...].astype(F32) + embedded).astype(BF16)
    state_out[...] = state
    partial = dot(adjacency[size : size + rows], state).astype(BF16)
    near_sum[...] = partial[:size]
    near[:, pl.ds(0, width)] = state[:size]
    near[:, pl.ds(width, size)] = adjacency[:size, :size]
    far_sum[...] = partial[rows - size :]
    far[:, pl.ds(0, width)] = state[rows - size :]
    far[:, pl.ds(width, size)] = adjacency[rows + size :, rows - size :]
    batches[4][0].wait()
    crossing[pl.ds(kept, EXTRA), :] = jnp.broadcast_to(gains_buf[...].astype(F32), (EXTRA, width)).astype(BF16)
    batches[4][1].wait()


def waiting_kernel(
    adjacency, state, head, gains, weights,
    aggregate, weight, half_gain, head_row,
    gains_buf, sems,
):
    copies = [
        pltpu.make_async_copy(source, target, sems.at[index])
        for index, (source, target) in enumerate(((weights.at[0], weight), (head, head_row), (gains, gains_buf)))
    ]
    for copy in copies:
        copy.start()
    aggregate[...] = dot(adjacency[...], state[...])
    copies[2].wait()
    half_gain[...] = 0.5 * gains_buf[...].astype(F32)
    copies[0].wait()
    copies[1].wait()


def near_kernel(near, near_sum, aggregate, state, weight, half_gain, near_blocks):
    size, width = near.shape[0], aggregate.shape[1]
    near_state = near[:, pl.ds(0, width)]
    first, second = pl.ds(0, size), pl.ds(size, size)
    near_blocks[first, :] = (aggregate[first, :] + near_sum[...].astype(F32)).astype(BF16)
    near_blocks[second, :] = (aggregate[second, :] + dot(near[:, pl.ds(width, size)], near_state)).astype(BF16)

    @pl.when(lax.axis_index("section") == 0)
    def _():
        for span, before in ((first, near_state), (second, state[pl.ds(0, size), :])):
            near_blocks[span, :] = layer(near_blocks[span, :], weight[...], half_gain[...], before)


def far_kernel(far, near, near_blocks, aggregate, adjacency, state, weight, half_gain, far_blocks, inner, states):
    size = far.shape[0]
    rows, width = state.shape
    for start in range(0, rows - 2 * size, size):
        far_blocks[pl.ds(start, size), :] = aggregate[pl.ds(2 * size + start, size), :].astype(BF16)
    far_blocks[pl.ds(rows - 2 * size, size), :] = (
        aggregate[pl.ds(rows, size), :] + dot(far[:, pl.ds(width, size)], far[:, pl.ds(0, width)])
    ).astype(BF16)

    @pl.when(lax.axis_index("section") == 0)
    def _():
        for start in range(0, rows - size, size):
            span = pl.ds(start, size)
            far_blocks[span, :] = layer(
                far_blocks[span, :], weight[...], half_gain[...], state[pl.ds(size + start, size), :]
            )
        states[pl.ds(0, size), :] = near_blocks[pl.ds(size, size), :]
        states[pl.ds(size, rows - size), :] = far_blocks[...]
        inner[...] = dot(adjacency[pl.ds(size, rows), :], states[...])
        inner[pl.ds(0, size), :] += dot(near[:, pl.ds(width, size)], near_blocks[pl.ds(0, size), :])


def second_kernel(*refs):
    first = lax.axis_index("section") == 0

    @pl.when(first)
    def _():
        both_layers(True, *refs)

    @pl.when(jnp.logical_not(first))
    def _():
        both_layers(False, *refs)


def both_layers(
    own_first,
    adjacency, state, far, far_sum, near, crossed, relayed, near_blocks, far_blocks, known_inner, aggregate,
    own_weight, half_gain, head_row,
    outcome,
    got_weight, next_states,
):
    shard = lax.axis_index("shard")
    even = lax.rem(shard, 2) == 0
    rows, width = state.shape
    size = near.shape[0]
    kept = crossed.shape[0] - EXTRA
    inside, last = pl.ds(size, rows), pl.ds(size + rows, size)

    for place, (one, two) in enumerate(((crossed, relayed), (relayed, crossed))):
        got_weight[pl.ds(place * kept, kept), :] = jnp.where(even, one[pl.ds(0, kept), :], two[pl.ds(0, kept), :])
    got_gain = 0.5 * crossed[pl.ds(kept, EXTRA), :].astype(F32)[0:1]
    used = ((own_weight, half_gain[...]), (got_weight, got_gain))
    (weight, gain), (last_weight, last_gain) = used if own_first else used[::-1]
    far_tile = far[:, pl.ds(width, size)]
    halo = (aggregate[last, :] + far_sum[...].astype(F32)).astype(BF16)

    if own_first:
        next_states[pl.ds(0, 2 * size), :] = near_blocks[...]
        next_states[pl.ds(2 * size, rows - size), :] = far_blocks[...]
    else:
        for start in range(0, rows, size):
            span = pl.ds(start, size)
            source = near_blocks[pl.ds(size, size), :] if start == 0 else far_blocks[pl.ds(start - size, size), :]
            next_states[pl.ds(size + start, size), :] = layer(source, weight[...], gain, state[span, :])
        next_states[pl.ds(0, size), :] = layer(
            near_blocks[pl.ds(0, size), :], weight[...], gain, near[:, pl.ds(0, width)]
        )
    next_states[last, :] = layer(halo, weight[...], gain, far[:, pl.ds(0, width)])

    if own_first:
        inner = known_inner[...]
    else:
        inner = dot(adjacency[inside, :], next_states[inside, :])
    for block in range(rows // size):
        start = block * size
        summed = inner[start : start + size]
        if block == 0 and not own_first:
            summed = summed + dot(near[:, pl.ds(width, size)], next_states[pl.ds(0, size), :])
        if block == rows // size - 1:
            summed = summed + dot(far_tile, next_states[last, :])
        before = next_states[pl.ds(size + start, size), :]
        after = layer(summed.astype(BF16), last_weight[...], last_gain, before)
        weighted = after.astype(F32) * head_row[...]
        folded = weighted[:, :size]
        for at in range(size, width, size):
            folded = folded + weighted[:, at : at + size]
        outcome[:, placed(block, rows // size, shard, size)] = jnp.sum(folded.T, axis=0, keepdims=True)


def paired(features, labels, label_table, tiles, tile_rows, tile_cols, tile_live, weights, gains, head_weight):
    shard_count = lax.axis_size("shard")
    groups, rows, width = features.shape
    _, slots, size, _ = tiles.shape
    depth = weights.shape[1]
    kept = depth // 2
    classes = label_table.shape[0]
    vmem = pl.BlockSpec(memory_space=pltpu.VMEM)
    hbm = pl.BlockSpec(memory_space=pltpu.HBM)
    table_rows = -(-3 * classes // PAD) * PAD

    far, far_sum, near, near_sum, crossing, state, adjacency = pl.pallas_call(
        first_kernel,
        out_shape=(
            jax.ShapeDtypeStruct((size, width + size), BF16),
            jax.ShapeDtypeStruct((size, width), BF16),
            jax.ShapeDtypeStruct((size, width + size), BF16),
            jax.ShapeDtypeStruct((size, width), BF16),
            jax.ShapeDtypeStruct((kept + EXTRA, width), BF16),
            jax.ShapeDtypeStruct((rows, width), BF16),
            jax.ShapeDtypeStruct((rows + 2 * size, rows), BF16),
        ),
        in_specs=[hbm] * 9,
        out_specs=(vmem,) * 7,
        scratch_shapes=[
            pltpu.SMEM((groups, slots), jnp.int32),
            pltpu.SMEM((groups, slots), jnp.int32),
            pltpu.SMEM((1, groups), jnp.int32),
            pltpu.VMEM((groups, rows), jnp.int32),
            pltpu.VMEM((classes, width), F32),
            pltpu.VMEM((slots, size, size), BF16),
            pltpu.VMEM((rows, width), BF16),
            pltpu.VMEM((1, width), BF16),
            pltpu.VMEM((table_rows, width), F32),
            pltpu.VMEM((rows + 2 * size, rows), F32),
            pltpu.SemaphoreType.DMA((7 + 2 * (rows // size),)),
        ],
        compiler_params=pltpu.CompilerParams(vmem_limit_bytes=16 * 2**20),
        name="messages",
    )(*in_hbm(tile_rows, tile_cols, tile_live.T, labels, label_table, tiles, features, gains, weights))

    beside = [(i, i ^ 1) for i in range(shard_count)]
    apart = [(i, (i + 1) % shard_count) for i in range(1, shard_count, 2)]
    apart += [(b, a) for a, b in apart]
    across = [(0, 1), (1, 0)]
    crossed = lax.ppermute(crossing, "section", across)
    far = lax.ppermute(far, "shard", apart)
    far_sum = lax.ppermute(far_sum, "shard", [pair for pair in apart if abs(pair[0] - pair[1]) == 1])
    near = lax.ppermute(near, "shard", beside)
    near_sum = lax.ppermute(near_sum, "shard", beside)

    aggregate, own_weight, half_gain, head_row = pl.pallas_call(
        waiting_kernel,
        out_shape=(
            jax.ShapeDtypeStruct((rows + 2 * size, width), F32),
            jax.ShapeDtypeStruct((depth, width), BF16),
            jax.ShapeDtypeStruct((1, width), F32),
            jax.ShapeDtypeStruct((1, width), F32),
        ),
        in_specs=[vmem] * 2 + [hbm] * 3,
        out_specs=(vmem,) * 4,
        scratch_shapes=[
            pltpu.VMEM((1, width), BF16),
            pltpu.SemaphoreType.DMA((3,)),
        ],
        compiler_params=pltpu.CompilerParams(vmem_limit_bytes=16 * 2**20),
        cost_estimate=pl.CostEstimate(flops=15 * 10**8, bytes_accessed=2**20, transcendentals=0),
        name="waiting",
    )(adjacency, state, *in_hbm(head_weight.reshape(1, width), gains, weights))

    near_blocks = pl.pallas_call(
        near_kernel,
        out_shape=jax.ShapeDtypeStruct((2 * size, width), BF16),
        in_specs=[vmem] * 6,
        out_specs=vmem,
        compiler_params=pltpu.CompilerParams(vmem_limit_bytes=16 * 2**20),
        name="beside",
    )(near, near_sum, aggregate, state, own_weight, half_gain)

    crossed, aggregate = lax.optimization_barrier((crossed, aggregate))
    relayed = lax.ppermute(crossed, "shard", beside)

    far_blocks, inner = pl.pallas_call(
        far_kernel,
        out_shape=(
            jax.ShapeDtypeStruct((rows - size, width), BF16),
            jax.ShapeDtypeStruct((rows, width), F32),
        ),
        in_specs=[vmem] * 8,
        out_specs=(vmem,) * 2,
        scratch_shapes=[pltpu.VMEM((rows, width), BF16)],
        compiler_params=pltpu.CompilerParams(vmem_limit_bytes=16 * 2**20),
        cost_estimate=pl.CostEstimate(flops=4 * 10**9, bytes_accessed=2**20, transcendentals=0),
        name="apart",
    )(far, near, near_blocks, aggregate, adjacency, state, own_weight, half_gain)

    return pl.pallas_call(
        second_kernel,
        out_shape=jax.ShapeDtypeStruct((1, rows), F32),
        in_specs=[vmem] * 14,
        out_specs=vmem,
        scratch_shapes=[
            pltpu.VMEM((depth, width), BF16),
            pltpu.VMEM((rows + 2 * size, width), BF16),
        ],
        compiler_params=pltpu.CompilerParams(vmem_limit_bytes=32 * 2**20),
        name="layers",
    )(
        adjacency, state, far, far_sum, near, crossed, relayed, near_blocks, far_blocks, inner, aggregate,
        own_weight, half_gain, head_row,
    )


def extended_2(block, sides, width):
    for axis, dim in sides:
        count = lax.axis_size(axis)
        forward = [(i, i + 1) for i in range(count - 1)]
        backward = [(target, source) for source, target in forward]
        low = lax.ppermute(
            lax.slice_in_dim(block, block.shape[dim] - width, None, axis=dim), axis, forward
        )
        high = lax.ppermute(lax.slice_in_dim(block, 0, width, axis=dim), axis, backward)
        block = jnp.concatenate([low, block, high], axis=dim)
    return block


def body(
    features,
    labels,
    label_table,
    tiles,
    tile_rows,
    tile_cols,
    tile_live,
    weights,
    gains,
    head_weight,
):
    section_count = lax.axis_size("section")
    section_index = lax.axis_index("section")
    shard_index = lax.axis_index("shard")
    batch_count = features.shape[0]
    row_count = features.shape[1]
    feature_width = features.shape[2]
    tile_size = tiles.shape[2]
    slot_count = tiles.shape[1]
    label_count = label_table.shape[0]
    per_rows = row_count // tile_size
    per_section = batch_count // section_count
    slot_ids = jnp.arange(slot_count, dtype=jnp.int32)
    place_ids = jnp.arange(per_rows + 2, dtype=jnp.int32)

    def apply_layer(state, parts, layer_weight, layer_gain):
        group_tiles, col_local, placing, from_below, from_above = parts
        block_view = state.reshape(per_rows, tile_size, feature_width)
        chosen_blocks = jnp.take(block_view, col_local, axis=0)
        products = jnp.einsum(
            "kab,kbd->kad", group_tiles, chosen_blocks, preferred_element_type=jnp.float32
        )
        partial_value = jnp.einsum(
            "kp,kad->pad", placing, products, precision=lax.Precision.HIGHEST
        )
        edge_states = jnp.concatenate([state[:tile_size], state[row_count - tile_size :]], axis=0)
        extended = extended_2(edge_states, (("shard", 0),), tile_size)
        below_block = extended[:tile_size].astype(jnp.float32)
        above_block = extended[extended.shape[0] - tile_size :].astype(jnp.float32)
        own_rows = partial_value.reshape(row_count, feature_width)
        own_rows = own_rows.at[:tile_size].add(
            jnp.dot(from_below, below_block, precision=lax.Precision.HIGHEST)
        )
        own_rows = own_rows.at[row_count - tile_size :].add(
            jnp.dot(from_above, above_block, precision=lax.Precision.HIGHEST)
        )
        aggregate = own_rows.astype(jnp.bfloat16)
        projected = jnp.dot(aggregate, layer_weight, preferred_element_type=jnp.float32)
        scale = lax.rsqrt(jnp.mean(projected * projected, axis=-1, keepdims=True) + 1e-06)
        normed = projected * scale * layer_gain.astype(jnp.float32)
        return (state.astype(jnp.float32) + jax.nn.gelu(normed)).astype(jnp.bfloat16)

    layer_mats, layer_gains = (
        lax.all_gather(weights, "section", axis=0, tiled=True),
        lax.all_gather(gains, "section", axis=0, tiled=True),
    )
    batch_index = section_index * per_section + 0
    group_tiles = lax.dynamic_index_in_dim(tiles, batch_index, 0, keepdims=False)
    group_rows = lax.dynamic_index_in_dim(tile_rows, batch_index, 0, keepdims=False)
    group_cols = lax.dynamic_index_in_dim(tile_cols, batch_index, 0, keepdims=False)
    group_live = lax.dynamic_index_in_dim(tile_live, batch_index, 0, keepdims=False)
    col_local = group_cols - shard_index * per_rows
    slot_local = group_rows - (shard_index * per_rows - 1)
    live_mask = (slot_ids < group_live[0]).astype(jnp.float32)
    placing = (slot_local[:, None] == place_ids[None, :]).astype(jnp.float32) * live_mask[:, None]
    edge_pick = jnp.stack([placing[:, 0], placing[:, per_rows + 1]], axis=1)
    edge_tiles = jnp.einsum(
        "kp,kab->pab", edge_pick, group_tiles.astype(jnp.float32), precision=lax.Precision.HIGHEST
    )
    received = extended_2(edge_tiles, (("shard", 0),), 1)
    parts = (group_tiles, col_local, placing[:, 1 : per_rows + 1], received[0], received[3])

    def through(layer_index, state):
        return apply_layer(state, parts, layer_mats[layer_index], layer_gains[layer_index])

    group_labels = lax.dynamic_index_in_dim(labels, batch_index, 0, keepdims=False)
    group_features = lax.dynamic_index_in_dim(features, batch_index, 0, keepdims=False)
    labels_hot = (
        group_labels[:, None] == jnp.arange(label_count, dtype=jnp.int32)[None, :]
    ).astype(jnp.float32)
    embedded = jnp.dot(labels_hot, label_table, precision=lax.Precision.HIGHEST)
    state = lax.fori_loop(
        0,
        section_count,
        through,
        (group_features.astype(jnp.float32) + embedded).astype(jnp.bfloat16),
    )
    results = [jnp.dot(state.astype(jnp.float32), head_weight, precision=lax.Precision.HIGHEST)]
    return jnp.stack(results)


def solution(mesh):
    return jax.shard_map(
        paired if mesh.shape["section"] == 2 else body,
        mesh=mesh,
        in_specs=(
            P(None, "shard", None),
            P(None, "shard"),
            P(),
            P(None, "shard", None, None),
            P(None, "shard"),
            P(None, "shard"),
            P(None, "shard"),
            P("section", None, None),
            P("section", None),
            P(),
        ),
        out_specs=P("section", "shard"),
        check_vma=False,
    )
```

```python
import jax
import jax.numpy as jnp
from jax import lax
from jax.experimental import pallas as pl
from jax.experimental.pallas import tpu as pltpu
from jax.sharding import PartitionSpec as P

BF16 = jnp.bfloat16
F32 = jnp.float32
PAD = 16
EXTRA = 8
GELU_LINEAR = 2.0 * (2.0 / 3.141592653589793) ** 0.5
GELU_CUBIC = 4.0 * GELU_LINEAR * 0.044715


def split3(value):
    high = value.astype(BF16).astype(F32)
    rest = value - high
    mid = rest.astype(BF16).astype(F32)
    return high, mid, rest - mid


def dot(a, b, dims=((1,), (0,))):
    return lax.dot_general(a, b, (dims, ((), ())), preferred_element_type=F32)


def in_hbm(*arrays):
    return [pltpu.with_memory_space_constraint(array, pltpu.HBM) for array in arrays]


def layer(aggregate, weight, half_gain, state):
    projected = dot(aggregate, weight)
    scale = lax.rsqrt(jnp.mean(projected * projected, axis=-1, keepdims=True) + 1e-06)
    half = (projected * scale * half_gain).astype(BF16)
    inner = half * (BF16(GELU_LINEAR) + BF16(GELU_CUBIC) * (half * half))
    return state + (half + half * jnp.tanh(inner))


def placed(block, blocks, shard, size):
    mirrored = 1 - lax.rem(shard, 2)
    return pl.ds(pl.multiple_of((block + mirrored * (blocks - 1 - 2 * block)) * size, size), size)


def first_kernel(
    tile_rows, tile_cols, tile_live, labels, label_table, tiles, features, gains, weights,
    far, far_sum, near, near_sum, crossing, state_out, adjacency_out,
    rows_buf, cols_buf, live_buf, labels_buf, classes_buf, tiles_buf, features_buf, gains_buf, table_buf, sums, sems,
):
    section = lax.axis_index("section")
    shard = lax.axis_index("shard")
    rows, width = features_buf.shape
    slots, size, _ = tiles_buf.shape
    blocks = rows // size
    kept = crossing.shape[0] - EXTRA
    group = section

    small = [(tile_rows, rows_buf), (tile_cols, cols_buf), (tile_live, live_buf)]
    named = [(label_table, classes_buf)]
    spread = []
    for block in range(blocks):
        span, place = pl.ds(block * size, size), placed(block, blocks, shard, size)
        named.append((labels.at[:, span], labels_buf.at[:, place]))
        spread.append((features.at[group, span], features_buf.at[place]))
    half = pl.ds(pl.multiple_of(lax.rem(shard, 2) * kept, kept), kept)
    sent = [(gains, gains_buf), (weights.at[0, half], crossing.at[pl.ds(0, kept)])]
    batches, count = [], 0
    for batch in (small, named, [(tiles.at[group], tiles_buf)], spread, sent):
        batches.append([
            pltpu.make_async_copy(source, target, sems.at[count + index])
            for index, (source, target) in enumerate(batch)
        ])
        count += len(batch)
    for batch in batches:
        for copy in batch:
            copy.start()
    sums[...] = jnp.zeros_like(sums)
    table_buf[...] = jnp.zeros_like(table_buf)

    for copy in batches[1]:
        copy.wait()
    classes = classes_buf.shape[0]
    for part, value in enumerate(split3(classes_buf[...])):
        table_buf[pl.ds(part * classes, classes), :] = value
    depth = table_buf.shape[0]
    index = lax.broadcasted_iota(jnp.int32, (depth, rows), 0)
    wanted = jnp.where(
        index < classes, index,
        jnp.where(index < 2 * classes, index - classes, jnp.where(index < 3 * classes, index - 2 * classes, -1)),
    )
    hot = (wanted == labels_buf[pl.ds(group, 1), :]).astype(F32).astype(BF16)
    embedded = dot(hot, table_buf[...].astype(BF16), ((0,), (0,)))

    for copy in batches[0] + batches[2]:
        copy.wait()
    for slot in range(slots):
        @pl.when(slot < live_buf[0, group])
        def _():
            row = rows_buf[group, slot] - (shard * blocks - 1)
            col = cols_buf[group, slot] - shard * blocks
            sums[placed(row, blocks + 2, shard, size), placed(col, blocks, shard, size)] += tiles_buf[slot].astype(F32)
    adjacency = sums[...].astype(BF16)
    adjacency_out[...] = adjacency

    for copy in batches[3]:
        copy.wait()
    state = (features_buf[...].astype(F32) + embedded).astype(BF16)
    state_out[...] = state
    partial = dot(adjacency[size : size + rows], state).astype(BF16)
    near_sum[...] = partial[:size]
    near[:, pl.ds(0, width)] = state[:size]
    near[:, pl.ds(width, size)] = adjacency[:size, :size]
    far_sum[...] = partial[rows - size :]
    far[:, pl.ds(0, width)] = state[rows - size :]
    far[:, pl.ds(width, size)] = adjacency[rows + size :, rows - size :]
    batches[4][0].wait()
    crossing[pl.ds(kept, EXTRA), :] = jnp.broadcast_to(gains_buf[...].astype(F32), (EXTRA, width)).astype(BF16)
    batches[4][1].wait()


def waiting_kernel(
    adjacency, state, head, gains, weights,
    aggregate, weight, half_gain, head_row,
    gains_buf, sems,
):
    copies = [
        pltpu.make_async_copy(source, target, sems.at[index])
        for index, (source, target) in enumerate(((weights.at[0], weight), (head, head_row), (gains, gains_buf)))
    ]
    for copy in copies:
        copy.start()
    aggregate[...] = dot(adjacency[...], state[...])
    copies[2].wait()
    half_gain[...] = 0.5 * gains_buf[...].astype(F32)
    copies[0].wait()
    copies[1].wait()


def near_kernel(near, near_sum, aggregate, state, weight, half_gain, near_blocks):
    size, width = near.shape[0], aggregate.shape[1]
    near_state = near[:, pl.ds(0, width)]
    first, second = pl.ds(0, size), pl.ds(size, size)
    near_blocks[first, :] = (aggregate[first, :] + near_sum[...].astype(F32)).astype(BF16)
    near_blocks[second, :] = (aggregate[second, :] + dot(near[:, pl.ds(width, size)], near_state)).astype(BF16)

    @pl.when(lax.axis_index("section") == 0)
    def _():
        for span, before in ((first, near_state), (second, state[pl.ds(0, size), :])):
            near_blocks[span, :] = layer(near_blocks[span, :], weight[...], half_gain[...], before)


def far_kernel(far, near, near_blocks, aggregate, adjacency, state, weight, half_gain, far_blocks, inner, states):
    size = far.shape[0]
    rows, width = state.shape
    for start in range(0, rows - 2 * size, size):
        far_blocks[pl.ds(start, size), :] = aggregate[pl.ds(2 * size + start, size), :].astype(BF16)
    far_blocks[pl.ds(rows - 2 * size, size), :] = (
        aggregate[pl.ds(rows, size), :] + dot(far[:, pl.ds(width, size)], far[:, pl.ds(0, width)])
    ).astype(BF16)

    @pl.when(lax.axis_index("section") == 0)
    def _():
        for start in range(0, rows - size, size):
            span = pl.ds(start, size)
            far_blocks[span, :] = layer(
                far_blocks[span, :], weight[...], half_gain[...], state[pl.ds(size + start, size), :]
            )
        states[pl.ds(0, size), :] = near_blocks[pl.ds(size, size), :]
        states[pl.ds(size, rows - size), :] = far_blocks[...]
        inner[...] = dot(adjacency[pl.ds(size, rows), :], states[...])
        inner[pl.ds(0, size), :] += dot(near[:, pl.ds(width, size)], near_blocks[pl.ds(0, size), :])


def second_kernel(*refs):
    first = lax.axis_index("section") == 0

    @pl.when(first)
    def _():
        both_layers(True, *refs)

    @pl.when(jnp.logical_not(first))
    def _():
        both_layers(False, *refs)


def both_layers(
    own_first,
    adjacency, state, far, far_sum, near, crossed, relayed, near_blocks, far_blocks, known_inner, aggregate,
    own_weight, half_gain, head_row,
    outcome,
    got_weight, next_states,
):
    shard = lax.axis_index("shard")
    even = lax.rem(shard, 2) == 0
    rows, width = state.shape
    size = near.shape[0]
    kept = crossed.shape[0] - EXTRA
    inside, last = pl.ds(size, rows), pl.ds(size + rows, size)

    for place, (one, two) in enumerate(((crossed, relayed), (relayed, crossed))):
        got_weight[pl.ds(place * kept, kept), :] = jnp.where(even, one[pl.ds(0, kept), :], two[pl.ds(0, kept), :])
    got_gain = 0.5 * crossed[pl.ds(kept, EXTRA), :].astype(F32)[0:1]
    used = ((own_weight, half_gain[...]), (got_weight, got_gain))
    (weight, gain), (last_weight, last_gain) = used if own_first else used[::-1]
    far_tile = far[:, pl.ds(width, size)]
    halo = (aggregate[last, :] + far_sum[...].astype(F32)).astype(BF16)

    if own_first:
        next_states[pl.ds(0, 2 * size), :] = near_blocks[...]
        next_states[pl.ds(2 * size, rows - size), :] = far_blocks[...]
    else:
        for start in range(0, rows, size):
            span = pl.ds(start, size)
            source = near_blocks[pl.ds(size, size), :] if start == 0 else far_blocks[pl.ds(start - size, size), :]
            next_states[pl.ds(size + start, size), :] = layer(source, weight[...], gain, state[span, :])
        next_states[pl.ds(0, size), :] = layer(
            near_blocks[pl.ds(0, size), :], weight[...], gain, near[:, pl.ds(0, width)]
        )
    next_states[last, :] = layer(halo, weight[...], gain, far[:, pl.ds(0, width)])

    if own_first:
        inner = known_inner[...]
    else:
        inner = dot(adjacency[inside, :], next_states[inside, :])
    for block in range(rows // size):
        start = block * size
        summed = inner[start : start + size]
        if block == 0 and not own_first:
            summed = summed + dot(near[:, pl.ds(width, size)], next_states[pl.ds(0, size), :])
        if block == rows // size - 1:
            summed = summed + dot(far_tile, next_states[last, :])
        before = next_states[pl.ds(size + start, size), :]
        after = layer(summed.astype(BF16), last_weight[...], last_gain, before)
        weighted = after.astype(F32) * head_row[...]
        folded = weighted[:, :size]
        for at in range(size, width, size):
            folded = folded + weighted[:, at : at + size]
        outcome[:, placed(block, rows // size, shard, size)] = jnp.sum(folded.T, axis=0, keepdims=True)


def paired(features, labels, label_table, tiles, tile_rows, tile_cols, tile_live, weights, gains, head_weight):
    shard_count = lax.axis_size("shard")
    groups, rows, width = features.shape
    _, slots, size, _ = tiles.shape
    depth = weights.shape[1]
    kept = depth // 2
    classes = label_table.shape[0]
    vmem = pl.BlockSpec(memory_space=pltpu.VMEM)
    hbm = pl.BlockSpec(memory_space=pltpu.HBM)
    table_rows = -(-3 * classes // PAD) * PAD

    far, far_sum, near, near_sum, crossing, state, adjacency = pl.pallas_call(
        first_kernel,
        out_shape=(
            jax.ShapeDtypeStruct((size, width + size), BF16),
            jax.ShapeDtypeStruct((size, width), BF16),
            jax.ShapeDtypeStruct((size, width + size), BF16),
            jax.ShapeDtypeStruct((size, width), BF16),
            jax.ShapeDtypeStruct((kept + EXTRA, width), BF16),
            jax.ShapeDtypeStruct((rows, width), BF16),
            jax.ShapeDtypeStruct((rows + 2 * size, rows), BF16),
        ),
        in_specs=[hbm] * 9,
        out_specs=(vmem,) * 7,
        scratch_shapes=[
            pltpu.SMEM((groups, slots), jnp.int32),
            pltpu.SMEM((groups, slots), jnp.int32),
            pltpu.SMEM((1, groups), jnp.int32),
            pltpu.VMEM((groups, rows), jnp.int32),
            pltpu.VMEM((classes, width), F32),
            pltpu.VMEM((slots, size, size), BF16),
            pltpu.VMEM((rows, width), BF16),
            pltpu.VMEM((1, width), BF16),
            pltpu.VMEM((table_rows, width), F32),
            pltpu.VMEM((rows + 2 * size, rows), F32),
            pltpu.SemaphoreType.DMA((7 + 2 * (rows // size),)),
        ],
        compiler_params=pltpu.CompilerParams(vmem_limit_bytes=16 * 2**20),
        name="messages",
    )(*in_hbm(tile_rows, tile_cols, tile_live.T, labels, label_table, tiles, features, gains, weights))

    beside = [(i, i ^ 1) for i in range(shard_count)]
    apart = [(i, (i + 1) % shard_count) for i in range(1, shard_count, 2)]
    apart += [(b, a) for a, b in apart]
    across = [(0, 1), (1, 0)]
    crossed = lax.ppermute(crossing, "section", across)
    far = lax.ppermute(far, "shard", apart)
    far_sum = lax.ppermute(far_sum, "shard", [pair for pair in apart if abs(pair[0] - pair[1]) == 1])
    near = lax.ppermute(near, "shard", beside)
    near_sum = lax.ppermute(near_sum, "shard", beside)

    aggregate, own_weight, half_gain, head_row = pl.pallas_call(
        waiting_kernel,
        out_shape=(
            jax.ShapeDtypeStruct((rows + 2 * size, width), F32),
            jax.ShapeDtypeStruct((depth, width), BF16),
            jax.ShapeDtypeStruct((1, width), F32),
            jax.ShapeDtypeStruct((1, width), F32),
        ),
        in_specs=[vmem] * 2 + [hbm] * 3,
        out_specs=(vmem,) * 4,
        scratch_shapes=[
            pltpu.VMEM((1, width), BF16),
            pltpu.SemaphoreType.DMA((3,)),
        ],
        compiler_params=pltpu.CompilerParams(vmem_limit_bytes=16 * 2**20),
        cost_estimate=pl.CostEstimate(flops=15 * 10**8, bytes_accessed=2**20, transcendentals=0),
        name="waiting",
    )(adjacency, state, *in_hbm(head_weight.reshape(1, width), gains, weights))

    crossed, aggregate, near = lax.optimization_barrier((crossed, aggregate, near))
    near_blocks = pl.pallas_call(
        near_kernel,
        out_shape=jax.ShapeDtypeStruct((2 * size, width), BF16),
        in_specs=[vmem] * 6,
        out_specs=vmem,
        compiler_params=pltpu.CompilerParams(vmem_limit_bytes=16 * 2**20),
        name="beside",
    )(near, near_sum, aggregate, state, own_weight, half_gain)

    relayed = lax.ppermute(crossed, "shard", beside)

    far_blocks, inner = pl.pallas_call(
        far_kernel,
        out_shape=(
            jax.ShapeDtypeStruct((rows - size, width), BF16),
            jax.ShapeDtypeStruct((rows, width), F32),
        ),
        in_specs=[vmem] * 8,
        out_specs=(vmem,) * 2,
        scratch_shapes=[pltpu.VMEM((rows, width), BF16)],
        compiler_params=pltpu.CompilerParams(vmem_limit_bytes=16 * 2**20),
        cost_estimate=pl.CostEstimate(flops=4 * 10**9, bytes_accessed=2**20, transcendentals=0),
        name="apart",
    )(far, near, near_blocks, aggregate, adjacency, state, own_weight, half_gain)

    return pl.pallas_call(
        second_kernel,
        out_shape=jax.ShapeDtypeStruct((1, rows), F32),
        in_specs=[vmem] * 14,
        out_specs=vmem,
        scratch_shapes=[
            pltpu.VMEM((depth, width), BF16),
            pltpu.VMEM((rows + 2 * size, width), BF16),
        ],
        compiler_params=pltpu.CompilerParams(vmem_limit_bytes=32 * 2**20),
        name="layers",
    )(
        adjacency, state, far, far_sum, near, crossed, relayed, near_blocks, far_blocks, inner, aggregate,
        own_weight, half_gain, head_row,
    )


def extended_2(block, sides, width):
    for axis, dim in sides:
        count = lax.axis_size(axis)
        forward = [(i, i + 1) for i in range(count - 1)]
        backward = [(target, source) for source, target in forward]
        low = lax.ppermute(
            lax.slice_in_dim(block, block.shape[dim] - width, None, axis=dim), axis, forward
        )
        high = lax.ppermute(lax.slice_in_dim(block, 0, width, axis=dim), axis, backward)
        block = jnp.concatenate([low, block, high], axis=dim)
    return block


def body(
    features,
    labels,
    label_table,
    tiles,
    tile_rows,
    tile_cols,
    tile_live,
    weights,
    gains,
    head_weight,
):
    section_count = lax.axis_size("section")
    section_index = lax.axis_index("section")
    shard_index = lax.axis_index("shard")
    batch_count = features.shape[0]
    row_count = features.shape[1]
    feature_width = features.shape[2]
    tile_size = tiles.shape[2]
    slot_count = tiles.shape[1]
    label_count = label_table.shape[0]
    per_rows = row_count // tile_size
    per_section = batch_count // section_count
    slot_ids = jnp.arange(slot_count, dtype=jnp.int32)
    place_ids = jnp.arange(per_rows + 2, dtype=jnp.int32)

    def apply_layer(state, parts, layer_weight, layer_gain):
        group_tiles, col_local, placing, from_below, from_above = parts
        block_view = state.reshape(per_rows, tile_size, feature_width)
        chosen_blocks = jnp.take(block_view, col_local, axis=0)
        products = jnp.einsum(
            "kab,kbd->kad", group_tiles, chosen_blocks, preferred_element_type=jnp.float32
        )
        partial_value = jnp.einsum(
            "kp,kad->pad", placing, products, precision=lax.Precision.HIGHEST
        )
        edge_states = jnp.concatenate([state[:tile_size], state[row_count - tile_size :]], axis=0)
        extended = extended_2(edge_states, (("shard", 0),), tile_size)
        below_block = extended[:tile_size].astype(jnp.float32)
        above_block = extended[extended.shape[0] - tile_size :].astype(jnp.float32)
        own_rows = partial_value.reshape(row_count, feature_width)
        own_rows = own_rows.at[:tile_size].add(
            jnp.dot(from_below, below_block, precision=lax.Precision.HIGHEST)
        )
        own_rows = own_rows.at[row_count - tile_size :].add(
            jnp.dot(from_above, above_block, precision=lax.Precision.HIGHEST)
        )
        aggregate = own_rows.astype(jnp.bfloat16)
        projected = jnp.dot(aggregate, layer_weight, preferred_element_type=jnp.float32)
        scale = lax.rsqrt(jnp.mean(projected * projected, axis=-1, keepdims=True) + 1e-06)
        normed = projected * scale * layer_gain.astype(jnp.float32)
        return (state.astype(jnp.float32) + jax.nn.gelu(normed)).astype(jnp.bfloat16)

    layer_mats, layer_gains = (
        lax.all_gather(weights, "section", axis=0, tiled=True),
        lax.all_gather(gains, "section", axis=0, tiled=True),
    )
    batch_index = section_index * per_section + 0
    group_tiles = lax.dynamic_index_in_dim(tiles, batch_index, 0, keepdims=False)
    group_rows = lax.dynamic_index_in_dim(tile_rows, batch_index, 0, keepdims=False)
    group_cols = lax.dynamic_index_in_dim(tile_cols, batch_index, 0, keepdims=False)
    group_live = lax.dynamic_index_in_dim(tile_live, batch_index, 0, keepdims=False)
    col_local = group_cols - shard_index * per_rows
    slot_local = group_rows - (shard_index * per_rows - 1)
    live_mask = (slot_ids < group_live[0]).astype(jnp.float32)
    placing = (slot_local[:, None] == place_ids[None, :]).astype(jnp.float32) * live_mask[:, None]
    edge_pick = jnp.stack([placing[:, 0], placing[:, per_rows + 1]], axis=1)
    edge_tiles = jnp.einsum(
        "kp,kab->pab", edge_pick, group_tiles.astype(jnp.float32), precision=lax.Precision.HIGHEST
    )
    received = extended_2(edge_tiles, (("shard", 0),), 1)
    parts = (group_tiles, col_local, placing[:, 1 : per_rows + 1], received[0], received[3])

    def through(layer_index, state):
        return apply_layer(state, parts, layer_mats[layer_index], layer_gains[layer_index])

    group_labels = lax.dynamic_index_in_dim(labels, batch_index, 0, keepdims=False)
    group_features = lax.dynamic_index_in_dim(features, batch_index, 0, keepdims=False)
    labels_hot = (
        group_labels[:, None] == jnp.arange(label_count, dtype=jnp.int32)[None, :]
    ).astype(jnp.float32)
    embedded = jnp.dot(labels_hot, label_table, precision=lax.Precision.HIGHEST)
    state = lax.fori_loop(
        0,
        section_count,
        through,
        (group_features.astype(jnp.float32) + embedded).astype(jnp.bfloat16),
    )
    results = [jnp.dot(state.astype(jnp.float32), head_weight, precision=lax.Precision.HIGHEST)]
    return jnp.stack(results)


def solution(mesh):
    return jax.shard_map(
        paired if mesh.shape["section"] == 2 else body,
        mesh=mesh,
        in_specs=(
            P(None, "shard", None),
            P(None, "shard"),
            P(),
            P(None, "shard", None, None),
            P(None, "shard"),
            P(None, "shard"),
            P(None, "shard"),
            P("section", None, None),
            P("section", None),
            P(),
        ),
        out_specs=P("section", "shard"),
        check_vma=False,
    )
```

```python
import jax
import jax.numpy as jnp
from jax import lax
from jax.experimental import pallas as pl
from jax.experimental.pallas import tpu as pltpu
from jax.sharding import PartitionSpec as P

BF16 = jnp.bfloat16
F32 = jnp.float32
PAD = 16
EXTRA = 8
GELU_LINEAR = 2.0 * (2.0 / 3.141592653589793) ** 0.5
GELU_CUBIC = 4.0 * GELU_LINEAR * 0.044715


def split3(value):
    high = value.astype(BF16).astype(F32)
    rest = value - high
    mid = rest.astype(BF16).astype(F32)
    return high, mid, rest - mid


def dot(a, b, dims=((1,), (0,))):
    return lax.dot_general(a, b, (dims, ((), ())), preferred_element_type=F32)


def in_hbm(*arrays):
    return [pltpu.with_memory_space_constraint(array, pltpu.HBM) for array in arrays]


def layer(aggregate, weight, half_gain, state):
    projected = dot(aggregate, weight)
    scale = lax.rsqrt(jnp.mean(projected * projected, axis=-1, keepdims=True) + 1e-06)
    half = (projected * scale * half_gain).astype(BF16)
    inner = half * (BF16(GELU_LINEAR) + BF16(GELU_CUBIC) * (half * half))
    return state + (half + half * jnp.tanh(inner))


def placed(block, blocks, shard, size):
    mirrored = 1 - lax.rem(shard, 2)
    return pl.ds(pl.multiple_of((block + mirrored * (blocks - 1 - 2 * block)) * size, size), size)


def first_kernel(
    tile_rows, tile_cols, tile_live, labels, label_table, tiles, features, gains, weights,
    far, far_sum, near, near_sum, crossing, state_out, adjacency_out,
    rows_buf, cols_buf, live_buf, labels_buf, classes_buf, tiles_buf, features_buf, gains_buf, table_buf, sums, sems,
):
    section = lax.axis_index("section")
    shard = lax.axis_index("shard")
    rows, width = features_buf.shape
    slots, size, _ = tiles_buf.shape
    blocks = rows // size
    kept = crossing.shape[0] - EXTRA
    group = section

    small = [(tile_rows, rows_buf), (tile_cols, cols_buf), (tile_live, live_buf)]
    named = [(label_table, classes_buf)]
    spread = []
    for block in range(blocks):
        span, place = pl.ds(block * size, size), placed(block, blocks, shard, size)
        named.append((labels.at[:, span], labels_buf.at[:, place]))
        spread.append((features.at[group, span], features_buf.at[place]))
    half = pl.ds(pl.multiple_of(lax.rem(shard, 2) * kept, kept), kept)
    sent = [(gains, gains_buf), (weights.at[0, half], crossing.at[pl.ds(0, kept)])]
    batches, count = [], 0
    for batch in (small, named, [(tiles.at[group], tiles_buf)], spread, sent):
        batches.append([
            pltpu.make_async_copy(source, target, sems.at[count + index])
            for index, (source, target) in enumerate(batch)
        ])
        count += len(batch)
    for batch in batches:
        for copy in batch:
            copy.start()
    sums[...] = jnp.zeros_like(sums)
    table_buf[...] = jnp.zeros_like(table_buf)

    for copy in batches[1]:
        copy.wait()
    classes = classes_buf.shape[0]
    for part, value in enumerate(split3(classes_buf[...])):
        table_buf[pl.ds(part * classes, classes), :] = value
    depth = table_buf.shape[0]
    index = lax.broadcasted_iota(jnp.int32, (depth, rows), 0)
    wanted = jnp.where(
        index < classes, index,
        jnp.where(index < 2 * classes, index - classes, jnp.where(index < 3 * classes, index - 2 * classes, -1)),
    )
    hot = (wanted == labels_buf[pl.ds(group, 1), :]).astype(F32).astype(BF16)
    embedded = dot(hot, table_buf[...].astype(BF16), ((0,), (0,)))

    for copy in batches[0] + batches[2]:
        copy.wait()
    for slot in range(slots):
        @pl.when(slot < live_buf[0, group])
        def _():
            row = rows_buf[group, slot] - (shard * blocks - 1)
            col = cols_buf[group, slot] - shard * blocks
            sums[placed(row, blocks + 2, shard, size), placed(col, blocks, shard, size)] += tiles_buf[slot].astype(F32)
    adjacency = sums[...].astype(BF16)
    adjacency_out[...] = adjacency

    for copy in batches[3]:
        copy.wait()
    state = (features_buf[...].astype(F32) + embedded).astype(BF16)
    state_out[...] = state
    partial = dot(adjacency[size : size + rows], state).astype(BF16)
    near_sum[...] = partial[:size]
    near[:, pl.ds(0, width)] = state[:size]
    near[:, pl.ds(width, size)] = adjacency[:size, :size]
    far_sum[...] = partial[rows - size :]
    far[:, pl.ds(0, width)] = state[rows - size :]
    far[:, pl.ds(width, size)] = adjacency[rows + size :, rows - size :]
    batches[4][0].wait()
    crossing[pl.ds(kept, EXTRA), :] = jnp.broadcast_to(gains_buf[...].astype(F32), (EXTRA, width)).astype(BF16)
    batches[4][1].wait()


def waiting_kernel(
    adjacency, state, head, gains, weights,
    aggregate, weight, half_gain, head_row,
    gains_buf, sems,
):
    copies = [
        pltpu.make_async_copy(source, target, sems.at[index])
        for index, (source, target) in enumerate(((weights.at[0], weight), (head, head_row), (gains, gains_buf)))
    ]
    for copy in copies:
        copy.start()
    aggregate[...] = dot(adjacency[...], state[...])
    copies[2].wait()
    half_gain[...] = 0.5 * gains_buf[...].astype(F32)
    copies[0].wait()
    copies[1].wait()


def near_kernel(near, near_sum, aggregate, state, weight, half_gain, near_blocks):
    size, width = near.shape[0], aggregate.shape[1]
    near_state = near[:, pl.ds(0, width)]
    first, second = pl.ds(0, size), pl.ds(size, size)
    near_blocks[first, :] = (aggregate[first, :] + near_sum[...].astype(F32)).astype(BF16)
    near_blocks[second, :] = (aggregate[second, :] + dot(near[:, pl.ds(width, size)], near_state)).astype(BF16)

    @pl.when(lax.axis_index("section") == 0)
    def _():
        for span, before in ((first, near_state), (second, state[pl.ds(0, size), :])):
            near_blocks[span, :] = layer(near_blocks[span, :], weight[...], half_gain[...], before)


def far_kernel(far, near, near_blocks, aggregate, adjacency, state, weight, half_gain, far_blocks, inner, states):
    size = far.shape[0]
    rows, width = state.shape
    for start in range(0, rows - 2 * size, size):
        far_blocks[pl.ds(start, size), :] = aggregate[pl.ds(2 * size + start, size), :].astype(BF16)
    far_blocks[pl.ds(rows - 2 * size, size), :] = (
        aggregate[pl.ds(rows, size), :] + dot(far[:, pl.ds(width, size)], far[:, pl.ds(0, width)])
    ).astype(BF16)

    @pl.when(lax.axis_index("section") == 0)
    def _():
        for start in range(0, rows - size, size):
            span = pl.ds(start, size)
            far_blocks[span, :] = layer(
                far_blocks[span, :], weight[...], half_gain[...], state[pl.ds(size + start, size), :]
            )
        states[pl.ds(0, size), :] = near_blocks[pl.ds(size, size), :]
        states[pl.ds(size, rows - size), :] = far_blocks[...]
        inner[...] = dot(adjacency[pl.ds(size, rows), :], states[...])
        inner[pl.ds(0, size), :] += dot(near[:, pl.ds(width, size)], near_blocks[pl.ds(0, size), :])


def second_kernel(*refs):
    first = lax.axis_index("section") == 0

    @pl.when(first)
    def _():
        both_layers(True, *refs)

    @pl.when(jnp.logical_not(first))
    def _():
        both_layers(False, *refs)


def both_layers(
    own_first,
    adjacency, state, far, far_sum, near, crossed, relayed, near_blocks, far_blocks, known_inner, aggregate,
    own_weight, half_gain, head_row,
    outcome,
    got_weight, next_states,
):
    shard = lax.axis_index("shard")
    even = lax.rem(shard, 2) == 0
    rows, width = state.shape
    size = near.shape[0]
    kept = crossed.shape[0] - EXTRA
    inside, last = pl.ds(size, rows), pl.ds(size + rows, size)

    for place, (one, two) in enumerate(((crossed, relayed), (relayed, crossed))):
        got_weight[pl.ds(place * kept, kept), :] = jnp.where(even, one[pl.ds(0, kept), :], two[pl.ds(0, kept), :])
    got_gain = 0.5 * crossed[pl.ds(kept, EXTRA), :].astype(F32)[0:1]
    used = ((own_weight, half_gain[...]), (got_weight, got_gain))
    (weight, gain), (last_weight, last_gain) = used if own_first else used[::-1]
    far_tile = far[:, pl.ds(width, size)]
    halo = (aggregate[last, :] + far_sum[...].astype(F32)).astype(BF16)

    if not own_first:
        for start in range(0, rows, size):
            span = pl.ds(start, size)
            source = near_blocks[pl.ds(size, size), :] if start == 0 else far_blocks[pl.ds(start - size, size), :]
            next_states[pl.ds(size + start, size), :] = layer(source, weight[...], gain, state[span, :])
        next_states[pl.ds(0, size), :] = layer(
            near_blocks[pl.ds(0, size), :], weight[...], gain, near[:, pl.ds(0, width)]
        )
    next_states[last, :] = layer(halo, weight[...], gain, far[:, pl.ds(0, width)])

    if own_first:
        inner = known_inner[...]
    else:
        inner = dot(adjacency[inside, :], next_states[inside, :])
    for block in range(rows // size):
        start = block * size
        summed = inner[start : start + size]
        if block == 0 and not own_first:
            summed = summed + dot(near[:, pl.ds(width, size)], next_states[pl.ds(0, size), :])
        if block == rows // size - 1:
            summed = summed + dot(far_tile, next_states[last, :])
        if not own_first:
            before = next_states[pl.ds(size + start, size), :]
        else:
            before = near_blocks[pl.ds(size, size), :] if block == 0 else far_blocks[pl.ds(start - size, size), :]
        after = layer(summed.astype(BF16), last_weight[...], last_gain, before)
        weighted = after.astype(F32) * head_row[...]
        folded = weighted[:, :size]
        for at in range(size, width, size):
            folded = folded + weighted[:, at : at + size]
        outcome[:, placed(block, rows // size, shard, size)] = jnp.sum(folded.T, axis=0, keepdims=True)


def paired(features, labels, label_table, tiles, tile_rows, tile_cols, tile_live, weights, gains, head_weight):
    shard_count = lax.axis_size("shard")
    groups, rows, width = features.shape
    _, slots, size, _ = tiles.shape
    depth = weights.shape[1]
    kept = depth // 2
    classes = label_table.shape[0]
    vmem = pl.BlockSpec(memory_space=pltpu.VMEM)
    hbm = pl.BlockSpec(memory_space=pltpu.HBM)
    table_rows = -(-3 * classes // PAD) * PAD

    far, far_sum, near, near_sum, crossing, state, adjacency = pl.pallas_call(
        first_kernel,
        out_shape=(
            jax.ShapeDtypeStruct((size, width + size), BF16),
            jax.ShapeDtypeStruct((size, width), BF16),
            jax.ShapeDtypeStruct((size, width + size), BF16),
            jax.ShapeDtypeStruct((size, width), BF16),
            jax.ShapeDtypeStruct((kept + EXTRA, width), BF16),
            jax.ShapeDtypeStruct((rows, width), BF16),
            jax.ShapeDtypeStruct((rows + 2 * size, rows), BF16),
        ),
        in_specs=[hbm] * 9,
        out_specs=(vmem,) * 7,
        scratch_shapes=[
            pltpu.SMEM((groups, slots), jnp.int32),
            pltpu.SMEM((groups, slots), jnp.int32),
            pltpu.SMEM((1, groups), jnp.int32),
            pltpu.VMEM((groups, rows), jnp.int32),
            pltpu.VMEM((classes, width), F32),
            pltpu.VMEM((slots, size, size), BF16),
            pltpu.VMEM((rows, width), BF16),
            pltpu.VMEM((1, width), BF16),
            pltpu.VMEM((table_rows, width), F32),
            pltpu.VMEM((rows + 2 * size, rows), F32),
            pltpu.SemaphoreType.DMA((7 + 2 * (rows // size),)),
        ],
        compiler_params=pltpu.CompilerParams(vmem_limit_bytes=16 * 2**20),
        name="messages",
    )(*in_hbm(tile_rows, tile_cols, tile_live.T, labels, label_table, tiles, features, gains, weights))

    beside = [(i, i ^ 1) for i in range(shard_count)]
    apart = [(i, (i + 1) % shard_count) for i in range(1, shard_count, 2)]
    apart += [(b, a) for a, b in apart]
    across = [(0, 1), (1, 0)]
    crossed = lax.ppermute(crossing, "section", across)
    far = lax.ppermute(far, "shard", apart)
    far_sum = lax.ppermute(far_sum, "shard", [pair for pair in apart if abs(pair[0] - pair[1]) == 1])
    near = lax.ppermute(near, "shard", beside)
    near_sum = lax.ppermute(near_sum, "shard", beside)

    aggregate, own_weight, half_gain, head_row = pl.pallas_call(
        waiting_kernel,
        out_shape=(
            jax.ShapeDtypeStruct((rows + 2 * size, width), F32),
            jax.ShapeDtypeStruct((depth, width), BF16),
            jax.ShapeDtypeStruct((1, width), F32),
            jax.ShapeDtypeStruct((1, width), F32),
        ),
        in_specs=[vmem] * 2 + [hbm] * 3,
        out_specs=(vmem,) * 4,
        scratch_shapes=[
            pltpu.VMEM((1, width), BF16),
            pltpu.SemaphoreType.DMA((3,)),
        ],
        compiler_params=pltpu.CompilerParams(vmem_limit_bytes=16 * 2**20),
        cost_estimate=pl.CostEstimate(flops=15 * 10**8, bytes_accessed=2**20, transcendentals=0),
        name="waiting",
    )(adjacency, state, *in_hbm(head_weight.reshape(1, width), gains, weights))

    crossed, aggregate, near = lax.optimization_barrier((crossed, aggregate, near))
    near_blocks = pl.pallas_call(
        near_kernel,
        out_shape=jax.ShapeDtypeStruct((2 * size, width), BF16),
        in_specs=[vmem] * 6,
        out_specs=vmem,
        compiler_params=pltpu.CompilerParams(vmem_limit_bytes=16 * 2**20),
        name="beside",
    )(near, near_sum, aggregate, state, own_weight, half_gain)

    relayed = lax.ppermute(crossed, "shard", beside)

    far_blocks, inner = pl.pallas_call(
        far_kernel,
        out_shape=(
            jax.ShapeDtypeStruct((rows - size, width), BF16),
            jax.ShapeDtypeStruct((rows, width), F32),
        ),
        in_specs=[vmem] * 8,
        out_specs=(vmem,) * 2,
        scratch_shapes=[pltpu.VMEM((rows, width), BF16)],
        compiler_params=pltpu.CompilerParams(vmem_limit_bytes=16 * 2**20),
        cost_estimate=pl.CostEstimate(flops=4 * 10**9, bytes_accessed=2**20, transcendentals=0),
        name="apart",
    )(far, near, near_blocks, aggregate, adjacency, state, own_weight, half_gain)

    return pl.pallas_call(
        second_kernel,
        out_shape=jax.ShapeDtypeStruct((1, rows), F32),
        in_specs=[vmem] * 14,
        out_specs=vmem,
        scratch_shapes=[
            pltpu.VMEM((depth, width), BF16),
            pltpu.VMEM((rows + 2 * size, width), BF16),
        ],
        compiler_params=pltpu.CompilerParams(vmem_limit_bytes=32 * 2**20),
        name="layers",
    )(
        adjacency, state, far, far_sum, near, crossed, relayed, near_blocks, far_blocks, inner, aggregate,
        own_weight, half_gain, head_row,
    )


def extended_2(block, sides, width):
    for axis, dim in sides:
        count = lax.axis_size(axis)
        forward = [(i, i + 1) for i in range(count - 1)]
        backward = [(target, source) for source, target in forward]
        low = lax.ppermute(
            lax.slice_in_dim(block, block.shape[dim] - width, None, axis=dim), axis, forward
        )
        high = lax.ppermute(lax.slice_in_dim(block, 0, width, axis=dim), axis, backward)
        block = jnp.concatenate([low, block, high], axis=dim)
    return block


def body(
    features,
    labels,
    label_table,
    tiles,
    tile_rows,
    tile_cols,
    tile_live,
    weights,
    gains,
    head_weight,
):
    section_count = lax.axis_size("section")
    section_index = lax.axis_index("section")
    shard_index = lax.axis_index("shard")
    batch_count = features.shape[0]
    row_count = features.shape[1]
    feature_width = features.shape[2]
    tile_size = tiles.shape[2]
    slot_count = tiles.shape[1]
    label_count = label_table.shape[0]
    per_rows = row_count // tile_size
    per_section = batch_count // section_count
    slot_ids = jnp.arange(slot_count, dtype=jnp.int32)
    place_ids = jnp.arange(per_rows + 2, dtype=jnp.int32)

    def apply_layer(state, parts, layer_weight, layer_gain):
        group_tiles, col_local, placing, from_below, from_above = parts
        block_view = state.reshape(per_rows, tile_size, feature_width)
        chosen_blocks = jnp.take(block_view, col_local, axis=0)
        products = jnp.einsum(
            "kab,kbd->kad", group_tiles, chosen_blocks, preferred_element_type=jnp.float32
        )
        partial_value = jnp.einsum(
            "kp,kad->pad", placing, products, precision=lax.Precision.HIGHEST
        )
        edge_states = jnp.concatenate([state[:tile_size], state[row_count - tile_size :]], axis=0)
        extended = extended_2(edge_states, (("shard", 0),), tile_size)
        below_block = extended[:tile_size].astype(jnp.float32)
        above_block = extended[extended.shape[0] - tile_size :].astype(jnp.float32)
        own_rows = partial_value.reshape(row_count, feature_width)
        own_rows = own_rows.at[:tile_size].add(
            jnp.dot(from_below, below_block, precision=lax.Precision.HIGHEST)
        )
        own_rows = own_rows.at[row_count - tile_size :].add(
            jnp.dot(from_above, above_block, precision=lax.Precision.HIGHEST)
        )
        aggregate = own_rows.astype(jnp.bfloat16)
        projected = jnp.dot(aggregate, layer_weight, preferred_element_type=jnp.float32)
        scale = lax.rsqrt(jnp.mean(projected * projected, axis=-1, keepdims=True) + 1e-06)
        normed = projected * scale * layer_gain.astype(jnp.float32)
        return (state.astype(jnp.float32) + jax.nn.gelu(normed)).astype(jnp.bfloat16)

    layer_mats, layer_gains = (
        lax.all_gather(weights, "section", axis=0, tiled=True),
        lax.all_gather(gains, "section", axis=0, tiled=True),
    )
    batch_index = section_index * per_section + 0
    group_tiles = lax.dynamic_index_in_dim(tiles, batch_index, 0, keepdims=False)
    group_rows = lax.dynamic_index_in_dim(tile_rows, batch_index, 0, keepdims=False)
    group_cols = lax.dynamic_index_in_dim(tile_cols, batch_index, 0, keepdims=False)
    group_live = lax.dynamic_index_in_dim(tile_live, batch_index, 0, keepdims=False)
    col_local = group_cols - shard_index * per_rows
    slot_local = group_rows - (shard_index * per_rows - 1)
    live_mask = (slot_ids < group_live[0]).astype(jnp.float32)
    placing = (slot_local[:, None] == place_ids[None, :]).astype(jnp.float32) * live_mask[:, None]
    edge_pick = jnp.stack([placing[:, 0], placing[:, per_rows + 1]], axis=1)
    edge_tiles = jnp.einsum(
        "kp,kab->pab", edge_pick, group_tiles.astype(jnp.float32), precision=lax.Precision.HIGHEST
    )
    received = extended_2(edge_tiles, (("shard", 0),), 1)
    parts = (group_tiles, col_local, placing[:, 1 : per_rows + 1], received[0], received[3])

    def through(layer_index, state):
        return apply_layer(state, parts, layer_mats[layer_index], layer_gains[layer_index])

    group_labels = lax.dynamic_index_in_dim(labels, batch_index, 0, keepdims=False)
    group_features = lax.dynamic_index_in_dim(features, batch_index, 0, keepdims=False)
    labels_hot = (
        group_labels[:, None] == jnp.arange(label_count, dtype=jnp.int32)[None, :]
    ).astype(jnp.float32)
    embedded = jnp.dot(labels_hot, label_table, precision=lax.Precision.HIGHEST)
    state = lax.fori_loop(
        0,
        section_count,
        through,
        (group_features.astype(jnp.float32) + embedded).astype(jnp.bfloat16),
    )
    results = [jnp.dot(state.astype(jnp.float32), head_weight, precision=lax.Precision.HIGHEST)]
    return jnp.stack(results)


def solution(mesh):
    return jax.shard_map(
        paired if mesh.shape["section"] == 2 else body,
        mesh=mesh,
        in_specs=(
            P(None, "shard", None),
            P(None, "shard"),
            P(),
            P(None, "shard", None, None),
            P(None, "shard"),
            P(None, "shard"),
            P(None, "shard"),
            P("section", None, None),
            P("section", None),
            P(),
        ),
        out_specs=P("section", "shard"),
        check_vma=False,
    )
```

```python
import jax
import jax.numpy as jnp
from jax import lax
from jax.experimental import pallas as pl
from jax.experimental.pallas import tpu as pltpu
from jax.sharding import PartitionSpec as P

BF16 = jnp.bfloat16
F32 = jnp.float32
PAD = 16
EXTRA = 8
GELU_LINEAR = 2.0 * (2.0 / 3.141592653589793) ** 0.5
GELU_CUBIC = 4.0 * GELU_LINEAR * 0.044715


def split3(value):
    high = value.astype(BF16).astype(F32)
    rest = value - high
    mid = rest.astype(BF16).astype(F32)
    return high, mid, rest - mid


def dot(a, b, dims=((1,), (0,))):
    return lax.dot_general(a, b, (dims, ((), ())), preferred_element_type=F32)


def in_hbm(*arrays):
    return [pltpu.with_memory_space_constraint(array, pltpu.HBM) for array in arrays]


def layer(aggregate, weight, half_gain, state):
    projected = dot(aggregate, weight)
    scale = lax.rsqrt(jnp.mean(projected * projected, axis=-1, keepdims=True) + 1e-06)
    half = (projected * half_gain * scale).astype(BF16)
    inner = half * (BF16(GELU_LINEAR) + BF16(GELU_CUBIC) * (half * half))
    return state + (half + half * jnp.tanh(inner))


def placed(block, blocks, shard, size):
    mirrored = 1 - lax.rem(shard, 2)
    return pl.ds(pl.multiple_of((block + mirrored * (blocks - 1 - 2 * block)) * size, size), size)


def first_kernel(
    tile_rows, tile_cols, tile_live, labels, label_table, tiles, features, gains, weights,
    far, far_sum, near, near_sum, crossing, state_out, adjacency_out,
    rows_buf, cols_buf, live_buf, labels_buf, classes_buf, tiles_buf, features_buf, gains_buf, table_buf, sums, sems,
):
    section = lax.axis_index("section")
    shard = lax.axis_index("shard")
    rows, width = features_buf.shape
    slots, size, _ = tiles_buf.shape
    blocks = rows // size
    kept = crossing.shape[0] - EXTRA
    group = section

    small = [(tile_rows, rows_buf), (tile_cols, cols_buf), (tile_live, live_buf)]
    named = [(label_table, classes_buf)]
    spread = []
    for block in range(blocks):
        span, place = pl.ds(block * size, size), placed(block, blocks, shard, size)
        named.append((labels.at[:, span], labels_buf.at[:, place]))
        spread.append((features.at[group, span], features_buf.at[place]))
    half = pl.ds(pl.multiple_of(lax.rem(shard, 2) * kept, kept), kept)
    sent = [(gains, gains_buf), (weights.at[0, half], crossing.at[pl.ds(0, kept)])]
    batches, count = [], 0
    for batch in (small, named, [(tiles.at[group], tiles_buf)], spread, sent):
        batches.append([
            pltpu.make_async_copy(source, target, sems.at[count + index])
            for index, (source, target) in enumerate(batch)
        ])
        count += len(batch)
    for batch in batches:
        for copy in batch:
            copy.start()
    sums[...] = jnp.zeros_like(sums)
    table_buf[...] = jnp.zeros_like(table_buf)

    for copy in batches[1]:
        copy.wait()
    classes = classes_buf.shape[0]
    for part, value in enumerate(split3(classes_buf[...])):
        table_buf[pl.ds(part * classes, classes), :] = value
    depth = table_buf.shape[0]
    index = lax.broadcasted_iota(jnp.int32, (depth, rows), 0)
    wanted = jnp.where(
        index < classes, index,
        jnp.where(index < 2 * classes, index - classes, jnp.where(index < 3 * classes, index - 2 * classes, -1)),
    )
    hot = (wanted == labels_buf[pl.ds(group, 1), :]).astype(F32).astype(BF16)
    embedded = dot(hot, table_buf[...].astype(BF16), ((0,), (0,)))

    for copy in batches[0] + batches[2]:
        copy.wait()
    for slot in range(slots):
        @pl.when(slot < live_buf[0, group])
        def _():
            row = rows_buf[group, slot] - (shard * blocks - 1)
            col = cols_buf[group, slot] - shard * blocks
            sums[placed(row, blocks + 2, shard, size), placed(col, blocks, shard, size)] += tiles_buf[slot].astype(F32)
    adjacency = sums[...].astype(BF16)
    adjacency_out[...] = adjacency

    for copy in batches[3]:
        copy.wait()
    state = (features_buf[...].astype(F32) + embedded).astype(BF16)
    state_out[...] = state
    partial = dot(adjacency[size : size + rows], state).astype(BF16)
    near_sum[...] = partial[:size]
    near[:, pl.ds(0, width)] = state[:size]
    near[:, pl.ds(width, size)] = adjacency[:size, :size]
    far_sum[...] = partial[rows - size :]
    far[:, pl.ds(0, width)] = state[rows - size :]
    far[:, pl.ds(width, size)] = adjacency[rows + size :, rows - size :]
    batches[4][0].wait()
    crossing[pl.ds(kept, EXTRA), :] = jnp.broadcast_to(gains_buf[...].astype(F32), (EXTRA, width)).astype(BF16)
    batches[4][1].wait()


def waiting_kernel(
    adjacency, state, head, gains, weights,
    aggregate, weight, half_gain, head_row,
    gains_buf, sems,
):
    copies = [
        pltpu.make_async_copy(source, target, sems.at[index])
        for index, (source, target) in enumerate(((weights.at[0], weight), (head, head_row), (gains, gains_buf)))
    ]
    for copy in copies:
        copy.start()
    aggregate[...] = dot(adjacency[...], state[...])
    copies[2].wait()
    half_gain[...] = 0.5 * gains_buf[...].astype(F32)
    copies[0].wait()
    copies[1].wait()


def near_kernel(near, near_sum, aggregate, state, weight, half_gain, near_blocks):
    size, width = near.shape[0], aggregate.shape[1]
    near_state = near[:, pl.ds(0, width)]
    first, second = pl.ds(0, size), pl.ds(size, size)
    near_blocks[first, :] = (aggregate[first, :] + near_sum[...].astype(F32)).astype(BF16)
    near_blocks[second, :] = (aggregate[second, :] + dot(near[:, pl.ds(width, size)], near_state)).astype(BF16)

    @pl.when(lax.axis_index("section") == 0)
    def _():
        for span, before in ((first, near_state), (second, state[pl.ds(0, size), :])):
            near_blocks[span, :] = layer(near_blocks[span, :], weight[...], half_gain[...], before)


def far_kernel(far, near, near_blocks, aggregate, adjacency, state, weight, half_gain, far_blocks, inner, states):
    size = far.shape[0]
    rows, width = state.shape
    for start in range(0, rows - 2 * size, size):
        far_blocks[pl.ds(start, size), :] = aggregate[pl.ds(2 * size + start, size), :].astype(BF16)
    far_blocks[pl.ds(rows - 2 * size, size), :] = (
        aggregate[pl.ds(rows, size), :] + dot(far[:, pl.ds(width, size)], far[:, pl.ds(0, width)])
    ).astype(BF16)

    @pl.when(lax.axis_index("section") == 0)
    def _():
        for start in range(0, rows - size, size):
            span = pl.ds(start, size)
            far_blocks[span, :] = layer(
                far_blocks[span, :], weight[...], half_gain[...], state[pl.ds(size + start, size), :]
            )
        states[pl.ds(0, size), :] = near_blocks[pl.ds(size, size), :]
        states[pl.ds(size, rows - size), :] = far_blocks[...]
        inner[...] = dot(adjacency[pl.ds(size, rows), :], states[...])
        inner[pl.ds(0, size), :] += dot(near[:, pl.ds(width, size)], near_blocks[pl.ds(0, size), :])


def second_kernel(*refs):
    first = lax.axis_index("section") == 0

    @pl.when(first)
    def _():
        both_layers(True, *refs)

    @pl.when(jnp.logical_not(first))
    def _():
        both_layers(False, *refs)


def both_layers(
    own_first,
    adjacency, state, far, far_sum, near, crossed, relayed, near_blocks, far_blocks, known_inner, aggregate,
    own_weight, half_gain, head_row,
    outcome,
    got_weight, next_states,
):
    shard = lax.axis_index("shard")
    even = lax.rem(shard, 2) == 0
    rows, width = state.shape
    size = near.shape[0]
    kept = crossed.shape[0] - EXTRA
    inside, last = pl.ds(size, rows), pl.ds(size + rows, size)

    for place, (one, two) in enumerate(((crossed, relayed), (relayed, crossed))):
        got_weight[pl.ds(place * kept, kept), :] = jnp.where(even, one[pl.ds(0, kept), :], two[pl.ds(0, kept), :])
    got_gain = 0.5 * crossed[pl.ds(kept, EXTRA), :].astype(F32)[0:1]
    used = ((own_weight, half_gain[...]), (got_weight, got_gain))
    (weight, gain), (last_weight, last_gain) = used if own_first else used[::-1]
    far_tile = far[:, pl.ds(width, size)]
    halo = (aggregate[last, :] + far_sum[...].astype(F32)).astype(BF16)

    if own_first:
        next_states[pl.ds(0, 2 * size), :] = near_blocks[...]
        next_states[pl.ds(2 * size, rows - size), :] = far_blocks[...]
    else:
        for start in range(0, rows, size):
            span = pl.ds(start, size)
            source = near_blocks[pl.ds(size, size), :] if start == 0 else far_blocks[pl.ds(start - size, size), :]
            next_states[pl.ds(size + start, size), :] = layer(source, weight[...], gain, state[span, :])
        next_states[pl.ds(0, size), :] = layer(
            near_blocks[pl.ds(0, size), :], weight[...], gain, near[:, pl.ds(0, width)]
        )
    next_states[last, :] = layer(halo, weight[...], gain, far[:, pl.ds(0, width)])

    if own_first:
        inner = known_inner[...]
    else:
        inner = dot(adjacency[inside, :], next_states[inside, :])
    for block in range(rows // size):
        start = block * size
        summed = inner[start : start + size]
        if block == 0 and not own_first:
            summed = summed + dot(near[:, pl.ds(width, size)], next_states[pl.ds(0, size), :])
        if block == rows // size - 1:
            summed = summed + dot(far_tile, next_states[last, :])
        before = next_states[pl.ds(size + start, size), :]
        after = layer(summed.astype(BF16), last_weight[...], last_gain, before)
        weighted = after.astype(F32) * head_row[...]
        folded = weighted[:, :size]
        for at in range(size, width, size):
            folded = folded + weighted[:, at : at + size]
        outcome[:, placed(block, rows // size, shard, size)] = jnp.sum(folded.T, axis=0, keepdims=True)


def paired(features, labels, label_table, tiles, tile_rows, tile_cols, tile_live, weights, gains, head_weight):
    shard_count = lax.axis_size("shard")
    groups, rows, width = features.shape
    _, slots, size, _ = tiles.shape
    depth = weights.shape[1]
    kept = depth // 2
    classes = label_table.shape[0]
    vmem = pl.BlockSpec(memory_space=pltpu.VMEM)
    hbm = pl.BlockSpec(memory_space=pltpu.HBM)
    table_rows = -(-3 * classes // PAD) * PAD

    far, far_sum, near, near_sum, crossing, state, adjacency = pl.pallas_call(
        first_kernel,
        out_shape=(
            jax.ShapeDtypeStruct((size, width + size), BF16),
            jax.ShapeDtypeStruct((size, width), BF16),
            jax.ShapeDtypeStruct((size, width + size), BF16),
            jax.ShapeDtypeStruct((size, width), BF16),
            jax.ShapeDtypeStruct((kept + EXTRA, width), BF16),
            jax.ShapeDtypeStruct((rows, width), BF16),
            jax.ShapeDtypeStruct((rows + 2 * size, rows), BF16),
        ),
        in_specs=[hbm] * 9,
        out_specs=(vmem,) * 7,
        scratch_shapes=[
            pltpu.SMEM((groups, slots), jnp.int32),
            pltpu.SMEM((groups, slots), jnp.int32),
            pltpu.SMEM((1, groups), jnp.int32),
            pltpu.VMEM((groups, rows), jnp.int32),
            pltpu.VMEM((classes, width), F32),
            pltpu.VMEM((slots, size, size), BF16),
            pltpu.VMEM((rows, width), BF16),
            pltpu.VMEM((1, width), BF16),
            pltpu.VMEM((table_rows, width), F32),
            pltpu.VMEM((rows + 2 * size, rows), F32),
            pltpu.SemaphoreType.DMA((7 + 2 * (rows // size),)),
        ],
        compiler_params=pltpu.CompilerParams(vmem_limit_bytes=16 * 2**20),
        name="messages",
    )(*in_hbm(tile_rows, tile_cols, tile_live.T, labels, label_table, tiles, features, gains, weights))

    beside = [(i, i ^ 1) for i in range(shard_count)]
    apart = [(i, (i + 1) % shard_count) for i in range(1, shard_count, 2)]
    apart += [(b, a) for a, b in apart]
    across = [(0, 1), (1, 0)]
    crossed = lax.ppermute(crossing, "section", across)
    far = lax.ppermute(far, "shard", apart)
    far_sum = lax.ppermute(far_sum, "shard", [pair for pair in apart if abs(pair[0] - pair[1]) == 1])
    near = lax.ppermute(near, "shard", beside)
    near_sum = lax.ppermute(near_sum, "shard", beside)

    aggregate, own_weight, half_gain, head_row = pl.pallas_call(
        waiting_kernel,
        out_shape=(
            jax.ShapeDtypeStruct((rows + 2 * size, width), F32),
            jax.ShapeDtypeStruct((depth, width), BF16),
            jax.ShapeDtypeStruct((1, width), F32),
            jax.ShapeDtypeStruct((1, width), F32),
        ),
        in_specs=[vmem] * 2 + [hbm] * 3,
        out_specs=(vmem,) * 4,
        scratch_shapes=[
            pltpu.VMEM((1, width), BF16),
            pltpu.SemaphoreType.DMA((3,)),
        ],
        compiler_params=pltpu.CompilerParams(vmem_limit_bytes=16 * 2**20),
        cost_estimate=pl.CostEstimate(flops=15 * 10**8, bytes_accessed=2**20, transcendentals=0),
        name="waiting",
    )(adjacency, state, *in_hbm(head_weight.reshape(1, width), gains, weights))

    crossed, aggregate, near = lax.optimization_barrier((crossed, aggregate, near))
    near_blocks = pl.pallas_call(
        near_kernel,
        out_shape=jax.ShapeDtypeStruct((2 * size, width), BF16),
        in_specs=[vmem] * 6,
        out_specs=vmem,
        compiler_params=pltpu.CompilerParams(vmem_limit_bytes=16 * 2**20),
        name="beside",
    )(near, near_sum, aggregate, state, own_weight, half_gain)

    relayed = lax.ppermute(crossed, "shard", beside)

    far_blocks, inner = pl.pallas_call(
        far_kernel,
        out_shape=(
            jax.ShapeDtypeStruct((rows - size, width), BF16),
            jax.ShapeDtypeStruct((rows, width), F32),
        ),
        in_specs=[vmem] * 8,
        out_specs=(vmem,) * 2,
        scratch_shapes=[pltpu.VMEM((rows, width), BF16)],
        compiler_params=pltpu.CompilerParams(vmem_limit_bytes=16 * 2**20),
        cost_estimate=pl.CostEstimate(flops=4 * 10**9, bytes_accessed=2**20, transcendentals=0),
        name="apart",
    )(far, near, near_blocks, aggregate, adjacency, state, own_weight, half_gain)

    return pl.pallas_call(
        second_kernel,
        out_shape=jax.ShapeDtypeStruct((1, rows), F32),
        in_specs=[vmem] * 14,
        out_specs=vmem,
        scratch_shapes=[
            pltpu.VMEM((depth, width), BF16),
            pltpu.VMEM((rows + 2 * size, width), BF16),
        ],
        compiler_params=pltpu.CompilerParams(vmem_limit_bytes=32 * 2**20),
        name="layers",
    )(
        adjacency, state, far, far_sum, near, crossed, relayed, near_blocks, far_blocks, inner, aggregate,
        own_weight, half_gain, head_row,
    )


def extended_2(block, sides, width):
    for axis, dim in sides:
        count = lax.axis_size(axis)
        forward = [(i, i + 1) for i in range(count - 1)]
        backward = [(target, source) for source, target in forward]
        low = lax.ppermute(
            lax.slice_in_dim(block, block.shape[dim] - width, None, axis=dim), axis, forward
        )
        high = lax.ppermute(lax.slice_in_dim(block, 0, width, axis=dim), axis, backward)
        block = jnp.concatenate([low, block, high], axis=dim)
    return block


def body(
    features,
    labels,
    label_table,
    tiles,
    tile_rows,
    tile_cols,
    tile_live,
    weights,
    gains,
    head_weight,
):
    section_count = lax.axis_size("section")
    section_index = lax.axis_index("section")
    shard_index = lax.axis_index("shard")
    batch_count = features.shape[0]
    row_count = features.shape[1]
    feature_width = features.shape[2]
    tile_size = tiles.shape[2]
    slot_count = tiles.shape[1]
    label_count = label_table.shape[0]
    per_rows = row_count // tile_size
    per_section = batch_count // section_count
    slot_ids = jnp.arange(slot_count, dtype=jnp.int32)
    place_ids = jnp.arange(per_rows + 2, dtype=jnp.int32)

    def apply_layer(state, parts, layer_weight, layer_gain):
        group_tiles, col_local, placing, from_below, from_above = parts
        block_view = state.reshape(per_rows, tile_size, feature_width)
        chosen_blocks = jnp.take(block_view, col_local, axis=0)
        products = jnp.einsum(
            "kab,kbd->kad", group_tiles, chosen_blocks, preferred_element_type=jnp.float32
        )
        partial_value = jnp.einsum(
            "kp,kad->pad", placing, products, precision=lax.Precision.HIGHEST
        )
        edge_states = jnp.concatenate([state[:tile_size], state[row_count - tile_size :]], axis=0)
        extended = extended_2(edge_states, (("shard", 0),), tile_size)
        below_block = extended[:tile_size].astype(jnp.float32)
        above_block = extended[extended.shape[0] - tile_size :].astype(jnp.float32)
        own_rows = partial_value.reshape(row_count, feature_width)
        own_rows = own_rows.at[:tile_size].add(
            jnp.dot(from_below, below_block, precision=lax.Precision.HIGHEST)
        )
        own_rows = own_rows.at[row_count - tile_size :].add(
            jnp.dot(from_above, above_block, precision=lax.Precision.HIGHEST)
        )
        aggregate = own_rows.astype(jnp.bfloat16)
        projected = jnp.dot(aggregate, layer_weight, preferred_element_type=jnp.float32)
        scale = lax.rsqrt(jnp.mean(projected * projected, axis=-1, keepdims=True) + 1e-06)
        normed = projected * scale * layer_gain.astype(jnp.float32)
        return (state.astype(jnp.float32) + jax.nn.gelu(normed)).astype(jnp.bfloat16)

    layer_mats, layer_gains = (
        lax.all_gather(weights, "section", axis=0, tiled=True),
        lax.all_gather(gains, "section", axis=0, tiled=True),
    )
    batch_index = section_index * per_section + 0
    group_tiles = lax.dynamic_index_in_dim(tiles, batch_index, 0, keepdims=False)
    group_rows = lax.dynamic_index_in_dim(tile_rows, batch_index, 0, keepdims=False)
    group_cols = lax.dynamic_index_in_dim(tile_cols, batch_index, 0, keepdims=False)
    group_live = lax.dynamic_index_in_dim(tile_live, batch_index, 0, keepdims=False)
    col_local = group_cols - shard_index * per_rows
    slot_local = group_rows - (shard_index * per_rows - 1)
    live_mask = (slot_ids < group_live[0]).astype(jnp.float32)
    placing = (slot_local[:, None] == place_ids[None, :]).astype(jnp.float32) * live_mask[:, None]
    edge_pick = jnp.stack([placing[:, 0], placing[:, per_rows + 1]], axis=1)
    edge_tiles = jnp.einsum(
        "kp,kab->pab", edge_pick, group_tiles.astype(jnp.float32), precision=lax.Precision.HIGHEST
    )
    received = extended_2(edge_tiles, (("shard", 0),), 1)
    parts = (group_tiles, col_local, placing[:, 1 : per_rows + 1], received[0], received[3])

    def through(layer_index, state):
        return apply_layer(state, parts, layer_mats[layer_index], layer_gains[layer_index])

    group_labels = lax.dynamic_index_in_dim(labels, batch_index, 0, keepdims=False)
    group_features = lax.dynamic_index_in_dim(features, batch_index, 0, keepdims=False)
    labels_hot = (
        group_labels[:, None] == jnp.arange(label_count, dtype=jnp.int32)[None, :]
    ).astype(jnp.float32)
    embedded = jnp.dot(labels_hot, label_table, precision=lax.Precision.HIGHEST)
    state = lax.fori_loop(
        0,
        section_count,
        through,
        (group_features.astype(jnp.float32) + embedded).astype(jnp.bfloat16),
    )
    results = [jnp.dot(state.astype(jnp.float32), head_weight, precision=lax.Precision.HIGHEST)]
    return jnp.stack(results)


def solution(mesh):
    return jax.shard_map(
        paired if mesh.shape["section"] == 2 else body,
        mesh=mesh,
        in_specs=(
            P(None, "shard", None),
            P(None, "shard"),
            P(),
            P(None, "shard", None, None),
            P(None, "shard"),
            P(None, "shard"),
            P(None, "shard"),
            P("section", None, None),
            P("section", None),
            P(),
        ),
        out_specs=P("section", "shard"),
        check_vma=False,
    )
```
